32 devices in a mesh: dp: 8 (over z, core), expert: 4 (over y, x).
Axes of the slice: x: 2, y: 2, z: 4, core: 2. Of those that a mesh axis runs over, the one named last changes fastest.
Arguments:
- tokens: bfloat16 [75264, 512], P(('dp', 'expert')), may hold values from -6 to 6
- gain_one: float32 [512], replicated, may hold values from 0.5 to 1.5
- w_qkv: bfloat16 [512, 1536], replicated, may hold values from -0.25 to 0.25
- w_proj: bfloat16 [512, 512], replicated, may hold values from -1 to 1
- gain_two: float32 [512], replicated, may hold values from 0.5 to 1.5
- w_router: float32 [512, 8], replicated, may hold values from -0.1875 to 0.1875
- w_in: bfloat16 [8, 512, 2048], P('expert'), may hold values from -0.25 to 0.25
- w_eout: bfloat16 [8, 2048, 512], P('expert'), may hold values from -3 to 3
- picks: int32 [75264, 2], P(('dp', 'expert')), may hold values from 0 to 7, all different within a row; in each aligned block of 2352 rows (0 to 2351, 2352 to 4703, ...) at most 624 rows name the same one
- keep: int32 [75264, 2], P(('dp', 'expert')), may hold values 0 or 1
- grad_out: bfloat16 [75264, 512], P(('dp', 'expert')), may hold values from -6 to 6
Outputs:
- block_out: bfloat16 [75264, 512], P(('dp', 'expert'))
- grad_tokens: float32 [75264, 512], P(('dp', 'expert'))
- grad_gain_one: float32 [512], replicated
- grad_qkv: float32 [512, 1536], replicated
- grad_proj: float32 [512, 512], replicated
- grad_gain_two: float32 [512], replicated
- grad_router: float32 [512, 8], replicated
- grad_in: float32 [8, 512, 2048], P('expert', 'dp')
- grad_eout: float32 [8, 2048, 512], P('expert', 'dp')
The draws below stay inside these ranges and needn't reach their ends.
Inputs may be any that keep to these rules, and one draw needn't show every extreme that they name: `picks`: each row names two different experts; among the 2352 rows of one device no expert is named by more than 624 rows, a bound that some block reaches. `keep`: 1 keeps the pick, 0 drops it.
All inputs are finite; a program needn't handle non-finite values. No bound on the sum of `keep` on one device may be relied on, other than what follows from the above.
Results may differ from the reference program's by a relative error of at most 0.015.
Values may be sent and summed in bfloat16 or wider, within the bound.
No kernel may reach another device: no remote copies, remote signals or barrier semaphores. Data moves between devices by JAX's collectives and lax.ppermute only.
A program may use at most 320 MiB of HBM per device.

```python
import math
import jax
import jax.numpy as jnp
import numpy as np
from jax import lax

D = 512
HEADS = 8
FF = 2048
PATCHES = 49
IMG_DEV = 48
HEAD_DIM = 64
EXPERTS = 8
TOK_DEV = 2352
CAP = 624
TOKENS = 75264
DEVICES = 32


def touch_ends(values, key, smallest, largest):
    longest = values.shape.index(max(values.shape))
    spots = []
    for shift in (0, 1):
        where = [jax.random.randint(jax.random.fold_in(key, axis), (), 0, length) for axis, length in enumerate(values.shape)]
        where[longest] = (where[longest] + shift) % values.shape[longest]
        spots.append(tuple(where))
    return values.at[spots[0]].set(smallest).at[spots[1]].set(largest)


def block_levels(stream_key, extent, shards, smallest, top_value):
    def one(position, parts):
        draws = jax.random.uniform(jax.random.fold_in(jax.random.fold_in(stream_key, 6), position), (parts,), jnp.float32, smallest / len(shards), top_value / len(shards))
        return jnp.repeat(jnp.exp(draws), extent[position] // parts).reshape((-1,) + (1,) * (len(extent) - position - 1))

    level = one(*shards[0])
    for cut in shards[1:]:
        level = level * one(*cut)
    return level


def shared_out(own_key, own, number, rows, count, top, limit, skew):
    ranking = jax.random.permutation(own_key, count)
    packed, ordinary = portions_of(count, rows * top, limit, skew, True), portions_of(count, rows * top, limit, skew, False)
    places = jnp.arange(count)

    def named(sizes, rotation):
        used = int((sizes > 0).sum())
        fixed = max(1, used // 4)
        passed = fixed + (places - fixed + rotation * (used - fixed)) % max(1, count - fixed)
        return jnp.zeros((count,), jnp.int32).at[ranking[jnp.where(places < fixed, places, passed)]].set(jnp.asarray(sizes, jnp.int32))

    sizes = jnp.where(number % 4 == 0, named(packed, number // 4), named(ordinary, number - number // 4 - 1))
    mixed = jax.random.permutation(jax.random.fold_in(own, 3), count)
    source_of, receiver = mixed[0:count // 2 * 2:2], mixed[1:count // 2 * 2:2]
    room = jnp.minimum(sizes[source_of] - 1, limit - sizes[receiver]) // 2
    room = jnp.where((source_of == ranking[0]) | (receiver == ranking[0]) | (sizes[receiver] == 0), 0, jnp.maximum(room, 0))
    passed = jax.random.randint(jax.random.fold_in(own, 4), (count // 2,), 0, 1 << 20) % (room + 1)
    sizes = sizes.at[source_of].add(-passed).at[receiver].add(passed)
    items = jnp.searchsorted(jnp.cumsum(sizes), jnp.arange(rows * top), side="right").astype(jnp.int32)
    table = items.reshape(top, rows).T
    table = table[jax.random.permutation(jax.random.fold_in(own, 1), rows)]
    rotation = jax.random.randint(jax.random.fold_in(own, 2), (rows, 1), 0, top)
    return jnp.take_along_axis(table, (jnp.arange(top)[None, :] + rotation) % top, axis=1)


def portions_of(count, total, bound, skew, full):
    loads = [(1 << 20) // math.isqrt(rank ** skew) + 1 for rank in range(1, count + 1)]
    largest = bound if full else min(bound, max(-(-total // count), total * loads[0] // sum(loads)))
    least = 1 if total - largest >= count - 1 else 0
    given, surplus = [largest] + [least] * (count - 1), total - largest - least * (count - 1)
    while surplus > 0:
        free = [i for i in range(1, count) if given[i] < largest] or [i for i in range(1, count) if given[i] < bound]
        mass, budget = sum([loads[i] for i in free]), surplus
        for i in free:
            more = min(bound - given[i], max(1, budget * loads[i] // mass), surplus)
            given[i] = given[i] + more
            surplus = surplus - more
    return np.array(given)


def scatter_about(own_key, shape, width, limit, shards=(), kind=jnp.bfloat16):
    values = jax.random.normal(own_key, shape, jnp.float32) * width
    if len(shards) > 0:
        values = block_levels(own_key, shape, shards, -0.22, 0.18) * values
    return jnp.clip(values, min=-limit, max=limit).astype(kind)


def setup_inputs(seed: int = 0) -> dict:
    arg_keys = jax.random.split(jax.random.key(seed), 12)
    tokens = scatter_about(arg_keys[0], (TOKENS, D), 1.0, 6.0, ((0, 32),))
    gain_one = jnp.clip(1.0 + 0.1 * jax.random.normal(arg_keys[1], (D,), jnp.float32), 0.5, 1.5)
    w_qkv = scatter_about(arg_keys[2], (D, 3 * D), D ** -0.5, 0.25)
    w_proj = scatter_about(arg_keys[3], (D, D), (D // 16) ** -0.5, 1.0)
    gain_two = jnp.clip(1.0 + 0.1 * jax.random.normal(arg_keys[4], (D,), jnp.float32), 0.5, 1.5)
    w_router = scatter_about(arg_keys[5], (D, EXPERTS), (2 * D) ** -0.5, 0.1875, (), jnp.float32)
    w_in = scatter_about(arg_keys[6], (EXPERTS, D, FF), D ** -0.5, 0.25, ((0, 4),))
    w_eout = scatter_about(arg_keys[7], (EXPERTS, FF, D), (max(FF // 512, 1)) ** -0.5, 3.0, ((0, 4),))
    picks_keys = jax.random.split(jax.random.fold_in(arg_keys[8], 1), TOKENS // TOK_DEV)
    picks_turns = jax.random.permutation(jax.random.fold_in(arg_keys[8], 3), TOKENS // TOK_DEV)
    picks = jax.vmap(lambda own, number: shared_out(jax.random.fold_in(arg_keys[8], 2), own, number, TOK_DEV, EXPERTS, 2, CAP, 1))(picks_keys, picks_turns).reshape((TOKENS, 2))
    keep = touch_ends((jax.random.randint(arg_keys[9], (TOKENS, 2), 0, 10) < 9).astype(jnp.int32), jax.random.fold_in(arg_keys[9], 1), 0, 1)
    grad_out = scatter_about(arg_keys[10], (TOKENS, D), 1.0, 6.0, ((0, 32),))
    return {"tokens": tokens, "gain_one": gain_one, "w_qkv": w_qkv, "w_proj": w_proj, "gain_two": gain_two, "w_router": w_router, "w_in": w_in, "w_eout": w_eout, "picks": picks, "keep": keep, "grad_out": grad_out}


@jax.custom_vjp
def low(v):
    return lax.optimization_barrier(v.astype(jnp.bfloat16)).astype(jnp.float32)

@jax.custom_vjp
def low_back(v):
    return v

def low_keep(v):
    return (low(v), None)

def low_pass(kept, grad):
    return (grad,)

def back_keep(v):
    return (v, None)

def back_low(kept, grad):
    return (low(grad),)
low.defvjp(low_keep, low_pass)
low_back.defvjp(back_keep, back_low)

def product(left, right):
    return jnp.dot(left, right, precision=lax.Precision.HIGHEST)

def layer_norm(values, gain):
    mean = lax.optimization_barrier(jnp.mean(values, axis=-1, keepdims=True))
    cent = values - mean
    var = lax.optimization_barrier(jnp.mean(cent * cent, axis=-1, keepdims=True))
    return cent * lax.rsqrt(var + 1e-06) * gain

def attend(block):
    query, keys, values = block
    scores = jnp.einsum('bqhd,bkhd->bhqk', query, keys, precision=lax.Precision.HIGHEST)
    scores = low_back(scores * HEAD_DIM ** (-0.5))
    probs = jax.nn.softmax(scores, axis=-1)
    return jnp.einsum('bhqk,bkhd->bqhd', low(probs), values, precision=lax.Precision.HIGHEST)

def expert_mlp(block):
    rows, w_up, w_down = block
    pre = low_back(product(rows, w_up))
    act = low(jax.nn.gelu(pre, approximate=False))
    return low_back(low(product(act, w_down)))

def pair_index(picks):
    expert_ids = jnp.arange(EXPERTS, dtype=jnp.int32)
    onehot = (picks[:, :, None] == expert_ids).astype(jnp.int32)
    counts = lax.optimization_barrier(jnp.sum(onehot, axis=1)).reshape(DEVICES, TOK_DEV, EXPERTS)
    before = (jnp.cumsum(counts, axis=1) - counts).reshape(TOKENS, EXPERTS)
    slot = lax.optimization_barrier(jnp.sum(before[:, None, :] * onehot, axis=2))
    source = (jnp.arange(TOKENS, dtype=jnp.int32) // TOK_DEV)[:, None]
    return ((picks * DEVICES + source) * CAP + slot).astype(jnp.int32)

def reference(tokens, gain_one, w_qkv, w_proj, gain_two, w_router, w_in, w_eout, picks, keep, grad_out):
    index = pair_index(picks)
    keep_f = keep.astype(jnp.float32)

    def forward(inputs, g_one, qkv_w, proj_w, g_two, router_w, up_w, down_w):
        normed = layer_norm(inputs, g_one)
        qkv = low_back(low(product(low(normed), qkv_w)))
        qkv = qkv.reshape(DEVICES, IMG_DEV, PATCHES, 3, HEADS, HEAD_DIM)
        mixed = lax.map(jax.checkpoint(attend), (qkv[:, :, :, 0], qkv[:, :, :, 1], qkv[:, :, :, 2]))
        attn = low_back(product(low(mixed.reshape(TOKENS, D)), proj_w))
        hidden = inputs + attn
        normed_two = layer_norm(hidden, g_two)
        gates = jax.nn.softmax(product(normed_two, router_w), axis=-1)
        chosen = jnp.take_along_axis(gates, picks, axis=1) * keep_f
        pair_rows = low(normed_two)[:, None, :] * keep_f[:, :, None]
        buffer = jnp.zeros((EXPERTS * DEVICES * CAP, D), jnp.float32)
        buffer = buffer.at[index.reshape(-1)].add(pair_rows.reshape(2 * TOKENS, D))
        buffer = low_back(buffer).reshape(EXPERTS, DEVICES * CAP, D)
        outputs = lax.map(jax.checkpoint(expert_mlp), (buffer, up_w, down_w))
        pair_out = outputs.reshape(EXPERTS * DEVICES * CAP, D)[index]
        return hidden + lax.optimization_barrier(jnp.sum(chosen[:, :, None] * pair_out, axis=1))
    result, pullback = jax.vjp(forward, tokens.astype(jnp.float32), gain_one, w_qkv.astype(jnp.float32), w_proj.astype(jnp.float32), gain_two, w_router, w_in.astype(jnp.float32), w_eout.astype(jnp.float32))
    grads = pullback(grad_out.astype(jnp.float32))
    return (result.astype(jnp.bfloat16), grads[0], grads[1], grads[2], grads[3], grads[4], grads[5], grads[6], grads[7])
```

```python
import functools

import jax
import jax.numpy as jnp
from jax import lax
from jax.experimental import pallas as pl
from jax.experimental.pallas import tpu as pltpu
from jax.sharding import PartitionSpec as P

HEADS = 8
PATCHES = 49
LANES = 128
PAIR = 2 * PATCHES
PAIR_PAD = 112
BLOCK_PAIRS = 4
BLOCK = BLOCK_PAIRS * PAIR
BLOCK_PAD = BLOCK_PAIRS * PAIR_PAD
BF = jnp.bfloat16
F32 = jnp.float32
VMEM_BYTES = 56 * 1024 * 1024


def params():
    return pltpu.CompilerParams(
        dimension_semantics=("arbitrary",), vmem_limit_bytes=VMEM_BYTES
    )


def cost(flops, moved, special=0):
    return pl.CostEstimate(
        flops=int(flops), bytes_accessed=int(moved), transcendentals=int(special)
    )


def whole(shape):
    return pl.BlockSpec(shape, lambda *_: (0,) * len(shape))


def dot(left, right):
    return jnp.dot(left, right, preferred_element_type=F32)


def dot_rt(left, right):
    return lax.dot_general(left, right, (((1,), (1,)), ((), ())), preferred_element_type=F32)


def dot_lt(left, right):
    return lax.dot_general(left, right, (((0,), (0,)), ((), ())), preferred_element_type=F32)


def norm_parts(values):
    mean = jnp.mean(values, axis=-1, keepdims=True)
    cent = values - mean
    factor = lax.rsqrt(jnp.mean(cent * cent, axis=-1, keepdims=True) + 1e-06)
    return cent * factor, factor


def norm_back(grad_normed, normed_hat, factor, gain):
    grad_hat = grad_normed * gain
    inner = grad_hat - jnp.mean(grad_hat, axis=-1, keepdims=True)
    inner = inner - normed_hat * jnp.mean(grad_hat * normed_hat, axis=-1, keepdims=True)
    return factor * inner


def spread_rows(compact, padded):
    for pair in range(BLOCK_PAIRS):
        padded[PAIR_PAD * pair : PAIR_PAD * pair + PAIR] = compact[PAIR * pair : PAIR * pair + PAIR]


def gather_rows(padded, compact):
    for pair in range(BLOCK_PAIRS):
        compact[PAIR * pair : PAIR * pair + PAIR] = padded[PAIR_PAD * pair : PAIR_PAD * pair + PAIR]


def clear_gaps(padded):
    for pair in range(BLOCK_PAIRS):
        low = PAIR_PAD * pair + PAIR
        padded[low : low + PAIR_PAD - PAIR] = jnp.zeros((PAIR_PAD - PAIR, padded.shape[1]), F32)


def image_of(position):
    return (position >= PATCHES).astype(jnp.int32) + (position >= PAIR).astype(jnp.int32)


def same_image():
    rows = lax.broadcasted_iota(jnp.int32, (2 * PAIR_PAD, PAIR_PAD), 0)
    rows = jnp.where(rows >= PAIR_PAD, rows - PAIR_PAD, rows)
    cols = lax.broadcasted_iota(jnp.int32, (2 * PAIR_PAD, PAIR_PAD), 1)
    return image_of(rows) == image_of(cols)


def low_half():
    return lax.broadcasted_iota(jnp.int32, (PAIR_PAD, LANES), 1) < LANES // 2


def two_heads(values, low):
    zero = jnp.zeros_like(values)
    return jnp.concatenate([jnp.where(low, values, zero), jnp.where(low, zero, values)], axis=0)


def one_row(values, low):
    return jnp.where(low, values[:PAIR_PAD], values[PAIR_PAD:])


def attend_kernel(
    tok_ref, gain_one_ref, qkv_w_ref, proj_w_ref, gain_two_ref,
    hidden_ref, rows_ref, qkv_ref, probs_ref, mixed_ref,
    compact, padded,
):
    width = tok_ref.shape[1]
    factor_qk = (width // HEADS) ** (-0.5)
    clear_gaps(padded)
    inputs = tok_ref[...].astype(F32)
    compact[...] = norm_parts(inputs)[0] * gain_one_ref[...]
    spread_rows(compact, padded)
    qkv_ref[...] = dot(padded[...].astype(BF), qkv_w_ref[...]).astype(BF)
    valid = same_image()
    low = low_half()
    for pair in range(BLOCK_PAIRS):
        rows = slice(PAIR_PAD * pair, PAIR_PAD * (pair + 1))
        for two in range(width // LANES):
            cols = slice(LANES * two, LANES * (two + 1))
            query = qkv_ref[rows, cols]
            keys = qkv_ref[rows, width + LANES * two : width + LANES * (two + 1)]
            values = qkv_ref[rows, 2 * width + LANES * two : 2 * width + LANES * (two + 1)]
            scores = jnp.where(valid, dot_rt(two_heads(query, low), keys), -1e30)
            highest = jnp.max(scores, axis=-1, keepdims=True)
            expo = jnp.exp((scores - highest) * factor_qk)
            probs = (expo / jnp.sum(expo, axis=-1, keepdims=True)).astype(BF)
            step = (pair * (width // LANES) + two) * 2 * PAIR_PAD
            probs_ref[step : step + 2 * PAIR_PAD, :] = probs
            mixed_ref[rows, cols] = one_row(dot(probs, values), low).astype(BF)
    padded[...] = dot(mixed_ref[...], proj_w_ref[...])
    gather_rows(padded, compact)
    hidden = inputs + compact[...]
    hidden_ref[...] = hidden
    rows_ref[...] = (norm_parts(hidden)[0] * gain_two_ref[...]).astype(BF)


def attend(tokens, gain_one, w_qkv, w_proj, gain_two):
    count, width = tokens.shape
    blocks = count // BLOCK
    prob_rows = BLOCK_PAIRS * (width // LANES) * 2 * PAIR_PAD
    row = lambda shape: pl.BlockSpec(shape, lambda step: (step, 0))
    flops = 2 * blocks * BLOCK_PAD * width * (4 * width + 4 * PAIR_PAD)
    return pl.pallas_call(
        attend_kernel,
        grid=(blocks,),
        in_specs=[
            row((BLOCK, width)), whole((1, width)), whole(w_qkv.shape), whole(w_proj.shape),
            whole((1, width)),
        ],
        out_specs=[
            row((BLOCK, width)), row((BLOCK, width)), row((BLOCK_PAD, 3 * width)),
            row((prob_rows, PAIR_PAD)), row((BLOCK_PAD, width)),
        ],
        out_shape=[
            jax.ShapeDtypeStruct((count, width), F32),
            jax.ShapeDtypeStruct((count, width), BF),
            jax.ShapeDtypeStruct((blocks * BLOCK_PAD, 3 * width), BF),
            jax.ShapeDtypeStruct((blocks * prob_rows, PAIR_PAD), BF),
            jax.ShapeDtypeStruct((blocks * BLOCK_PAD, width), BF),
        ],
        scratch_shapes=[pltpu.VMEM((BLOCK, width), F32), pltpu.VMEM((BLOCK_PAD, width), F32)],
        compiler_params=params(),
        cost_estimate=cost(flops, 30e6, blocks * prob_rows * LANES),
        name="attend",
    )(tokens, gain_one[None, :], w_qkv, w_proj, gain_two[None, :])


def dispatch_kernel(window, starts_ref, src_ref, index_ref, *refs):
    outs, total = refs, refs[0].shape[0]
    step = pl.program_id(0)
    experts = starts_ref.shape[1]
    owners = experts // len(outs)
    capacity = total // owners
    block = src_ref.shape[0]

    @pl.when(step == 0)
    def _():
        for out in outs:
            out[...] = jnp.zeros(out.shape, out.dtype)

    place = lax.broadcasted_iota(jnp.int32, (window, block), 0)
    for local, out in enumerate(outs):
        first, second = index_ref[0, 0:1, :], index_ref[0, 1:2, :]
        shift = local * total
        first = jnp.where((first >= shift) & (first < shift + total), first - shift, -1)
        second = jnp.where((second >= shift) & (second < shift + total), second - shift, -1)

        def one_expert(owner, carry):
            expert = local * owners + owner
            low = owner * capacity + starts_ref[step, expert]
            high = owner * capacity + starts_ref[step + 1, expert]
            base = (low // 16) * 16

            def one_window(chunk, inner):
                begin = base + chunk * window
                at = pl.multiple_of(jnp.minimum(begin, total - window), 16)
                near = (first >= begin) & (first >= low) & (first < high)
                far = (second >= begin) & (second >= low) & (second < high)
                hit = jnp.where(near, first - at, jnp.where(far, second - at, -1))
                spot = (place == hit).astype(F32).astype(BF)
                held = out[pl.ds(at, window), :].astype(F32)
                out[pl.ds(at, window), :] = (held + dot(spot, src_ref[...])).astype(BF)
                return inner

            return lax.fori_loop(0, (high - base + window - 1) // window, one_window, carry)

        lax.fori_loop(0, owners, one_expert, 0)


def dispatch(src, starts, index_rows, local, capacity):
    count, width = src.shape
    blocks = count // BLOCK
    experts = starts.shape[1]
    total = (experts // local) * capacity
    window = LANES
    return pl.pallas_call(
        functools.partial(dispatch_kernel, window),
        grid_spec=pltpu.PrefetchScalarGridSpec(
            num_scalar_prefetch=1,
            grid=(blocks,),
            in_specs=[
                pl.BlockSpec((BLOCK, width), lambda step, *_: (step, 0)),
                pl.BlockSpec((1, 2, BLOCK), lambda step, *_: (step, 0, 0)),
            ],
            out_specs=[whole((total, width))] * local,
        ),
        out_shape=[jax.ShapeDtypeStruct((total, width), BF)] * local,
        compiler_params=params(),
        cost_estimate=cost(12e9, 8e6),
        name="dispatch",
    )(starts, src, index_rows)


def combine_block(window, step, starts_ref, index_ref, bufs, acc):
    total = bufs[0].shape[0]
    experts = starts_ref.shape[1]
    owners = experts // len(bufs)
    capacity = total // owners
    block = index_ref.shape[0]
    first = jnp.broadcast_to(index_ref[:, 0:1], (block, window))
    second = jnp.broadcast_to(index_ref[:, 1:2], (block, window))
    place = lax.broadcasted_iota(jnp.int32, (block, window), 1)
    acc[...] = jnp.zeros(acc.shape, F32)
    for local, buf in enumerate(bufs):
        shift = local * total

        def one_expert(owner, carry):
            expert = local * owners + owner
            low = owner * capacity + starts_ref[step, expert]
            high = owner * capacity + starts_ref[step + 1, expert]
            base = (low // 16) * 16

            def one_window(chunk, inner):
                begin = base + chunk * window
                at = pl.multiple_of(jnp.minimum(begin, total - window), 16)
                seen = place + (at + shift)
                fresh = (seen >= begin + shift) & (seen < high + shift)
                hit = ((seen == first) | (seen == second)) & fresh
                acc[...] += dot(hit.astype(F32).astype(BF), buf[pl.ds(at, window), :])
                return inner

            return lax.fori_loop(0, (high - base + window - 1) // window, one_window, carry)

        lax.fori_loop(0, owners, one_expert, 0)


def combine_window(capacity):
    return 2 * LANES if capacity > 2 * LANES else LANES


def top_kernel(window, local, starts_ref, index_ref, hidden_ref, *refs):
    bufs, out_ref, acc = refs[:local], refs[local], refs[local + 1]
    combine_block(window, pl.program_id(0), starts_ref, index_ref, bufs, acc)
    out_ref[...] = (hidden_ref[...] + acc[...]).astype(BF)


def top(starts, index, hidden, bufs, capacity):
    count, width = hidden.shape
    blocks = count // BLOCK
    local = len(bufs)
    row = lambda shape: pl.BlockSpec(shape, lambda step, *_: (step, 0))
    return pl.pallas_call(
        functools.partial(top_kernel, combine_window(capacity), local),
        grid_spec=pltpu.PrefetchScalarGridSpec(
            num_scalar_prefetch=1,
            grid=(blocks,),
            in_specs=[row((BLOCK, 2)), row((BLOCK, width))] + [whole(bufs[0].shape)] * local,
            out_specs=row((BLOCK, width)),
            scratch_shapes=[pltpu.VMEM((BLOCK, width), F32)],
        ),
        out_shape=jax.ShapeDtypeStruct((count, width), BF),
        compiler_params=params(),
        cost_estimate=cost(12e9, 12e6),
        name="top",
    )(starts, index, hidden, *bufs)


def gelu_parts(values):
    size = jnp.abs(values)
    near = 1.0 / (1.0 + (0.3275911 * 0.7071067811865476) * size)
    expo = jnp.exp(-0.5 * (values * values))
    poly = 0.5 * 1.061405429
    for term in (-1.453152027, 1.421413741, -0.284496736, 0.254829592):
        poly = poly * near + 0.5 * term
    tail = poly * near * expo
    share = jnp.where(values >= 0, 1.0 - tail, tail)
    return values * share, share + values * (0.3989422804014327 * expo)


def expert_kernel(
    experts, fcut, mine_ref, x_ref, dy_ref, up_ref, down_ref, router_ref, back_ref,
    out_ref, dx_ref, gup_ref, gdown_ref, grouter_ref,
    acc_up, acc_down, acc_router, acc_out, acc_dx,
):
    step = pl.program_id(0)
    hidden_units = up_ref.shape[1]

    @pl.when(step == 0)
    def _():
        acc_up[...] = jnp.zeros(acc_up.shape, F32)
        acc_down[...] = jnp.zeros(acc_down.shape, F32)
        acc_router[...] = jnp.zeros(acc_router.shape, F32)

    rows = x_ref[...]
    count = rows.shape[0]
    logits = dot(rows, router_ref[...])
    logits = logits[:, :LANES] + logits[:, LANES:]
    lane = lax.broadcasted_iota(jnp.int32, (count, LANES), 1)
    logits = jnp.where(lane < experts, logits, -1e30)
    expo = jnp.exp(logits - jnp.max(logits, axis=-1, keepdims=True))
    gates = expo / jnp.sum(expo, axis=-1, keepdims=True)
    own = (lane == mine_ref[0]).astype(F32)
    chosen = jnp.sum(gates * own, axis=-1, keepdims=True)
    pair = (chosen * dy_ref[...].astype(F32)).astype(BF)
    rows_t = rows.T
    pair_t = pair.T
    inner = jnp.zeros((count, LANES), F32)
    for low in range(0, hidden_units, fcut):
        cols = slice(low, low + fcut)
        pre = dot(rows, up_ref[:, cols])
        grad_act = dot_rt(pair, down_ref[cols, :])
        act, slope = gelu_parts(pre)
        both = act * grad_act
        for part in range(0, fcut, LANES):
            inner = inner + both[:, part : part + LANES]
        act = act.astype(BF)
        grad_pre = (grad_act * slope).astype(BF)
        acc_up[:, cols] += dot(rows_t, grad_pre)
        acc_down[:, cols] += dot(pair_t, act)
        if low == 0:
            acc_out[...] = dot(act, down_ref[cols, :])
            acc_dx[...] = dot_rt(grad_pre, up_ref[:, cols])
        else:
            acc_out[...] += dot(act, down_ref[cols, :])
            acc_dx[...] += dot_rt(grad_pre, up_ref[:, cols])
    grad_logits = jnp.sum(inner, axis=-1, keepdims=True) * (own - gates)
    head = grad_logits.astype(BF)
    rest = (grad_logits - head.astype(F32)).astype(BF)
    acc_router[...] += dot(rows_t, jnp.concatenate([head, rest], axis=1))
    out_ref[...] = (chosen * acc_out[...]).astype(BF)
    dx_ref[...] = (acc_dx[...] + dot(jnp.concatenate([head, head], axis=1), back_ref[...])).astype(BF)

    @pl.when(step == pl.num_programs(0) - 1)
    def _():
        gup_ref[...] = acc_up[...].astype(BF)
        for low in range(0, hidden_units, 512):
            gdown_ref[low : low + 512, :] = acc_down[:, low : low + 512].T.astype(BF)
        grouter_ref[...] = acc_router[:, :LANES] + acc_router[:, LANES:]


def expert_pass(mine, rows, grads, w_up, w_down, router, router_back, experts, capacity):
    count, width = rows.shape
    units = w_up.shape[1]
    parts = count // capacity
    times = max(n for n in range(1, parts + 1) if parts % n == 0 and n * capacity <= max(640, capacity))
    tile = times * capacity
    fcut = min(512, units)
    row = lambda shape: pl.BlockSpec(shape, lambda step, *_: (step, 0))
    return pl.pallas_call(
        functools.partial(expert_kernel, experts, fcut),
        grid_spec=pltpu.PrefetchScalarGridSpec(
            num_scalar_prefetch=1,
            grid=(count // tile,),
            in_specs=[
                row((tile, width)), row((tile, width)), whole(w_up.shape), whole(w_down.shape),
                whole(router.shape), whole(router_back.shape),
            ],
            out_specs=[
                row((tile, width)), row((tile, width)), whole(w_up.shape), whole(w_down.shape),
                whole((width, LANES)),
            ],
            scratch_shapes=[
                pltpu.VMEM((width, units), F32),
                pltpu.VMEM((width, units), F32),
                pltpu.VMEM((width, 2 * LANES), F32),
                pltpu.VMEM((tile, width), F32),
                pltpu.VMEM((tile, width), F32),
            ],
        ),
        out_shape=[
            jax.ShapeDtypeStruct((count, width), BF),
            jax.ShapeDtypeStruct((count, width), BF),
            jax.ShapeDtypeStruct(w_up.shape, BF),
            jax.ShapeDtypeStruct(w_down.shape, BF),
            jax.ShapeDtypeStruct((width, LANES), F32),
        ],
        compiler_params=params(),
        cost_estimate=cost(12 * count * width * units, 30e6, 2 * count * units),
        name="expert_pass",
    )(mine, rows, grads, w_up, w_down, router, router_back)


def back_kernel(
    window, local, starts_ref, index_ref, hidden_ref, tok_ref, dy_ref, qkv_ref, probs_ref,
    mixed_ref, gain_one_ref, qkv_w_ref, proj_w_ref, gain_two_ref, *refs,
):
    bufs = refs[:local]
    gtok_ref, gqkv_ref, gproj_ref, ggain_one_ref, ggain_two_ref = refs[local : local + 5]
    acc, compact, padded, dqkv = refs[local + 5 :]
    step = pl.program_id(0)
    width = tok_ref.shape[1]
    factor_qk = (width // HEADS) ** (-0.5)

    @pl.when(step == 0)
    def _():
        for ref in (gqkv_ref, gproj_ref, ggain_one_ref, ggain_two_ref):
            ref[...] = jnp.zeros(ref.shape, F32)

    combine_block(window, step, starts_ref, index_ref, bufs, acc)
    clear_gaps(padded)
    hat_two, scale_two = norm_parts(hidden_ref[...])
    grad_normed = acc[...]
    ggain_two_ref[...] += jnp.sum(grad_normed * hat_two, axis=0, keepdims=True)
    grad_hidden = dy_ref[...].astype(F32) + norm_back(
        grad_normed, hat_two, scale_two, gain_two_ref[...]
    )
    gtok_ref[...] = grad_hidden
    compact[...] = grad_hidden
    spread_rows(compact, padded)
    grad_attn = padded[...].astype(BF)
    gproj_ref[...] += dot_lt(mixed_ref[...], grad_attn)
    grad_mixed = dot_rt(grad_attn, proj_w_ref[...]).astype(BF)
    low = low_half()
    for pair in range(BLOCK_PAIRS):
        rows = slice(PAIR_PAD * pair, PAIR_PAD * (pair + 1))
        for two in range(width // LANES):
            cols = slice(LANES * two, LANES * (two + 1))
            key_cols = slice(width + LANES * two, width + LANES * (two + 1))
            value_cols = slice(2 * width + LANES * two, 2 * width + LANES * (two + 1))
            at = (pair * (width // LANES) + two) * 2 * PAIR_PAD
            probs = probs_ref[at : at + 2 * PAIR_PAD, :]
            wide = probs.astype(F32)
            grad_out = two_heads(grad_mixed[rows, cols], low)
            grad_probs = dot_rt(grad_out, qkv_ref[rows, value_cols])
            meet = jnp.sum(wide * grad_probs, axis=-1, keepdims=True)
            grad_scores = (wide * (grad_probs - meet) * factor_qk).astype(BF)
            grad_query = one_row(dot(grad_scores, qkv_ref[rows, key_cols]), low)
            dqkv[rows, cols] = grad_query.astype(BF)
            dqkv[rows, key_cols] = dot_lt(grad_scores, two_heads(qkv_ref[rows, cols], low)).astype(BF)
            dqkv[rows, value_cols] = dot_lt(probs, grad_out).astype(BF)
    hat_one, scale_one = norm_parts(tok_ref[...].astype(F32))
    compact[...] = hat_one * gain_one_ref[...]
    spread_rows(compact, padded)
    act_one = padded[...].astype(BF)
    gqkv_ref[...] += dot_lt(act_one, dqkv[...])
    padded[...] = dot_rt(dqkv[...], qkv_w_ref[...])
    gather_rows(padded, compact)
    grad_act_one = compact[...]
    ggain_one_ref[...] += jnp.sum(grad_act_one * hat_one, axis=0, keepdims=True)
    gtok_ref[...] += norm_back(grad_act_one, hat_one, scale_one, gain_one_ref[...])


def back(starts, index, hidden, tokens, dy, qkv, probs, mixed, gain_one, w_qkv, w_proj, gain_two, bufs, capacity):
    count, width = tokens.shape
    blocks = count // BLOCK
    local = len(bufs)
    row = lambda shape: pl.BlockSpec(shape, lambda step, *_: (step, 0))
    flops = 2 * blocks * BLOCK_PAD * width * (8 * width + 10 * PAIR_PAD)
    return pl.pallas_call(
        functools.partial(back_kernel, combine_window(capacity), local),
        grid_spec=pltpu.PrefetchScalarGridSpec(
            num_scalar_prefetch=1,
            grid=(blocks,),
            in_specs=[
                row((BLOCK, 2)), row((BLOCK, width)), row((BLOCK, width)), row((BLOCK, width)),
                row((BLOCK_PAD, 3 * width)), row((probs.shape[0] // blocks, PAIR_PAD)),
                row((BLOCK_PAD, width)),
                whole((1, width)), whole(w_qkv.shape), whole(w_proj.shape), whole((1, width)),
            ] + [whole(bufs[0].shape)] * local,
            out_specs=[
                row((BLOCK, width)), whole(w_qkv.shape), whole(w_proj.shape),
                whole((1, width)), whole((1, width)),
            ],
            scratch_shapes=[
                pltpu.VMEM((BLOCK, width), F32),
                pltpu.VMEM((BLOCK, width), F32),
                pltpu.VMEM((BLOCK_PAD, width), F32),
                pltpu.VMEM((BLOCK_PAD, 3 * width), BF),
            ],
        ),
        out_shape=[
            jax.ShapeDtypeStruct((count, width), F32),
            jax.ShapeDtypeStruct(w_qkv.shape, F32),
            jax.ShapeDtypeStruct(w_proj.shape, F32),
            jax.ShapeDtypeStruct((1, width), F32),
            jax.ShapeDtypeStruct((1, width), F32),
        ],
        compiler_params=params(),
        cost_estimate=cost(flops + 12e9, 40e6),
        name="back",
    )(
        starts, index, hidden, tokens, dy, qkv, probs, mixed, gain_one[None, :], w_qkv, w_proj,
        gain_two[None, :], *bufs,
    )


def places(picks, keep, experts, local, capacity):
    count = picks.shape[0]
    owners = experts // local
    picks_t, keep_t = picks.T, keep.T
    ids = jnp.arange(experts, dtype=jnp.int32)[:, None]
    named = ((picks_t[0][None, :] == ids) | (picks_t[1][None, :] == ids)).astype(jnp.int32)
    before = jnp.cumsum(named, axis=1) - named
    slot = jnp.stack([jnp.sum(jnp.where(picks_t[c][None, :] == ids, before, 0), axis=0) for c in (0, 1)])
    home = (picks_t % local) * owners + picks_t // local
    index = jnp.where(keep_t > 0, home * capacity + slot, -1)
    starts = jnp.concatenate([before[:, ::BLOCK], before[:, -1:] + named[:, -1:]], axis=1)
    order = jnp.arange(experts, dtype=jnp.int32).reshape(owners, local).T.reshape(-1)
    starts = starts[order].T
    index_rows = index.reshape(2, count // BLOCK, BLOCK).transpose(1, 0, 2)
    return index.T, index_rows, starts


def per_device(
    tokens, gain_one, w_qkv, w_proj, gain_two, w_router, w_in, w_eout, picks, keep, grad_out
):
    count, width = tokens.shape
    local = w_in.shape[0]
    owners = lax.axis_size("expert")
    experts = local * owners
    capacity = 8 * ((21 * count + 80 * experts - 1) // (80 * experts))

    def swap(part):
        sent = part.reshape(owners, capacity, width)
        got = lax.all_to_all(sent, "expert", split_axis=0, concat_axis=0, tiled=True)
        return got.reshape(owners * capacity, width)

    index, index_rows, starts = places(picks, keep, experts, local, capacity)
    grad_parts = [swap(part) for part in dispatch(grad_out, starts, index_rows, local, capacity)]
    hidden, rows, qkv, probs, mixed = attend(tokens, gain_one, w_qkv, w_proj, gain_two)
    row_parts = [swap(part) for part in dispatch(rows, starts, index_rows, local, capacity)]
    head = w_router.astype(BF)
    rest = (w_router - head.astype(F32)).astype(BF)
    gap = ((0, 0), (0, LANES - experts))
    router = jnp.concatenate([jnp.pad(head, gap), jnp.pad(rest, gap)], axis=1)
    router_back = jnp.concatenate([jnp.pad(head, gap).T, jnp.pad(rest, gap).T], axis=0)
    outs, downs, grad_ups, grad_downs, grad_router = [], [], [], [], 0
    for part in range(local):
        mine = (lax.axis_index("expert") * local + part).astype(jnp.int32)[None]
        out, grad_rows, grad_up, grad_down, router_part = expert_pass(
            mine, row_parts[part], grad_parts[part], w_in[part], w_eout[part], router,
            router_back, experts, capacity,
        )
        downs.append(swap(grad_rows))
        outs.append(swap(out))
        grad_ups.append(lax.psum_scatter(grad_up, "dp", scatter_dimension=0, tiled=True))
        grad_downs.append(lax.psum_scatter(grad_down, "dp", scatter_dimension=0, tiled=True))
        grad_router = grad_router + router_part[:, :experts]
    grad_tokens, grad_qkv, grad_proj, grad_gain_one, grad_gain_two = back(
        starts, index, hidden, tokens, grad_out, qkv, probs, mixed, gain_one, w_qkv, w_proj,
        gain_two, downs, capacity,
    )
    block_out = top(starts, index, hidden, outs, capacity)
    both = ("dp", "expert")
    big = lax.psum((grad_qkv.astype(BF), grad_proj.astype(BF)), both)
    small = lax.psum((grad_gain_one[0], grad_gain_two[0], grad_router), both)
    return (
        block_out,
        grad_tokens,
        small[0],
        big[0].astype(F32),
        big[1].astype(F32),
        small[1],
        small[2],
        jnp.stack(grad_ups).astype(F32),
        jnp.stack(grad_downs).astype(F32),
    )


def solution(mesh):
    rows = P(("dp", "expert"), None)
    experts = P("expert", None, None)
    return jax.shard_map(
        per_device,
        mesh=mesh,
        in_specs=(rows, P(), P(), P(), P(), P(), experts, experts, rows, rows, rows),
        out_specs=(
            rows, rows, P(), P(), P(), P(), P(), P("expert", "dp", None), P("expert", "dp", None),
        ),
        check_vma=False,
    )
```

```python
import functools

import jax
import jax.numpy as jnp
from jax import lax
from jax.experimental import pallas as pl
from jax.experimental.pallas import tpu as pltpu
from jax.sharding import PartitionSpec as P

HEADS = 8
PATCHES = 49
LANES = 128
PAIR = 2 * PATCHES
PAIR_PAD = 112
BLOCK_PAIRS = 4
BLOCK = BLOCK_PAIRS * PAIR
BLOCK_PAD = BLOCK_PAIRS * PAIR_PAD
BF = jnp.bfloat16
F32 = jnp.float32
VMEM_BYTES = 56 * 1024 * 1024
TILE_ROWS = 640
FCUT = 1024


def params():
    return pltpu.CompilerParams(
        dimension_semantics=("arbitrary",), vmem_limit_bytes=VMEM_BYTES
    )


def cost(flops, moved, special=0):
    return pl.CostEstimate(
        flops=int(flops), bytes_accessed=int(moved), transcendentals=int(special)
    )


def whole(shape):
    return pl.BlockSpec(shape, lambda *_: (0,) * len(shape))


def dot(left, right):
    return jnp.dot(left, right, preferred_element_type=F32)


def dot_rt(left, right):
    return lax.dot_general(left, right, (((1,), (1,)), ((), ())), preferred_element_type=F32)


def dot_lt(left, right):
    return lax.dot_general(left, right, (((0,), (0,)), ((), ())), preferred_element_type=F32)


def norm_parts(values):
    mean = jnp.mean(values, axis=-1, keepdims=True)
    cent = values - mean
    factor = lax.rsqrt(jnp.mean(cent * cent, axis=-1, keepdims=True) + 1e-06)
    return cent * factor, factor


def norm_back(grad_normed, normed_hat, factor, gain):
    grad_hat = grad_normed * gain
    inner = grad_hat - jnp.mean(grad_hat, axis=-1, keepdims=True)
    inner = inner - normed_hat * jnp.mean(grad_hat * normed_hat, axis=-1, keepdims=True)
    return factor * inner


def spread_rows(compact, padded):
    for pair in range(BLOCK_PAIRS):
        padded[PAIR_PAD * pair : PAIR_PAD * pair + PAIR] = compact[PAIR * pair : PAIR * pair + PAIR]


def gather_rows(padded, compact):
    for pair in range(BLOCK_PAIRS):
        compact[PAIR * pair : PAIR * pair + PAIR] = padded[PAIR_PAD * pair : PAIR_PAD * pair + PAIR]


def clear_gaps(padded):
    for pair in range(BLOCK_PAIRS):
        low = PAIR_PAD * pair + PAIR
        padded[low : low + PAIR_PAD - PAIR] = jnp.zeros((PAIR_PAD - PAIR, padded.shape[1]), F32)


def image_of(position):
    return (position >= PATCHES).astype(jnp.int32) + (position >= PAIR).astype(jnp.int32)


def same_image():
    rows = lax.broadcasted_iota(jnp.int32, (2 * PAIR_PAD, PAIR_PAD), 0)
    rows = jnp.where(rows >= PAIR_PAD, rows - PAIR_PAD, rows)
    cols = lax.broadcasted_iota(jnp.int32, (2 * PAIR_PAD, PAIR_PAD), 1)
    return image_of(rows) == image_of(cols)


def low_half():
    return lax.broadcasted_iota(jnp.int32, (PAIR_PAD, LANES), 1) < LANES // 2


def two_heads(values, low):
    zero = jnp.zeros_like(values)
    return jnp.concatenate([jnp.where(low, values, zero), jnp.where(low, zero, values)], axis=0)


def one_row(values, low):
    return jnp.where(low, values[:PAIR_PAD], values[PAIR_PAD:])


def attend_kernel(
    tok_ref, gain_one_ref, qkv_w_ref, proj_w_ref, gain_two_ref,
    hidden_ref, rows_ref, qkv_ref, probs_ref, mixed_ref,
    compact, padded,
):
    width = tok_ref.shape[1]
    factor_qk = (width // HEADS) ** (-0.5)
    clear_gaps(padded)
    inputs = tok_ref[...].astype(F32)
    compact[...] = norm_parts(inputs)[0] * gain_one_ref[...]
    spread_rows(compact, padded)
    qkv_ref[...] = dot(padded[...].astype(BF), qkv_w_ref[...]).astype(BF)
    valid = same_image()
    low = low_half()
    for pair in range(BLOCK_PAIRS):
        rows = slice(PAIR_PAD * pair, PAIR_PAD * (pair + 1))
        for two in range(width // LANES):
            cols = slice(LANES * two, LANES * (two + 1))
            query = qkv_ref[rows, cols]
            keys = qkv_ref[rows, width + LANES * two : width + LANES * (two + 1)]
            values = qkv_ref[rows, 2 * width + LANES * two : 2 * width + LANES * (two + 1)]
            scores = jnp.where(valid, dot_rt(two_heads(query, low), keys), -1e30)
            highest = jnp.max(scores, axis=-1, keepdims=True)
            expo = jnp.exp((scores - highest) * factor_qk)
            probs = (expo / jnp.sum(expo, axis=-1, keepdims=True)).astype(BF)
            step = (pair * (width // LANES) + two) * 2 * PAIR_PAD
            probs_ref[step : step + 2 * PAIR_PAD, :] = probs
            mixed_ref[rows, cols] = one_row(dot(probs, values), low).astype(BF)
    padded[...] = dot(mixed_ref[...], proj_w_ref[...])
    gather_rows(padded, compact)
    hidden = inputs + compact[...]
    hidden_ref[...] = hidden
    rows_ref[...] = (norm_parts(hidden)[0] * gain_two_ref[...]).astype(BF)


def attend(tokens, gain_one, w_qkv, w_proj, gain_two):
    count, width = tokens.shape
    blocks = count // BLOCK
    prob_rows = BLOCK_PAIRS * (width // LANES) * 2 * PAIR_PAD
    row = lambda shape: pl.BlockSpec(shape, lambda step: (step, 0))
    flops = 2 * blocks * BLOCK_PAD * width * (4 * width + 4 * PAIR_PAD)
    return pl.pallas_call(
        attend_kernel,
        grid=(blocks,),
        in_specs=[
            row((BLOCK, width)), whole((1, width)), whole(w_qkv.shape), whole(w_proj.shape),
            whole((1, width)),
        ],
        out_specs=[
            row((BLOCK, width)), row((BLOCK, width)), row((BLOCK_PAD, 3 * width)),
            row((prob_rows, PAIR_PAD)), row((BLOCK_PAD, width)),
        ],
        out_shape=[
            jax.ShapeDtypeStruct((count, width), F32),
            jax.ShapeDtypeStruct((count, width), BF),
            jax.ShapeDtypeStruct((blocks * BLOCK_PAD, 3 * width), BF),
            jax.ShapeDtypeStruct((blocks * prob_rows, PAIR_PAD), BF),
            jax.ShapeDtypeStruct((blocks * BLOCK_PAD, width), BF),
        ],
        scratch_shapes=[pltpu.VMEM((BLOCK, width), F32), pltpu.VMEM((BLOCK_PAD, width), F32)],
        compiler_params=params(),
        cost_estimate=cost(flops, 30e6, blocks * prob_rows * LANES),
        name="attend",
    )(tokens, gain_one[None, :], w_qkv, w_proj, gain_two[None, :])


def place_kernel(capacity, ids_ref, picks_ref, index_ref, starts_ref, carry):
    step = pl.program_id(0)

    @pl.when(step == 0)
    def _():
        carry[...] = jnp.zeros(carry.shape, F32)
        starts_ref[...] = jnp.zeros(starts_ref.shape, jnp.int32)

    experts, block = ids_ref.shape[0], picks_ref.shape[2]
    ids = ids_ref[...]
    names = [picks_ref[0, c : c + 1, :] == ids for c in (0, 1)]
    named = (names[0] | names[1]).astype(F32)
    earlier = lax.broadcasted_iota(jnp.int32, (block, block), 0) < lax.broadcasted_iota(
        jnp.int32, (block, block), 1
    )
    before = dot(named.astype(BF), earlier.astype(F32).astype(BF)) + carry[:, 0:1]
    spot = before + (lax.broadcasted_iota(jnp.int32, (experts, block), 0) * capacity).astype(F32)
    for c in (0, 1):
        found = jnp.sum(jnp.where(names[c], spot, 0.0), axis=0, keepdims=True).astype(jnp.int32)
        index_ref[0, c : c + 1, :] = jnp.where(picks_ref[0, 2 + c : 3 + c, :] > 0, found, -1)
    after = carry[...] + jnp.sum(named, axis=1, keepdims=True)
    carry[...] = after
    lane = lax.broadcasted_iota(jnp.int32, (experts, LANES), 1)
    starts_ref[...] = jnp.where(lane == step + 1, after.astype(jnp.int32), starts_ref[...])


def places(ids, picks, keep, capacity):
    count = picks.shape[0]
    blocks = count // BLOCK
    experts = ids.shape[0]
    turned = jnp.concatenate([picks, keep], axis=1).reshape(blocks, BLOCK, 4).transpose(0, 2, 1)
    return pl.pallas_call(
        functools.partial(place_kernel, capacity),
        grid=(blocks,),
        in_specs=[whole((experts, 1)), pl.BlockSpec((1, 4, BLOCK), lambda step: (step, 0, 0))],
        out_specs=[
            pl.BlockSpec((1, 2, BLOCK), lambda step: (step, 0, 0)), whole((experts, LANES)),
        ],
        out_shape=[
            jax.ShapeDtypeStruct((blocks, 2, BLOCK), jnp.int32),
            jax.ShapeDtypeStruct((experts, LANES), jnp.int32),
        ],
        scratch_shapes=[pltpu.VMEM((experts, LANES), F32)],
        compiler_params=params(),
        cost_estimate=cost(1e8, 1e5),
        name="places",
    )(ids[:, None], turned)


def window_rows(experts, capacity):
    return min(capacity, 16 * -(-2 * BLOCK * 8 // (5 * 16 * experts)))


def window_at(starts_ref, expert, step, turn, window, capacity):
    low = starts_ref[expert, step]
    begin = (low // 16) * 16 + turn * window
    at = pl.multiple_of(jnp.minimum(begin, capacity - window), 16)
    return begin, starts_ref[expert, step + 1], at


def turns(starts_ref, step, experts, window):
    most = 0
    for expert in experts:
        low = (starts_ref[expert, step] // 16) * 16
        most = jnp.maximum(most, (starts_ref[expert, step + 1] - low + window - 1) // window)
    return most


def dispatch_kernel(window, capacity, plan, sources, starts_ref, index_ref, *refs):
    src_refs, outs, (spots, got) = refs[:sources], refs[sources:-2], refs[-2:]
    owners = outs[0].shape[0]
    step = pl.program_id(0)
    named = [owners * part + owner for part, _ in plan for owner in range(owners)]

    @pl.when(step == 0)
    def _():
        for out in outs:
            out[...] = jnp.zeros(out.shape, out.dtype)

    place = lax.broadcasted_iota(jnp.int32, (window, index_ref.shape[2]), 0)
    first, second = index_ref[0, 0:1, :], index_ref[0, 1:2, :]

    def one_turn(turn, carry):
        for (part, used), out in zip(plan, outs):
            spans = []
            for owner in range(owners):
                expert = part * owners + owner
                begin, _, at = window_at(starts_ref, expert, step, turn, window, capacity)
                shift = expert * capacity
                near = jnp.where(first >= shift + begin, first - (shift + at), -1)
                far = jnp.where(second >= shift + begin, second - (shift + at), -1)
                hit = jnp.where((near >= 0) & (near < window), near, far)
                spots[window * owner : window * (owner + 1), :] = (
                    (place == hit).astype(F32).astype(BF)
                )
                spans.append(at)
            for order, which in enumerate(used):
                got[...] = dot(spots[...], src_refs[which][...])
                for owner, at in enumerate(spans):
                    rows = pl.ds(pl.multiple_of(at + order * capacity, 16), window)
                    held = out[owner, rows, :].astype(F32)
                    out[owner, rows, :] = (
                        held + got[window * owner : window * (owner + 1), :]
                    ).astype(BF)
        return carry

    lax.fori_loop(0, turns(starts_ref, step, named, window), one_turn, 0)


def dispatch(srcs, starts, index_rows, owners, capacity, plan):
    count, width = srcs[0].shape
    window = window_rows(starts.shape[0], capacity)
    shapes = [(owners, len(used) * capacity, width) for _, used in plan]
    return pl.pallas_call(
        functools.partial(dispatch_kernel, window, capacity, plan, len(srcs)),
        grid_spec=pltpu.PrefetchScalarGridSpec(
            num_scalar_prefetch=1,
            grid=(count // BLOCK,),
            in_specs=[pl.BlockSpec((1, 2, BLOCK), lambda step, *_: (step, 0, 0))]
            + [pl.BlockSpec((BLOCK, width), lambda step, *_: (step, 0))] * len(srcs),
            out_specs=[whole(shape) for shape in shapes],
            scratch_shapes=[
                pltpu.VMEM((owners * window, BLOCK), BF),
                pltpu.VMEM((owners * window, width), F32),
            ],
        ),
        out_shape=[jax.ShapeDtypeStruct(shape, BF) for shape in shapes],
        compiler_params=params(),
        cost_estimate=cost(6e9, 8e6),
        name="dispatch",
    )(starts, index_rows, *srcs)


def combine_block(window, step, starts_ref, index_ref, bufs, wins, acc):
    owners, capacity = bufs[0].shape[:2]
    experts = owners * len(bufs)
    lane = lax.broadcasted_iota(jnp.int32, (1, experts * window), 1)
    acc[...] = jnp.zeros(acc.shape, F32)

    def one_turn(turn, carry):
        seen = jnp.full((1, experts * window), -2, jnp.int32)
        for expert in range(experts):
            begin, high, at = window_at(starts_ref, expert, step, turn, window, capacity)
            slot = lane + (at - expert * window)
            fresh = (slot >= begin) & (slot < high)
            mine = (lane >= expert * window) & (lane < (expert + 1) * window)
            seen = jnp.where(mine & fresh, slot + expert * capacity, seen)
            wins[window * expert : window * (expert + 1), :] = (
                bufs[expert // owners][expert % owners, pl.ds(at, window), :]
            )
        hit = (index_ref[:, 0:1] == seen) | (index_ref[:, 1:2] == seen)
        acc[...] += dot(hit.astype(F32).astype(BF), wins[...])
        return carry

    lax.fori_loop(0, turns(starts_ref, step, range(experts), window), one_turn, 0)


def back_specs(parts, capacity):
    return [
        pl.BlockSpec((array.shape[0], capacity, array.shape[2]), lambda *_, at=at: (0, at, 0))
        for array, at in parts
    ]


def top_kernel(window, starts_ref, index_ref, hidden_ref, *refs):
    *bufs, out_ref, wins, acc = refs
    combine_block(window, pl.program_id(0), starts_ref, index_ref, bufs, wins, acc)
    out_ref[...] = (hidden_ref[...] + acc[...]).astype(BF)


def top(starts, index, hidden, parts, capacity):
    count, width = hidden.shape
    experts = starts.shape[0]
    window = window_rows(experts, capacity)
    row = lambda shape: pl.BlockSpec(shape, lambda step, *_: (step, 0))
    return pl.pallas_call(
        functools.partial(top_kernel, window),
        grid_spec=pltpu.PrefetchScalarGridSpec(
            num_scalar_prefetch=1,
            grid=(count // BLOCK,),
            in_specs=[row((BLOCK, 2)), row((BLOCK, width))] + back_specs(parts, capacity),
            out_specs=row((BLOCK, width)),
            scratch_shapes=[
                pltpu.VMEM((experts * window, width), BF), pltpu.VMEM((BLOCK, width), F32),
            ],
        ),
        out_shape=jax.ShapeDtypeStruct((count, width), BF),
        compiler_params=params(),
        cost_estimate=cost(6e9, 12e6),
        name="top",
    )(starts, index, hidden, *[array for array, _ in parts])


def gelu_parts(values):
    size = jnp.abs(values)
    near = 1.0 / (1.0 + (0.3275911 * 0.7071067811865476) * size)
    expo = jnp.exp(-0.5 * (values * values))
    poly = 0.5 * 1.061405429
    for term in (-1.453152027, 1.421413741, -0.284496736, 0.254829592):
        poly = poly * near + 0.5 * term
    tail = poly * near * expo
    share = jnp.where(values >= 0, 1.0 - tail, tail)
    return values * share, share + values * (0.3989422804014327 * expo)


def expert_kernel(
    experts, fcut, mine_ref, up_ref, down_ref, router_ref, back_ref, x_ref, dy_ref, *refs
):
    dx_ref, out_ref = refs[0], refs[-8]
    grad_ref, grouter_ref, acc_up, acc_down, acc_router, acc_out, acc_dx = refs[-7:]
    step = pl.program_id(0)
    hidden_units = up_ref.shape[1]
    times, capacity, width = x_ref.shape
    count = times * capacity

    @pl.when(step == 0)
    def _():
        acc_up[...] = jnp.zeros(acc_up.shape, F32)
        acc_down[...] = jnp.zeros(acc_down.shape, F32)
        acc_router[...] = jnp.zeros(acc_router.shape, F32)

    rows = x_ref[...].reshape(count, width)
    logits = dot(rows, router_ref[...])
    logits = logits[:, :LANES] + logits[:, LANES:]
    lane = lax.broadcasted_iota(jnp.int32, (count, LANES), 1)
    logits = jnp.where(lane < experts, logits, -1e30)
    expo = jnp.exp(logits - jnp.max(logits, axis=-1, keepdims=True))
    gates = expo / jnp.sum(expo, axis=-1, keepdims=True)
    own = (lane == mine_ref[0]).astype(F32)
    chosen = jnp.sum(gates * own, axis=-1, keepdims=True)
    pair = (chosen * dy_ref[...].reshape(count, width).astype(F32)).astype(BF)
    rows_t = rows.T
    pair_t = pair.T
    inner = jnp.zeros((count, LANES), F32)
    for low in range(0, hidden_units, fcut):
        cols = slice(low, low + fcut)
        pre = dot(rows, up_ref[:, cols])
        grad_act = dot_rt(pair, down_ref[cols, :])
        act, slope = gelu_parts(pre)
        both = act * grad_act
        for part in range(0, fcut, LANES):
            inner = inner + both[:, part : part + LANES]
        act = act.astype(BF)
        grad_pre = (grad_act * slope).astype(BF)
        acc_up[:, cols] += dot(rows_t, grad_pre)
        acc_down[:, cols] += dot(pair_t, act)
        if low == 0:
            acc_out[...] = dot(act, down_ref[cols, :])
            acc_dx[...] = dot_rt(grad_pre, up_ref[:, cols])
        else:
            acc_out[...] += dot(act, down_ref[cols, :])
            acc_dx[...] += dot_rt(grad_pre, up_ref[:, cols])
    grad_logits = jnp.sum(inner, axis=-1, keepdims=True) * (own - gates)
    head = grad_logits.astype(BF)
    rest = (grad_logits - head.astype(F32)).astype(BF)
    acc_router[...] += dot(rows_t, jnp.concatenate([head, rest], axis=1))
    shape = (times, capacity, width)
    out_ref[:, out_ref.shape[1] - capacity :, :] = (chosen * acc_out[...]).astype(BF).reshape(shape)
    dx_ref[:, :capacity, :] = (
        acc_dx[...] + dot(jnp.concatenate([head, head], axis=1), back_ref[...])
    ).astype(BF).reshape(shape)

    @pl.when(step == pl.num_programs(0) - 1)
    def _():
        shards, tall, _ = grad_ref.shape
        up_rows, down_rows = width // shards, hidden_units // shards
        piece = tall - up_rows
        for shard in range(shards):
            grad_ref[shard, :up_rows, :] = acc_up[up_rows * shard : up_rows * (shard + 1), :].astype(BF)
            turned = acc_down[:, down_rows * shard : down_rows * (shard + 1)].T.astype(BF)
            for part in range(down_rows // piece):
                grad_ref[shard, up_rows:, width * part : width * (part + 1)] = (
                    turned[piece * part : piece * (part + 1), :]
                )
        grouter_ref[...] = acc_router[:, :LANES] + acc_router[:, LANES:]


def expert_pass(mine, rows, grads, w_up, w_down, router, router_back, experts, capacity, shards, joined):
    (rows, rows_at), (grads, grads_at) = rows, grads
    sources, _, width = rows.shape
    units = w_up.shape[1]
    times = max(
        n for n in range(1, sources + 1) if sources % n == 0 and n * capacity <= max(TILE_ROWS, capacity)
    )
    tile = times * capacity
    block = lambda tall, at: pl.BlockSpec((times, tall, width), lambda step, *_: (step, at, 0))
    sent = [2 * capacity] if joined else [capacity, capacity]
    grad_shape = (shards, width // shards * 2, units)
    return pl.pallas_call(
        functools.partial(expert_kernel, experts, min(FCUT, units)),
        grid_spec=pltpu.PrefetchScalarGridSpec(
            num_scalar_prefetch=1,
            grid=(sources // times,),
            in_specs=[
                whole(w_up.shape), whole(w_down.shape), whole(router.shape), whole(router_back.shape),
                block(capacity, rows_at), block(capacity, grads_at),
            ],
            out_specs=[block(tall, 0) for tall in sent] + [whole(grad_shape), whole((width, LANES))],
            scratch_shapes=[
                pltpu.VMEM((width, units), F32),
                pltpu.VMEM((width, units), F32),
                pltpu.VMEM((width, 2 * LANES), F32),
                pltpu.VMEM((tile, width), F32),
                pltpu.VMEM((tile, width), F32),
            ],
        ),
        out_shape=[jax.ShapeDtypeStruct((sources, tall, width), BF) for tall in sent] + [
            jax.ShapeDtypeStruct(grad_shape, BF),
            jax.ShapeDtypeStruct((width, LANES), F32),
        ],
        compiler_params=params(),
        cost_estimate=cost(
            20 * sources * capacity * width * units, 30e6, 2 * sources * capacity * units
        ),
        name="expert_pass",
    )(mine, w_up, w_down, router, router_back, rows, grads)


def back_kernel(
    window, groups, starts_ref, here_ref, index_ref, hidden_ref, tok_ref, dy_ref, qkv_ref,
    probs_ref, mixed_ref, gain_one_ref, qkv_w_ref, proj_w_ref, gain_two_ref, *refs,
):
    *bufs, ghid_ref, dqkv_ref, sum_ref, ggain_one_ref, ggain_two_ref = refs[:-6]
    wins, acc, compact, padded, acc_qkv, acc_proj = refs[-6:]
    step = pl.program_id(0)
    width = tok_ref.shape[1]
    factor_qk = (width // HEADS) ** (-0.5)

    @pl.when(step == 0)
    def _():
        for ref in (acc_qkv, acc_proj, ggain_two_ref):
            ref[...] = jnp.zeros(ref.shape, F32)

    combine_block(window, step, starts_ref, index_ref, bufs, wins, acc)
    clear_gaps(padded)
    hat_two, scale_two = norm_parts(hidden_ref[...])
    grad_normed = acc[...]
    ggain_two_ref[...] += jnp.sum(grad_normed * hat_two, axis=0, keepdims=True)
    grad_hidden = dy_ref[...].astype(F32) + norm_back(
        grad_normed, hat_two, scale_two, gain_two_ref[...]
    )
    ghid_ref[...] = grad_hidden
    compact[...] = grad_hidden
    spread_rows(compact, padded)
    grad_attn = padded[...].astype(BF)
    acc_proj[...] += dot_lt(mixed_ref[...], grad_attn)
    grad_mixed = dot_rt(grad_attn, proj_w_ref[...]).astype(BF)
    low = low_half()
    for pair in range(BLOCK_PAIRS):
        rows = slice(PAIR_PAD * pair, PAIR_PAD * (pair + 1))
        for two in range(width // LANES):
            cols = slice(LANES * two, LANES * (two + 1))
            key_cols = slice(width + LANES * two, width + LANES * (two + 1))
            value_cols = slice(2 * width + LANES * two, 2 * width + LANES * (two + 1))
            at = (pair * (width // LANES) + two) * 2 * PAIR_PAD
            probs = probs_ref[at : at + 2 * PAIR_PAD, :]
            wide = probs.astype(F32)
            grad_out = two_heads(grad_mixed[rows, cols], low)
            grad_probs = dot_rt(grad_out, qkv_ref[rows, value_cols])
            meet = jnp.sum(wide * grad_probs, axis=-1, keepdims=True)
            grad_scores = (wide * (grad_probs - meet) * factor_qk).astype(BF)
            grad_query = one_row(dot(grad_scores, qkv_ref[rows, key_cols]), low)
            dqkv_ref[rows, cols] = grad_query.astype(BF)
            dqkv_ref[rows, key_cols] = dot_lt(
                grad_scores, two_heads(qkv_ref[rows, cols], low)
            ).astype(BF)
            dqkv_ref[rows, value_cols] = dot_lt(probs, grad_out).astype(BF)
    compact[...] = norm_parts(tok_ref[...].astype(F32))[0] * gain_one_ref[...]
    spread_rows(compact, padded)
    acc_qkv[...] += dot_lt(padded[...].astype(BF), dqkv_ref[...])

    @pl.when(step == pl.num_programs(0) - 1)
    def _():
        cores, sides, layers = groups
        tall = sum_ref.shape[2]
        for core in range(cores):
            for side in range(sides):
                for layer in range(layers):
                    low = ((core * sides + side) * layers + layer) * tall
                    part, at = low // width, low % width
                    if part < 3:
                        piece = acc_qkv[at : at + tall, width * part : width * (part + 1)]
                    else:
                        piece = acc_proj[at : at + tall, :]
                    spot = (side ^ here_ref[1]) * layers + (layer ^ here_ref[2])
                    sum_ref[core ^ here_ref[0], spot] = piece.astype(BF)
        ggain_one_ref[...] = jnp.sum(
            acc_qkv[...] * qkv_w_ref[...].astype(F32), axis=-1, keepdims=True
        )


def back(starts, here, groups, index, hidden, tokens, dy, qkv, probs, mixed, gain_one, w_qkv, w_proj, gain_two, parts, capacity):
    count, width = tokens.shape
    blocks = count // BLOCK
    experts = starts.shape[0]
    window = window_rows(experts, capacity)
    row = lambda shape: pl.BlockSpec(shape, lambda step, *_: (step, 0))
    cores, sides, layers = groups
    sum_shape = (cores, sides * layers, 4 * width // (cores * sides * layers), width)
    flops = 2 * blocks * BLOCK_PAD * width * (8 * width + 10 * PAIR_PAD)
    return pl.pallas_call(
        functools.partial(back_kernel, window, groups),
        grid_spec=pltpu.PrefetchScalarGridSpec(
            num_scalar_prefetch=2,
            grid=(blocks,),
            in_specs=[
                row((BLOCK, 2)), row((BLOCK, width)), row((BLOCK, width)), row((BLOCK, width)),
                row((BLOCK_PAD, 3 * width)), row((probs.shape[0] // blocks, PAIR_PAD)),
                row((BLOCK_PAD, width)),
                whole((1, width)), whole(w_qkv.shape), whole(w_proj.shape), whole((1, width)),
            ] + back_specs(parts, capacity),
            out_specs=[
                row((BLOCK, width)), row((BLOCK_PAD, 3 * width)), whole(sum_shape),
                whole((width, 1)), whole((1, width)),
            ],
            scratch_shapes=[
                pltpu.VMEM((experts * window, width), BF),
                pltpu.VMEM((BLOCK, width), F32),
                pltpu.VMEM((BLOCK, width), F32),
                pltpu.VMEM((BLOCK_PAD, width), F32),
                pltpu.VMEM(w_qkv.shape, F32),
                pltpu.VMEM(w_proj.shape, F32),
            ],
        ),
        out_shape=[
            jax.ShapeDtypeStruct((count, width), F32),
            jax.ShapeDtypeStruct(qkv.shape, BF),
            jax.ShapeDtypeStruct(sum_shape, BF),
            jax.ShapeDtypeStruct((width, 1), F32),
            jax.ShapeDtypeStruct((1, width), F32),
        ],
        compiler_params=params(),
        cost_estimate=cost(flops + 12e9, 40e6),
        name="back",
    )(
        starts, here, index, hidden, tokens, dy, qkv, probs, mixed, gain_one[None, :], w_qkv,
        w_proj, gain_two[None, :], *[array for array, _ in parts],
    )


def last_kernel(dqkv_ref, ghid_ref, tok_ref, gain_one_ref, qkv_w_ref, out_ref, compact, padded):
    padded[...] = dot_rt(dqkv_ref[...], qkv_w_ref[...])
    gather_rows(padded, compact)
    hat_one, scale_one = norm_parts(tok_ref[...].astype(F32))
    out_ref[...] = ghid_ref[...] + norm_back(compact[...], hat_one, scale_one, gain_one_ref[...])


def last(dqkv, ghid, tokens, gain_one, w_qkv):
    count, width = tokens.shape
    row = lambda shape: pl.BlockSpec(shape, lambda step: (step, 0))
    return pl.pallas_call(
        last_kernel,
        grid=(count // BLOCK,),
        in_specs=[
            row((BLOCK_PAD, 3 * width)), row((BLOCK, width)), row((BLOCK, width)),
            whole((1, width)), whole(w_qkv.shape),
        ],
        out_specs=row((BLOCK, width)),
        out_shape=jax.ShapeDtypeStruct((count, width), F32),
        scratch_shapes=[pltpu.VMEM((BLOCK, width), F32), pltpu.VMEM((BLOCK_PAD, width), F32)],
        compiler_params=params(),
        cost_estimate=cost(6 * dqkv.shape[0] * width * width, 20e6),
        name="last",
    )(dqkv, ghid, tokens, gain_one[None, :], w_qkv)


def lay_kernel(groups, here_ref, own_ref, other_ref, qkv_ref, proj_ref):
    cores, sides, layers = groups
    tall, width = own_ref.shape[1:]
    for core in range(cores):
        for side in range(sides):
            for layer in range(layers):
                low = ((core * sides + side) * layers + layer) * tall
                part, at = low // width, low % width
                spot = (side ^ here_ref[1]) * layers + (layer ^ here_ref[2])
                piece = jnp.where(core == here_ref[0], own_ref[spot].astype(F32), other_ref[spot].astype(F32))
                if part < 3:
                    qkv_ref[at : at + tall, width * part : width * (part + 1)] = piece
                else:
                    proj_ref[at : at + tall, :] = piece


def lay(groups, here, own, other):
    width = own.shape[2]
    return pl.pallas_call(
        functools.partial(lay_kernel, groups),
        grid_spec=pltpu.PrefetchScalarGridSpec(
            num_scalar_prefetch=1,
            grid=(1,),
            in_specs=[whole(own.shape)] * 2,
            out_specs=[whole((width, 3 * width)), whole((width, width))],
        ),
        out_shape=[
            jax.ShapeDtypeStruct((width, 3 * width), F32),
            jax.ShapeDtypeStruct((width, width), F32),
        ],
        compiler_params=params(),
        cost_estimate=cost(1e6, 8e6),
        name="lay",
    )(here, own, other)


def jump(value, axis, far):
    size = lax.axis_size(axis)
    return lax.ppermute(value, axis, [(at, at ^ far) for at in range(size)])


def add_up(parts):
    return sum(part.astype(F32) for part in parts).astype(BF)


def sum_over_all(sums, groups):
    cores, sides, layers = groups
    half = add_up([sums[0], jump(sums[1], "dp", 1)])
    tall, width = half.shape[1:]
    half = half.reshape(sides, layers, tall, width)
    flat = add_up([half[0]] + [jump(half[side], "expert", side) for side in range(1, sides)])
    spot = add_up([flat[0]] + [jump(flat[layer], "dp", cores * layer) for layer in range(1, layers)])
    flat = jnp.stack([spot] + [jump(spot, "dp", cores * layer) for layer in range(1, layers)])
    half = jnp.stack([flat] + [jump(flat, "expert", side) for side in range(1, sides)])
    half = half.reshape(sides * layers, tall, width)
    return half, jump(half, "dp", 1)


def sum_small(value):
    for axis in ("dp", "expert"):
        far = 1
        while far < lax.axis_size(axis):
            value = value + jump(value, axis, far)
            far = far * 2
    return value


def per_device(
    tokens, gain_one, w_qkv, w_proj, gain_two, w_router, w_in, w_eout, picks, keep, grad_out
):
    count, width = tokens.shape
    local = w_in.shape[0]
    owners = lax.axis_size("expert")
    shards = lax.axis_size("dp")
    experts = local * owners
    capacity = 8 * ((21 * count + 80 * experts - 1) // (80 * experts))
    me, row = lax.axis_index("expert"), lax.axis_index("dp")
    cores = 2
    groups = (cores, owners, shards // cores)
    here = jnp.stack([row % cores, me, row // cores]).astype(jnp.int32)
    ids = jnp.arange(experts, dtype=jnp.int32).reshape(owners, local).T.reshape(-1)

    def swap(sent):
        return lax.all_to_all(sent, "expert", split_axis=0, concat_axis=0, tiled=True)

    def after(value, *others):
        return lax.optimization_barrier((value, *others))[0]

    index_rows, starts = places(ids, picks, keep, capacity)
    (sent,) = dispatch([grad_out], starts, index_rows, owners, capacity, ((0, (0,)),))
    grads_first = swap(sent)
    hidden, rows, qkv, probs, mixed = attend(after(tokens, sent), gain_one, w_qkv, w_proj, gain_two)
    plan = ((0, (0,)),) + tuple((part, (0, 1)) for part in range(1, local))
    sent, *others = dispatch(
        [after(rows, grads_first), grad_out], starts, index_rows, owners, capacity, plan
    )
    got = swap(sent)
    came = [((got, 0), (grads_first, 0))]
    for sent in others:
        got = swap(after(sent, got))
        came.append(((got, 0), (got, 1)))
    index = index_rows.transpose(0, 2, 1).reshape(count, 2)
    head = w_router.astype(BF)
    rest = (w_router - head.astype(F32)).astype(BF)
    gap = ((0, 0), (0, LANES - experts))
    router = jnp.concatenate([jnp.pad(head, gap), jnp.pad(rest, gap)], axis=1)
    router_back = jnp.concatenate([jnp.pad(head, gap).T, jnp.pad(rest, gap).T], axis=0)
    outs, downs, sums, grad_router = [], [], [], 0
    for part in range(local):
        mine = (me * local + part).astype(jnp.int32)[None]
        joined = part < local - 1
        *sent, grad, router_part = expert_pass(
            mine, *came[part], w_in[part], w_eout[part], router, router_back, experts, capacity,
            shards, joined,
        )
        if part:
            sent = [after(sent[0], got), *sent[1:]]
        got = swap(sent[0])
        downs.append((got, 0))
        outs.append((got, 1))
        grad = grad.reshape(shards * grad.shape[1], grad.shape[2])
        sums.append(lax.psum_scatter(grad, "dp", scatter_dimension=0, tiled=True))
        grad_router = grad_router + router_part[:, :experts]
    outs[-1] = (swap(after(sent[1], got)), 0)
    grad_hidden, dqkv, pieces, grad_gain_one, grad_gain_two = back(
        starts, here, groups, index, hidden, tokens, grad_out, qkv, probs, mixed, gain_one,
        w_qkv, w_proj, gain_two, downs, capacity,
    )
    pieces = after(pieces, outs[-1][0])
    small = jnp.concatenate([grad_router.T, grad_gain_two, grad_gain_one.T], axis=0)
    small = sum_small(small)
    own, other = sum_over_all(pieces, groups)
    block_out = top(starts, index, hidden, outs, capacity)
    grad_tokens = last(dqkv, grad_hidden, tokens, gain_one, w_qkv)
    grad_qkv, grad_proj = lay(groups, here, own, other)
    tall = width // shards
    grad_in = jnp.stack([part[:tall] for part in sums]).astype(F32)
    grad_eout = jnp.stack(
        [part[tall:].reshape(tall, -1, width).transpose(1, 0, 2).reshape(-1, width) for part in sums]
    ).astype(F32)
    return (
        block_out,
        grad_tokens,
        small[experts + 1] / gain_one,
        grad_qkv,
        grad_proj,
        small[experts],
        small[:experts].T,
        grad_in,
        grad_eout,
    )


def solution(mesh):
    rows = P(("dp", "expert"), None)
    experts = P("expert", None, None)
    return jax.shard_map(
        per_device,
        mesh=mesh,
        in_specs=(rows, P(), P(), P(), P(), P(), experts, experts, rows, rows, rows),
        out_specs=(
            rows, rows, P(), P(), P(), P(), P(), P("expert", "dp", None), P("expert", "dp", None),
        ),
        check_vma=False,
    )
```

```python
import functools

import jax
import jax.numpy as jnp
from jax import lax
from jax.experimental import pallas as pl
from jax.experimental.pallas import tpu as pltpu
from jax.sharding import PartitionSpec as P

HEADS = 8
PATCHES = 49
LANES = 128
PAIR = 2 * PATCHES
PAIR_PAD = 112
BLOCK_PAIRS = 4
BLOCK = BLOCK_PAIRS * PAIR
BLOCK_PAD = BLOCK_PAIRS * PAIR_PAD
BF = jnp.bfloat16
F32 = jnp.float32
VMEM_BYTES = 56 * 1024 * 1024
FCUT = 1024


def params():
    return pltpu.CompilerParams(
        dimension_semantics=("arbitrary",), vmem_limit_bytes=VMEM_BYTES
    )


def cost(flops, moved, special=0):
    return pl.CostEstimate(
        flops=int(flops), bytes_accessed=int(moved), transcendentals=int(special)
    )


def whole(shape):
    return pl.BlockSpec(shape, lambda *_: (0,) * len(shape))


def dot(left, right):
    return jnp.dot(left, right, preferred_element_type=F32)


def dot_rt(left, right):
    return lax.dot_general(left, right, (((1,), (1,)), ((), ())), preferred_element_type=F32)


def dot_lt(left, right):
    return lax.dot_general(left, right, (((0,), (0,)), ((), ())), preferred_element_type=F32)


def norm_parts(values):
    mean = jnp.mean(values, axis=-1, keepdims=True)
    cent = values - mean
    factor = lax.rsqrt(jnp.mean(cent * cent, axis=-1, keepdims=True) + 1e-06)
    return cent * factor, factor


def norm_back(grad_normed, normed_hat, factor, gain):
    grad_hat = grad_normed * gain
    inner = grad_hat - jnp.mean(grad_hat, axis=-1, keepdims=True)
    inner = inner - normed_hat * jnp.mean(grad_hat * normed_hat, axis=-1, keepdims=True)
    return factor * inner


def spread_rows(compact, padded):
    for pair in range(BLOCK_PAIRS):
        padded[PAIR_PAD * pair : PAIR_PAD * pair + PAIR] = compact[PAIR * pair : PAIR * pair + PAIR]


def gather_rows(padded, compact):
    for pair in range(BLOCK_PAIRS):
        compact[PAIR * pair : PAIR * pair + PAIR] = padded[PAIR_PAD * pair : PAIR_PAD * pair + PAIR]


def clear_gaps(padded):
    for pair in range(BLOCK_PAIRS):
        low = PAIR_PAD * pair + PAIR
        padded[low : low + PAIR_PAD - PAIR] = jnp.zeros((PAIR_PAD - PAIR, padded.shape[1]), F32)


def image_of(position):
    return (position >= PATCHES).astype(jnp.int32) + (position >= PAIR).astype(jnp.int32)


def same_image():
    rows = lax.broadcasted_iota(jnp.int32, (2 * PAIR_PAD, PAIR_PAD), 0)
    rows = jnp.where(rows >= PAIR_PAD, rows - PAIR_PAD, rows)
    cols = lax.broadcasted_iota(jnp.int32, (2 * PAIR_PAD, PAIR_PAD), 1)
    return image_of(rows) == image_of(cols)


def low_half():
    return lax.broadcasted_iota(jnp.int32, (PAIR_PAD, LANES), 1) < LANES // 2


def two_heads(values, low):
    zero = jnp.zeros_like(values)
    return jnp.concatenate([jnp.where(low, values, zero), jnp.where(low, zero, values)], axis=0)


def one_row(values, low):
    return jnp.where(low, values[:PAIR_PAD], values[PAIR_PAD:])


def attend_kernel(
    tok_ref, gain_one_ref, qkv_w_ref, proj_w_ref, gain_two_ref,
    hidden_ref, rows_ref, qkv_ref, probs_ref, mixed_ref,
    compact, padded,
):
    width = tok_ref.shape[1]
    factor_qk = (width // HEADS) ** (-0.5)
    clear_gaps(padded)
    inputs = tok_ref[...].astype(F32)
    compact[...] = norm_parts(inputs)[0] * gain_one_ref[...]
    spread_rows(compact, padded)
    qkv_ref[...] = dot(padded[...].astype(BF), qkv_w_ref[...]).astype(BF)
    valid = same_image()
    low = low_half()
    for pair in range(BLOCK_PAIRS):
        rows = slice(PAIR_PAD * pair, PAIR_PAD * (pair + 1))
        for two in range(width // LANES):
            cols = slice(LANES * two, LANES * (two + 1))
            query = qkv_ref[rows, cols]
            keys = qkv_ref[rows, width + LANES * two : width + LANES * (two + 1)]
            values = qkv_ref[rows, 2 * width + LANES * two : 2 * width + LANES * (two + 1)]
            scores = jnp.where(valid, dot_rt(two_heads(query, low), keys), -1e30)
            highest = jnp.max(scores, axis=-1, keepdims=True)
            expo = jnp.exp((scores - highest) * factor_qk)
            probs = (expo / jnp.sum(expo, axis=-1, keepdims=True)).astype(BF)
            step = (pair * (width // LANES) + two) * 2 * PAIR_PAD
            probs_ref[step : step + 2 * PAIR_PAD, :] = probs
            mixed_ref[rows, cols] = one_row(dot(probs, values), low).astype(BF)
    padded[...] = dot(mixed_ref[...], proj_w_ref[...])
    gather_rows(padded, compact)
    hidden = inputs + compact[...]
    hidden_ref[...] = hidden
    rows_ref[...] = (norm_parts(hidden)[0] * gain_two_ref[...]).astype(BF)


def attend(tokens, gain_one, w_qkv, w_proj, gain_two):
    count, width = tokens.shape
    blocks = count // BLOCK
    prob_rows = BLOCK_PAIRS * (width // LANES) * 2 * PAIR_PAD
    row = lambda shape: pl.BlockSpec(shape, lambda step: (step, 0))
    flops = 2 * blocks * BLOCK_PAD * width * (4 * width + 4 * PAIR_PAD)
    return pl.pallas_call(
        attend_kernel,
        grid=(blocks,),
        in_specs=[
            row((BLOCK, width)), whole((1, width)), whole(w_qkv.shape), whole(w_proj.shape),
            whole((1, width)),
        ],
        out_specs=[
            row((BLOCK, width)), row((BLOCK, width)), row((BLOCK_PAD, 3 * width)),
            row((prob_rows, PAIR_PAD)), row((BLOCK_PAD, width)),
        ],
        out_shape=[
            jax.ShapeDtypeStruct((count, width), F32),
            jax.ShapeDtypeStruct((count, width), BF),
            jax.ShapeDtypeStruct((blocks * BLOCK_PAD, 3 * width), BF),
            jax.ShapeDtypeStruct((blocks * prob_rows, PAIR_PAD), BF),
            jax.ShapeDtypeStruct((blocks * BLOCK_PAD, width), BF),
        ],
        scratch_shapes=[pltpu.VMEM((BLOCK, width), F32), pltpu.VMEM((BLOCK_PAD, width), F32)],
        compiler_params=params(),
        cost_estimate=cost(flops, 30e6, blocks * prob_rows * LANES),
        name="attend",
    )(tokens, gain_one[None, :], w_qkv, w_proj, gain_two[None, :])


def place_kernel(capacity, ids_ref, picks_ref, index_ref, starts_ref, carry):
    step = pl.program_id(0)

    @pl.when(step == 0)
    def _():
        carry[...] = jnp.zeros(carry.shape, F32)
        starts_ref[...] = jnp.zeros(starts_ref.shape, jnp.int32)

    experts, block = ids_ref.shape[0], picks_ref.shape[2]
    ids = ids_ref[...]
    names = [picks_ref[0, c : c + 1, :] == ids for c in (0, 1)]
    named = (names[0] | names[1]).astype(F32)
    earlier = lax.broadcasted_iota(jnp.int32, (block, block), 0) < lax.broadcasted_iota(
        jnp.int32, (block, block), 1
    )
    before = dot(named.astype(BF), earlier.astype(F32).astype(BF)) + carry[:, 0:1]
    spot = before + (lax.broadcasted_iota(jnp.int32, (experts, block), 0) * capacity).astype(F32)
    for c in (0, 1):
        found = jnp.sum(jnp.where(names[c], spot, 0.0), axis=0, keepdims=True).astype(jnp.int32)
        index_ref[0, c : c + 1, :] = jnp.where(picks_ref[0, 2 + c : 3 + c, :] > 0, found, -1)
    after = carry[...] + jnp.sum(named, axis=1, keepdims=True)
    carry[...] = after
    lane = lax.broadcasted_iota(jnp.int32, (experts, LANES), 1)
    starts_ref[...] = jnp.where(lane == step + 1, after.astype(jnp.int32), starts_ref[...])


def places(ids, picks, keep, capacity):
    count = picks.shape[0]
    blocks = count // BLOCK
    experts = ids.shape[0]
    turned = jnp.concatenate([picks, keep], axis=1).reshape(blocks, BLOCK, 4).transpose(0, 2, 1)
    return pl.pallas_call(
        functools.partial(place_kernel, capacity),
        grid=(blocks,),
        in_specs=[whole((experts, 1)), pl.BlockSpec((1, 4, BLOCK), lambda step: (step, 0, 0))],
        out_specs=[
            pl.BlockSpec((1, 2, BLOCK), lambda step: (step, 0, 0)), whole((experts, LANES)),
        ],
        out_shape=[
            jax.ShapeDtypeStruct((blocks, 2, BLOCK), jnp.int32),
            jax.ShapeDtypeStruct((experts, LANES), jnp.int32),
        ],
        scratch_shapes=[pltpu.VMEM((experts, LANES), F32)],
        compiler_params=params(),
        cost_estimate=cost(1e8, 1e5),
        name="places",
    )(ids[:, None], turned)


def window_rows(experts, capacity):
    return min(capacity, 16 * -(-2 * BLOCK * 8 // (5 * 16 * experts)))


def window_at(starts_ref, expert, step, turn, window, capacity):
    low = starts_ref[expert, step]
    begin = (low // 16) * 16 + turn * window
    at = pl.multiple_of(jnp.minimum(begin, capacity - window), 16)
    return begin, starts_ref[expert, step + 1], at


def turns(starts_ref, step, experts, window):
    most = 0
    for expert in experts:
        low = (starts_ref[expert, step] // 16) * 16
        most = jnp.maximum(most, (starts_ref[expert, step + 1] - low + window - 1) // window)
    return most


def dispatch_kernel(window, capacity, plan, sources, starts_ref, index_ref, *refs):
    src_refs, outs, (spots, got) = refs[:sources], refs[sources:-2], refs[-2:]
    owners = outs[0].shape[0]
    step = pl.program_id(0)
    named = [owners * part + owner for part, _ in plan for owner in range(owners)]

    @pl.when(step == 0)
    def _():
        for out in outs:
            out[...] = jnp.zeros(out.shape, out.dtype)

    place = lax.broadcasted_iota(jnp.int32, (window, index_ref.shape[2]), 0)
    first, second = index_ref[0, 0:1, :], index_ref[0, 1:2, :]

    def one_turn(turn, carry):
        for (part, used), out in zip(plan, outs):
            spans = []
            for owner in range(owners):
                expert = part * owners + owner
                begin, _, at = window_at(starts_ref, expert, step, turn, window, capacity)
                shift = expert * capacity
                near = jnp.where(first >= shift + begin, first - (shift + at), -1)
                far = jnp.where(second >= shift + begin, second - (shift + at), -1)
                hit = jnp.where((near >= 0) & (near < window), near, far)
                spots[window * owner : window * (owner + 1), :] = (
                    (place == hit).astype(F32).astype(BF)
                )
                spans.append(at)
            for order, which in enumerate(used):
                got[...] = dot(spots[...], src_refs[which][...])
                for owner, at in enumerate(spans):
                    rows = pl.ds(pl.multiple_of(at + order * capacity, 16), window)
                    held = out[owner, rows, :].astype(F32)
                    out[owner, rows, :] = (
                        held + got[window * owner : window * (owner + 1), :]
                    ).astype(BF)
        return carry

    lax.fori_loop(0, turns(starts_ref, step, named, window), one_turn, 0)


def dispatch(srcs, starts, index_rows, owners, capacity, plan):
    count, width = srcs[0].shape
    window = window_rows(starts.shape[0], capacity)
    shapes = [(owners, len(used) * capacity, width) for _, used in plan]
    return pl.pallas_call(
        functools.partial(dispatch_kernel, window, capacity, plan, len(srcs)),
        grid_spec=pltpu.PrefetchScalarGridSpec(
            num_scalar_prefetch=1,
            grid=(count // BLOCK,),
            in_specs=[pl.BlockSpec((1, 2, BLOCK), lambda step, *_: (step, 0, 0))]
            + [pl.BlockSpec((BLOCK, width), lambda step, *_: (step, 0))] * len(srcs),
            out_specs=[whole(shape) for shape in shapes],
            scratch_shapes=[
                pltpu.VMEM((owners * window, BLOCK), BF),
                pltpu.VMEM((owners * window, width), F32),
            ],
        ),
        out_shape=[jax.ShapeDtypeStruct(shape, BF) for shape in shapes],
        compiler_params=params(),
        cost_estimate=cost(6e9, 8e6),
        name="dispatch",
    )(starts, index_rows, *srcs)


def combine_block(window, step, me, starts_ref, index_ref, bufs, own_bufs, wins, acc):
    owners, capacity = bufs[0].shape[:2]
    experts = owners * len(bufs)
    lane = lax.broadcasted_iota(jnp.int32, (1, experts * window), 1)
    acc[...] = jnp.zeros(acc.shape, F32)

    def one_turn(turn, carry):
        seen = jnp.full((1, experts * window), -2, jnp.int32)
        for expert in range(experts):
            part, owner = expert // owners, expert % owners
            begin, high, at = window_at(starts_ref, expert, step, turn, window, capacity)
            slot = lane + (at - expert * window)
            fresh = (slot >= begin) & (slot < high)
            mine = (lane >= expert * window) & (lane < (expert + 1) * window)
            seen = jnp.where(mine & fresh, slot + expert * capacity, seen)
            wins[window * expert : window * (expert + 1), :] = jnp.where(
                me == owner, own_bufs[part][0, pl.ds(at, window), :],
                bufs[part][owner, pl.ds(at, window), :],
            )
        hit = (index_ref[:, 0:1] == seen) | (index_ref[:, 1:2] == seen)
        acc[...] += dot(hit.astype(F32).astype(BF), wins[...])
        return carry

    lax.fori_loop(0, turns(starts_ref, step, range(experts), window), one_turn, 0)


def back_specs(parts, own, capacity):
    width = own[0].shape[2]
    return [
        pl.BlockSpec((array.shape[0], capacity, width), lambda *_, at=at: (0, at, 0))
        for array, at in parts
    ] + [whole((1, capacity, width))] * len(own)


def top_kernel(window, local, starts_ref, here_ref, index_ref, hidden_ref, *refs):
    bufs, own_bufs, (out_ref, wins, acc) = refs[:local], refs[local : 2 * local], refs[2 * local :]
    combine_block(
        window, pl.program_id(0), here_ref[1], starts_ref, index_ref, bufs, own_bufs, wins, acc
    )
    out_ref[...] = (hidden_ref[...] + acc[...]).astype(BF)


def top(starts, here, index, hidden, parts, own, capacity):
    count, width = hidden.shape
    experts = starts.shape[0]
    window = window_rows(experts, capacity)
    row = lambda shape: pl.BlockSpec(shape, lambda step, *_: (step, 0))
    return pl.pallas_call(
        functools.partial(top_kernel, window, len(parts)),
        grid_spec=pltpu.PrefetchScalarGridSpec(
            num_scalar_prefetch=2,
            grid=(count // BLOCK,),
            in_specs=[row((BLOCK, 2)), row((BLOCK, width))] + back_specs(parts, own, capacity),
            out_specs=row((BLOCK, width)),
            scratch_shapes=[
                pltpu.VMEM((experts * window, width), BF), pltpu.VMEM((BLOCK, width), F32),
            ],
        ),
        out_shape=jax.ShapeDtypeStruct((count, width), BF),
        compiler_params=params(),
        cost_estimate=cost(6e9, 12e6),
        name="top",
    )(starts, here, index, hidden, *[array for array, _ in parts], *own)


def gelu_parts(values):
    size = jnp.abs(values)
    near = 1.0 / (1.0 + (0.3275911 * 0.7071067811865476) * size)
    expo = jnp.exp(-0.5 * (values * values))
    poly = 0.5 * 1.061405429
    for term in (-1.453152027, 1.421413741, -0.284496736, 0.254829592):
        poly = poly * near + 0.5 * term
    tail = poly * near * expo
    share = jnp.where(values >= 0, 1.0 - tail, tail)
    return values * share, share + values * (0.3989422804014327 * expo)


def expert_kernel(
    experts, fcut, begun, ends, mine_ref, up_ref, down_ref, router_ref, back_ref, x_ref, dy_ref, *refs
):
    given, refs = refs[: 3 * begun], refs[3 * begun :]
    acc_up, acc_down, acc_router, acc_out, acc_dx = refs[-5:]
    grouter_ref = refs[-6]
    grad_refs = refs[-7:-6] if ends else refs[-8:-6]
    dx_ref, out_ref = refs[-9:-7] if ends else refs[-10:-8]
    step = pl.program_id(0)
    hidden_units = up_ref.shape[1]
    _, capacity, width = x_ref.shape
    count = capacity

    @pl.when(step == 0)
    def _():
        if begun:
            acc_up[...] = given[0][...].astype(F32)
            acc_down[...] = given[1][...].astype(F32)
            acc_router[:, :LANES] = given[2][...]
            acc_router[:, LANES:] = jnp.zeros((width, LANES), F32)
        else:
            acc_up[...] = jnp.zeros(acc_up.shape, F32)
            acc_down[...] = jnp.zeros(acc_down.shape, F32)
            acc_router[...] = jnp.zeros(acc_router.shape, F32)

    rows = x_ref[...].reshape(count, width)
    logits = dot(rows, router_ref[...])
    logits = logits[:, :LANES] + logits[:, LANES:]
    lane = lax.broadcasted_iota(jnp.int32, (count, LANES), 1)
    logits = jnp.where(lane < experts, logits, -1e30)
    expo = jnp.exp(logits - jnp.max(logits, axis=-1, keepdims=True))
    gates = expo / jnp.sum(expo, axis=-1, keepdims=True)
    own = (lane == mine_ref[0]).astype(F32)
    chosen = jnp.sum(gates * own, axis=-1, keepdims=True)
    pair = (chosen * dy_ref[...].reshape(count, width).astype(F32)).astype(BF)
    rows_t = rows.T
    pair_t = pair.T
    inner = jnp.zeros((count, LANES), F32)
    for low in range(0, hidden_units, fcut):
        cols = slice(low, low + fcut)
        pre = dot(rows, up_ref[:, cols])
        grad_act = dot_rt(pair, down_ref[cols, :])
        act, slope = gelu_parts(pre)
        both = act * grad_act
        for part in range(0, fcut, LANES):
            inner = inner + both[:, part : part + LANES]
        act = act.astype(BF)
        grad_pre = (grad_act * slope).astype(BF)
        acc_up[:, cols] += dot(rows_t, grad_pre)
        acc_down[:, cols] += dot(pair_t, act)
        if low == 0:
            acc_out[...] = dot(act, down_ref[cols, :])
            acc_dx[...] = dot_rt(grad_pre, up_ref[:, cols])
        else:
            acc_out[...] += dot(act, down_ref[cols, :])
            acc_dx[...] += dot_rt(grad_pre, up_ref[:, cols])
    grad_logits = jnp.sum(inner, axis=-1, keepdims=True) * (own - gates)
    head = grad_logits.astype(BF)
    rest = (grad_logits - head.astype(F32)).astype(BF)
    acc_router[...] += dot(rows_t, jnp.concatenate([head, rest], axis=1))
    out_ref[0] = (chosen * acc_out[...]).astype(BF)
    dx_ref[0] = (
        acc_dx[...] + dot(jnp.concatenate([head, head], axis=1), back_ref[...])
    ).astype(BF)

    @pl.when(step == pl.num_programs(0) - 1)
    def _():
        grouter_ref[...] = acc_router[:, :LANES] + acc_router[:, LANES:]
        if not ends:
            grad_refs[0][...] = acc_up[...].astype(BF)
            grad_refs[1][...] = acc_down[...].astype(BF)
            return
        grad_ref = grad_refs[0]
        shards, tall, _ = grad_ref.shape
        up_rows, down_rows = width // shards, hidden_units // shards
        piece = tall - up_rows
        for shard in range(shards):
            grad_ref[shard, :up_rows, :] = acc_up[up_rows * shard : up_rows * (shard + 1), :].astype(BF)
            turned = acc_down[:, down_rows * shard : down_rows * (shard + 1)].T.astype(BF)
            for part in range(down_rows // piece):
                grad_ref[shard, up_rows:, width * part : width * (part + 1)] = (
                    turned[piece * part : piece * (part + 1), :]
                )


def expert_pass(part, mine, rows, grads, w_up, w_down, router, router_back, experts, capacity, shards, own, given, outs):
    (rows, rows_at), (grads, grads_at) = rows, grads
    sources, _, width = rows.shape
    local, _, units = w_up.shape
    ends = given is not None
    source = lambda step, mine_ref: (mine_ref[1] + (0 if own else 1) + step) % sources
    block = lambda at: pl.BlockSpec(
        (1, capacity, width), lambda step, mine_ref: (source(step, mine_ref), at, 0)
    )
    only = whole((1, capacity, width))
    weight = lambda shape: pl.BlockSpec((None,) + shape[1:], lambda *_: (part, 0, 0))
    grad_shape = (shards, width // shards * 2, units)
    given = list(given or ())
    taken = [] if outs is None else [outs]
    if own:
        sent = [jax.ShapeDtypeStruct((1, capacity, width), BF)] * 2
        sent_specs = [only, only]
    else:
        sent = [
            jax.ShapeDtypeStruct((sources, capacity, width), BF),
            jax.ShapeDtypeStruct((sources, local * capacity, width), BF),
        ]
        sent_specs = [block(0), block(part)]
    if ends:
        sums = [jax.ShapeDtypeStruct(grad_shape, BF)]
    else:
        sums = [jax.ShapeDtypeStruct((width, units), BF)] * 2
    sums.append(jax.ShapeDtypeStruct((width, LANES), F32))
    steps = 1 if own else sources - 1

    def body(*refs):
        refs = list(refs)
        if taken:
            del refs[7 + len(given)]
        expert_kernel(experts, min(FCUT, units), bool(given), ends, *refs)

    return pl.pallas_call(
        body,
        grid_spec=pltpu.PrefetchScalarGridSpec(
            num_scalar_prefetch=1,
            grid=(steps,),
            in_specs=[
                weight(w_up.shape), weight(w_down.shape), whole(router.shape),
                whole(router_back.shape), block(rows_at), block(grads_at),
            ] + [whole(array.shape) for array in given] + [pl.BlockSpec(memory_space=pl.ANY)] * len(taken),
            out_specs=sent_specs + [whole(array.shape) for array in sums],
            scratch_shapes=[
                pltpu.VMEM((width, units), F32),
                pltpu.VMEM((width, units), F32),
                pltpu.VMEM((width, 2 * LANES), F32),
                pltpu.VMEM((capacity, width), F32),
                pltpu.VMEM((capacity, width), F32),
            ],
        ),
        out_shape=sent + sums,
        input_output_aliases={7 + len(given): 1} if taken else {},
        compiler_params=params(),
        cost_estimate=cost(
            20 * steps * capacity * width * units, 30e6, 2 * steps * capacity * units
        ),
        name="expert_own" if own else "expert_others",
    )(mine, w_up, w_down, router, router_back, rows, grads, *given, *taken)


def back_kernel(
    window, groups, local, starts_ref, here_ref, index_ref, hidden_ref, tok_ref, dy_ref, qkv_ref,
    probs_ref, mixed_ref, gain_one_ref, qkv_w_ref, proj_w_ref, gain_two_ref, *refs,
):
    bufs, own_bufs = refs[:local], refs[local : 2 * local]
    router_refs = refs[2 * local : 3 * local]
    ghid_ref, dqkv_ref, own_ref, sent_ref = refs[3 * local : -7]
    wins, acc, compact, padded, acc_qkv, acc_proj, acc_gain = refs[-7:]
    experts = starts_ref.shape[0]
    step = pl.program_id(0)
    width = tok_ref.shape[1]
    factor_qk = (width // HEADS) ** (-0.5)

    @pl.when(step == 0)
    def _():
        for ref in (acc_qkv, acc_proj, acc_gain):
            ref[...] = jnp.zeros(ref.shape, F32)

    combine_block(window, step, here_ref[1], starts_ref, index_ref, bufs, own_bufs, wins, acc)
    clear_gaps(padded)
    hat_two, scale_two = norm_parts(hidden_ref[...])
    grad_normed = acc[...]
    acc_gain[...] += jnp.sum(grad_normed * hat_two, axis=0, keepdims=True)
    grad_hidden = dy_ref[...].astype(F32) + norm_back(
        grad_normed, hat_two, scale_two, gain_two_ref[...]
    )
    ghid_ref[...] = grad_hidden
    compact[...] = grad_hidden
    spread_rows(compact, padded)
    grad_attn = padded[...].astype(BF)
    acc_proj[...] += dot_lt(mixed_ref[...], grad_attn)
    grad_mixed = dot_rt(grad_attn, proj_w_ref[...]).astype(BF)
    low = low_half()
    for pair in range(BLOCK_PAIRS):
        rows = slice(PAIR_PAD * pair, PAIR_PAD * (pair + 1))
        for two in range(width // LANES):
            cols = slice(LANES * two, LANES * (two + 1))
            key_cols = slice(width + LANES * two, width + LANES * (two + 1))
            value_cols = slice(2 * width + LANES * two, 2 * width + LANES * (two + 1))
            at = (pair * (width // LANES) + two) * 2 * PAIR_PAD
            probs = probs_ref[at : at + 2 * PAIR_PAD, :]
            wide = probs.astype(F32)
            grad_out = two_heads(grad_mixed[rows, cols], low)
            grad_probs = dot_rt(grad_out, qkv_ref[rows, value_cols])
            meet = jnp.sum(wide * grad_probs, axis=-1, keepdims=True)
            grad_scores = (wide * (grad_probs - meet) * factor_qk).astype(BF)
            grad_query = one_row(dot(grad_scores, qkv_ref[rows, key_cols]), low)
            dqkv_ref[rows, cols] = grad_query.astype(BF)
            dqkv_ref[rows, key_cols] = dot_lt(
                grad_scores, two_heads(qkv_ref[rows, cols], low)
            ).astype(BF)
            dqkv_ref[rows, value_cols] = dot_lt(probs, grad_out).astype(BF)
    compact[...] = norm_parts(tok_ref[...].astype(F32))[0] * gain_one_ref[...]
    spread_rows(compact, padded)
    acc_qkv[...] += dot_lt(padded[...].astype(BF), dqkv_ref[...])

    @pl.when(step == pl.num_programs(0) - 1)
    def _():
        cores, sides, layers = groups
        half = acc_qkv.shape[0] * 4 // cores
        tall = half // (sides * layers)

        def piece(row):
            part, at = row // width, row % width
            if part < 3:
                return acc_qkv[at : at + tall, width * part : width * (part + 1)]
            return acc_proj[at : at + tall, :]

        for side in range(sides):
            for layer in range(layers):
                low = (side * layers + layer) * tall
                spot = (side ^ here_ref[1]) * layers + (layer ^ here_ref[2])
                to = pl.ds(pl.multiple_of(spot * tall, tall), tall)
                even, odd = piece(low), piece(half + low)
                own_ref[to, :] = jnp.where(here_ref[0] == 0, even, odd).astype(BF)
                sent_ref[to, :] = jnp.where(here_ref[0] == 0, odd, even).astype(BF)
        gain_one_sum = jnp.sum(acc_qkv[...] * qkv_w_ref[...].astype(F32), axis=-1, keepdims=True)
        lane = lax.broadcasted_iota(jnp.int32, (width, LANES), 1)
        router = sum(ref[...] for ref in router_refs)
        small = jnp.where(lane == experts, gain_one_sum, router).T[: own_ref.shape[0] - half, :]
        row = lax.broadcasted_iota(jnp.int32, small.shape, 0)
        small = jnp.where(row == experts + 1, acc_gain[...], small).astype(BF)
        own_ref[half:, :] = small
        sent_ref[half:, :] = small


def small_rows(experts):
    return 16 * -(-(experts + 2) // 16)


def back(starts, here, groups, index, hidden, tokens, dy, qkv, probs, mixed, gain_one, w_qkv, w_proj, gain_two, parts, own, routers, capacity):
    count, width = tokens.shape
    blocks = count // BLOCK
    experts = starts.shape[0]
    window = window_rows(experts, capacity)
    row = lambda shape: pl.BlockSpec(shape, lambda step, *_: (step, 0))
    cores, sides, layers = groups
    assert cores == 2
    sum_shape = (2 * width + small_rows(experts), width)
    flops = 2 * blocks * BLOCK_PAD * width * (8 * width + 10 * PAIR_PAD)
    return pl.pallas_call(
        functools.partial(back_kernel, window, groups, len(parts)),
        grid_spec=pltpu.PrefetchScalarGridSpec(
            num_scalar_prefetch=2,
            grid=(blocks,),
            in_specs=[
                row((BLOCK, 2)), row((BLOCK, width)), row((BLOCK, width)), row((BLOCK, width)),
                row((BLOCK_PAD, 3 * width)), row((probs.shape[0] // blocks, PAIR_PAD)),
                row((BLOCK_PAD, width)),
                whole((1, width)), whole(w_qkv.shape), whole(w_proj.shape), whole((1, width)),
            ] + back_specs(parts, own, capacity) + [whole((width, LANES))] * len(routers),
            out_specs=[
                row((BLOCK, width)), row((BLOCK_PAD, 3 * width)), whole(sum_shape), whole(sum_shape),
            ],
            scratch_shapes=[
                pltpu.VMEM((experts * window, width), BF),
                pltpu.VMEM((BLOCK, width), F32),
                pltpu.VMEM((BLOCK, width), F32),
                pltpu.VMEM((BLOCK_PAD, width), F32),
                pltpu.VMEM(w_qkv.shape, F32),
                pltpu.VMEM(w_proj.shape, F32),
                pltpu.VMEM((1, width), F32),
            ],
        ),
        out_shape=[
            jax.ShapeDtypeStruct((count, width), F32),
            jax.ShapeDtypeStruct(qkv.shape, BF),
            jax.ShapeDtypeStruct(sum_shape, BF),
            jax.ShapeDtypeStruct(sum_shape, BF),
        ],
        compiler_params=params(),
        cost_estimate=cost(flops + 12e9, 40e6),
        name="back",
    )(
        starts, here, index, hidden, tokens, dy, qkv, probs, mixed, gain_one[None, :], w_qkv,
        w_proj, gain_two[None, :], *[array for array, _ in parts], *own, *routers,
    )


def last_kernel(dqkv_ref, ghid_ref, tok_ref, gain_one_ref, qkv_w_ref, *refs):
    out_ref, compact, padded = refs[-3:]
    padded[...] = dot_rt(dqkv_ref[...], qkv_w_ref[...])
    gather_rows(padded, compact)
    hat_one, scale_one = norm_parts(tok_ref[...].astype(F32))
    out_ref[...] = ghid_ref[...] + norm_back(compact[...], hat_one, scale_one, gain_one_ref[...])


def last(low, high, so_far, dqkv, ghid, tokens, gain_one, w_qkv):
    count, width = tokens.shape
    row = lambda shape: pl.BlockSpec(shape, lambda step: (step + low, 0))
    taken = [] if so_far is None else [so_far]
    return pl.pallas_call(
        last_kernel,
        grid=(high - low,),
        in_specs=[
            row((BLOCK_PAD, 3 * width)), row((BLOCK, width)), row((BLOCK, width)),
            whole((1, width)), whole(w_qkv.shape),
        ] + [pl.BlockSpec(memory_space=pl.ANY)] * len(taken),
        out_specs=row((BLOCK, width)),
        out_shape=jax.ShapeDtypeStruct((count, width), F32),
        scratch_shapes=[pltpu.VMEM((BLOCK, width), F32), pltpu.VMEM((BLOCK_PAD, width), F32)],
        input_output_aliases={5: 0} if taken else {},
        compiler_params=params(),
        cost_estimate=cost(6 * BLOCK_PAD * (high - low) * width * width, 20e6),
        name="last",
    )(dqkv, ghid, tokens, gain_one[None, :], w_qkv, *taken)


def lay_kernel(groups, here_ref, own_ref, other_ref, qkv_ref, proj_ref):
    cores, sides, layers = groups
    tall, width = own_ref.shape[1:]
    for core in range(cores):
        for side in range(sides):
            for layer in range(layers):
                low = ((core * sides + side) * layers + layer) * tall
                part, at = low // width, low % width
                spot = (side ^ here_ref[1]) * layers + (layer ^ here_ref[2])
                piece = jnp.where(core == here_ref[0], own_ref[spot].astype(F32), other_ref[spot].astype(F32))
                if part < 3:
                    qkv_ref[at : at + tall, width * part : width * (part + 1)] = piece
                else:
                    proj_ref[at : at + tall, :] = piece


def lay(groups, here, own, other):
    width = own.shape[2]
    return pl.pallas_call(
        functools.partial(lay_kernel, groups),
        grid_spec=pltpu.PrefetchScalarGridSpec(
            num_scalar_prefetch=1,
            grid=(1,),
            in_specs=[whole(own.shape)] * 2,
            out_specs=[whole((width, 3 * width)), whole((width, width))],
        ),
        out_shape=[
            jax.ShapeDtypeStruct((width, 3 * width), F32),
            jax.ShapeDtypeStruct((width, width), F32),
        ],
        compiler_params=params(),
        cost_estimate=cost(1e6, 8e6),
        name="lay",
    )(here, own, other)


def jump(value, axis, far):
    size = lax.axis_size(axis)
    return lax.ppermute(value, axis, [(at, at ^ far) for at in range(size)])


def merge_kernel(cuts, extra, count, *refs):
    parts, outs = refs[:count], refs[count:]
    tall = (parts[0].shape[0] - extra) // cuts

    def total(rows):
        value = parts[0][rows, :].astype(F32)
        for part in parts[1:]:
            value = value + part[rows, :].astype(F32)
        return value

    small = total(slice(cuts * tall, None))
    for cut, out in enumerate(outs):
        if cut == cuts:
            out[...] = small
            continue
        out[:tall, :] = total(slice(cut * tall, (cut + 1) * tall)).astype(BF)
        if out.shape[0] > tall:
            out[tall:, :] = small.astype(BF)


def merge(parts, cuts, extra, ends):
    rows, width = parts[0].shape
    tall = (rows - extra) // cuts
    if ends:
        outs = [jax.ShapeDtypeStruct((tall, width), BF), jax.ShapeDtypeStruct((extra, width), F32)]
    else:
        outs = [jax.ShapeDtypeStruct((tall + extra, width), BF)] * cuts
    return pl.pallas_call(
        functools.partial(merge_kernel, cuts, extra, len(parts)),
        grid=(1,),
        in_specs=[whole((rows, width))] * len(parts),
        out_specs=[whole(out.shape) for out in outs],
        out_shape=outs,
        compiler_params=params(),
        cost_estimate=cost(1e6, 4e6),
        name="merge",
    )(*parts)


def after(value, *others):
    return lax.optimization_barrier((value, *others))[0]


def sum_over_all(own, sent, groups, extra, beside):
    cores, sides, layers = groups
    done = []

    def spread(own, sent, axis, scale):
        came = [jump(part, axis, scale * far) for far, part in enumerate(sent, 1)]
        work = beside[len(done)](own)
        done.append(work)
        return [own] + list(after(tuple(came), work))

    half = merge([own, jump(sent, "dp", 1)], sides, extra, False)
    flat = merge(spread(half[0], half[1:], "expert", 1), layers, extra, False)
    spot, small = merge(spread(flat[0], flat[1:], "dp", cores), 1, extra, True)
    flat = jnp.stack(spread(spot, [spot] * (layers - 1), "dp", cores))
    half = jnp.stack(spread(flat, [flat] * (sides - 1), "expert", 1))
    half = half.reshape(sides * layers, *spot.shape)
    return half, jump(half, "dp", 1), small, done


def per_device(
    tokens, gain_one, w_qkv, w_proj, gain_two, w_router, w_in, w_eout, picks, keep, grad_out
):
    count, width = tokens.shape
    local = w_in.shape[0]
    owners = lax.axis_size("expert")
    shards = lax.axis_size("dp")
    experts = local * owners
    capacity = 8 * ((21 * count + 80 * experts - 1) // (80 * experts))
    me, row = lax.axis_index("expert"), lax.axis_index("dp")
    cores = 2
    groups = (cores, owners, shards // cores)
    here = jnp.stack([row % cores, me, row // cores]).astype(jnp.int32)
    ids = jnp.arange(experts, dtype=jnp.int32).reshape(owners, local).T.reshape(-1)

    def swap(sent):
        return lax.all_to_all(sent, "expert", split_axis=0, concat_axis=0, tiled=True)

    index_rows, starts = places(ids, picks, keep, capacity)
    send = lambda srcs, *plan: dispatch(srcs, starts, index_rows, owners, capacity, plan)
    (dy_first,) = send([grad_out], (0, (0,)))
    got = swap(dy_first)
    hidden, rows, qkv, probs, mixed = attend(
        after(tokens, dy_first), gain_one, w_qkv, w_proj, gain_two
    )
    (x_first,) = send([rows], (0, (0,)))
    arrived = [[(swap(after(x_first, got)), 0), (got, 0)]]
    kept = [[(x_first, 0), (dy_first, 0)]]
    others = send([after(rows, x_first), grad_out], *[(part, (0, 1)) for part in range(1, local)])
    for sent in others:
        got = swap(after(sent, arrived[-1][0][0]))
        arrived.append([(got, 0), (got, 1)])
        kept.append([(sent, 0), (sent, 1)])
    index = index_rows.transpose(0, 2, 1).reshape(count, 2)
    head = w_router.astype(BF)
    rest = (w_router - head.astype(F32)).astype(BF)
    gap = ((0, 0), (0, LANES - experts))
    router = jnp.concatenate([jnp.pad(head, gap), jnp.pad(rest, gap)], axis=1)
    router_back = jnp.concatenate([jnp.pad(head, gap).T, jnp.pad(rest, gap).T], axis=0)
    downs, own_dx, own_out, sums, outs, routers = [], [], [], [], None, []
    for part in range(local):
        mine = jnp.stack([me * local + part, me]).astype(jnp.int32)
        final = part == local - 1
        one = lambda own, given, outs: expert_pass(
            part, mine, *(kept if own else arrived)[part], w_in, w_eout, router, router_back,
            experts, capacity, shards, own, given, outs,
        )
        if final:
            dx, outs, *given = one(False, None, outs)
            own_parts = list(one(True, given, None))
        else:
            own_parts = list(one(True, None, None))
            dx, outs, *own_parts[2:] = one(False, own_parts[2:], outs)
        got = swap(after(dx, got))
        downs.append((got, 0))
        own_dx.append(own_parts[0])
        own_out.append(own_parts[1])
        grad, router_part = own_parts[2:]
        grad = grad.reshape(shards * grad.shape[1], grad.shape[2])
        sums.append(lax.psum_scatter(grad, "dp", scatter_dimension=0, tiled=True))
        routers.append(router_part)
    outs = swap(after(outs, got))
    grad_hidden, dqkv, own, sent = back(
        starts, here, groups, index, hidden, tokens, grad_out, qkv, probs, mixed, gain_one,
        w_qkv, w_proj, gain_two, downs, own_dx, routers, capacity,
    )
    sent = after(sent, outs)
    blocks = count // BLOCK
    cuts = [0, blocks // 3, 2 * blocks // 3, blocks]
    grad_tokens = [None]

    def make_top(tie):
        parts = [(outs, part) for part in range(local)]
        return top(starts, here, index, after(hidden, tie), parts, own_out, capacity)

    def make_last(turn, tie):
        grad_tokens.append(
            last(
                cuts[turn], cuts[turn + 1], grad_tokens[-1], after(dqkv, tie), grad_hidden,
                tokens, gain_one, w_qkv,
            )
        )
        return grad_tokens[-1]

    own, other, small, done = sum_over_all(
        own, sent, groups, small_rows(experts), [make_top] + [functools.partial(make_last, turn) for turn in range(3)]
    )
    block_out, grad_tokens = done[0], done[3]
    grad_qkv, grad_proj = lay(groups, here, own, other)
    tall = width // shards
    grad_in = jnp.stack([part[:tall] for part in sums]).astype(F32)
    grad_eout = jnp.stack(
        [part[tall:].reshape(tall, -1, width).transpose(1, 0, 2).reshape(-1, width) for part in sums]
    ).astype(F32)
    return (
        block_out,
        grad_tokens,
        small[experts] / gain_one,
        grad_qkv,
        grad_proj,
        small[experts + 1],
        small[:experts].T,
        grad_in,
        grad_eout,
    )


def solution(mesh):
    rows = P(("dp", "expert"), None)
    experts = P("expert", None, None)
    return jax.shard_map(
        per_device,
        mesh=mesh,
        in_specs=(rows, P(), P(), P(), P(), P(), experts, experts, rows, rows, rows),
        out_specs=(
            rows, rows, P(), P(), P(), P(), P(), P("expert", "dp", None), P("expert", "dp", None),
        ),
        check_vma=False,
    )
```

```python
import functools

import jax
import jax.numpy as jnp
from jax import lax
from jax.experimental import pallas as pl
from jax.experimental.pallas import tpu as pltpu
from jax.sharding import PartitionSpec as P

HEADS = 8
PATCHES = 49
LANES = 128
PAIR = 2 * PATCHES
PAIR_PAD = 112
BLOCK_PAIRS = 4
BLOCK = BLOCK_PAIRS * PAIR
BLOCK_PAD = BLOCK_PAIRS * PAIR_PAD
BF = jnp.bfloat16
F32 = jnp.float32
VMEM_BYTES = 62 * 1024 * 1024
FCUT = 256


def params():
    return pltpu.CompilerParams(
        dimension_semantics=("arbitrary",), vmem_limit_bytes=VMEM_BYTES
    )


def cost(flops, moved, special=0):
    return pl.CostEstimate(
        flops=int(flops), bytes_accessed=int(moved), transcendentals=int(special)
    )


def whole(shape):
    return pl.BlockSpec(shape, lambda *_: (0,) * len(shape))


def dot(left, right):
    return jnp.dot(left, right, preferred_element_type=F32)


def dot_rt(left, right):
    return lax.dot_general(left, right, (((1,), (1,)), ((), ())), preferred_element_type=F32)


def dot_lt(left, right):
    return lax.dot_general(left, right, (((0,), (0,)), ((), ())), preferred_element_type=F32)


def norm_parts(values):
    mean = jnp.mean(values, axis=-1, keepdims=True)
    cent = values - mean
    factor = lax.rsqrt(jnp.mean(cent * cent, axis=-1, keepdims=True) + 1e-06)
    return cent * factor, factor


def norm_back(grad_normed, normed_hat, factor, gain):
    grad_hat = grad_normed * gain
    inner = grad_hat - jnp.mean(grad_hat, axis=-1, keepdims=True)
    inner = inner - normed_hat * jnp.mean(grad_hat * normed_hat, axis=-1, keepdims=True)
    return factor * inner


def spread_rows(compact, padded):
    for pair in range(BLOCK_PAIRS):
        padded[PAIR_PAD * pair : PAIR_PAD * pair + PAIR] = compact[PAIR * pair : PAIR * pair + PAIR]


def gather_rows(padded, compact):
    for pair in range(BLOCK_PAIRS):
        compact[PAIR * pair : PAIR * pair + PAIR] = padded[PAIR_PAD * pair : PAIR_PAD * pair + PAIR]


def clear_gaps(padded):
    for pair in range(BLOCK_PAIRS):
        low = PAIR_PAD * pair + PAIR
        padded[low : low + PAIR_PAD - PAIR] = jnp.zeros((PAIR_PAD - PAIR, padded.shape[1]), F32)


def image_of(position):
    return (position >= PATCHES).astype(jnp.int32) + (position >= PAIR).astype(jnp.int32)


def same_image():
    rows = lax.broadcasted_iota(jnp.int32, (2 * PAIR_PAD, PAIR_PAD), 0)
    rows = jnp.where(rows >= PAIR_PAD, rows - PAIR_PAD, rows)
    cols = lax.broadcasted_iota(jnp.int32, (2 * PAIR_PAD, PAIR_PAD), 1)
    return image_of(rows) == image_of(cols)


def low_half():
    return lax.broadcasted_iota(jnp.int32, (PAIR_PAD, LANES), 1) < LANES // 2


def two_heads(values, low):
    zero = jnp.zeros_like(values)
    return jnp.concatenate([jnp.where(low, values, zero), jnp.where(low, zero, values)], axis=0)


def one_row(values, low):
    return jnp.where(low, values[:PAIR_PAD], values[PAIR_PAD:])


def attend_kernel(
    tok_ref, gain_one_ref, qkv_w_ref, proj_w_ref, gain_two_ref,
    hidden_ref, rows_ref, qkv_ref, probs_ref, mixed_ref,
    compact, padded, scores,
):
    width = tok_ref.shape[1]
    factor_qk = (width // HEADS) ** (-0.5)
    clear_gaps(padded)
    inputs = tok_ref[...].astype(F32)
    compact[...] = norm_parts(inputs)[0] * gain_one_ref[...]
    spread_rows(compact, padded)
    qkv_ref[...] = dot(padded[...].astype(BF), qkv_w_ref[...]).astype(BF)
    valid = same_image()
    low = low_half()
    for pair in range(BLOCK_PAIRS):
        rows = slice(PAIR_PAD * pair, PAIR_PAD * (pair + 1))
        for two in range(width // LANES):
            cols = slice(LANES * two, LANES * (two + 1))
            query = qkv_ref[rows, cols]
            keys = qkv_ref[rows, width + LANES * two : width + LANES * (two + 1)]
            step = (pair * (width // LANES) + two) * 2 * PAIR_PAD
            scores[step : step + 2 * PAIR_PAD, :] = jnp.where(
                valid, dot_rt(two_heads(query, low), keys), -1e30
            )
    for pair in range(BLOCK_PAIRS):
        each = 2 * PAIR_PAD * (width // LANES)
        part = slice(each * pair, each * (pair + 1))
        logits = scores[part, :]
        highest = jnp.max(logits, axis=-1, keepdims=True)
        expo = jnp.exp((logits - highest) * factor_qk)
        probs_ref[part, :] = (expo / jnp.sum(expo, axis=-1, keepdims=True)).astype(BF)
    for pair in range(BLOCK_PAIRS):
        rows = slice(PAIR_PAD * pair, PAIR_PAD * (pair + 1))
        for two in range(width // LANES):
            cols = slice(LANES * two, LANES * (two + 1))
            values = qkv_ref[rows, 2 * width + LANES * two : 2 * width + LANES * (two + 1)]
            step = (pair * (width // LANES) + two) * 2 * PAIR_PAD
            probs = probs_ref[step : step + 2 * PAIR_PAD, :]
            mixed_ref[rows, cols] = one_row(dot(probs, values), low).astype(BF)
    padded[...] = dot(mixed_ref[...], proj_w_ref[...])
    gather_rows(padded, compact)
    hidden = inputs + compact[...]
    hidden_ref[...] = hidden
    rows_ref[...] = (norm_parts(hidden)[0] * gain_two_ref[...]).astype(BF)


def attend(tokens, gain_one, w_qkv, w_proj, gain_two):
    count, width = tokens.shape
    blocks = count // BLOCK
    prob_rows = BLOCK_PAIRS * (width // LANES) * 2 * PAIR_PAD
    row = lambda shape: pl.BlockSpec(shape, lambda step: (step, 0))
    flops = 2 * blocks * BLOCK_PAD * width * (4 * width + 4 * PAIR_PAD)
    return pl.pallas_call(
        attend_kernel,
        grid=(blocks,),
        in_specs=[
            row((BLOCK, width)), whole((1, width)), whole(w_qkv.shape), whole(w_proj.shape),
            whole((1, width)),
        ],
        out_specs=[
            row((BLOCK, width)), row((BLOCK, width)), row((BLOCK_PAD, 3 * width)),
            row((prob_rows, PAIR_PAD)), row((BLOCK_PAD, width)),
        ],
        out_shape=[
            jax.ShapeDtypeStruct((count, width), F32),
            jax.ShapeDtypeStruct((count, width), BF),
            jax.ShapeDtypeStruct((blocks * BLOCK_PAD, 3 * width), BF),
            jax.ShapeDtypeStruct((blocks * prob_rows, PAIR_PAD), BF),
            jax.ShapeDtypeStruct((blocks * BLOCK_PAD, width), BF),
        ],
        scratch_shapes=[
            pltpu.VMEM((BLOCK, width), F32), pltpu.VMEM((BLOCK_PAD, width), F32),
            pltpu.VMEM((prob_rows, PAIR_PAD), F32),
        ],
        compiler_params=params(),
        cost_estimate=cost(flops, 30e6, blocks * prob_rows * LANES),
        name="attend",
    )(tokens, gain_one[None, :], w_qkv, w_proj, gain_two[None, :])


def place_kernel(capacity, ids_ref, picks_ref, index_ref, starts_ref, carry):
    step = pl.program_id(0)

    @pl.when(step == 0)
    def _():
        carry[...] = jnp.zeros(carry.shape, F32)
        starts_ref[...] = jnp.zeros(starts_ref.shape, jnp.int32)

    experts, block = ids_ref.shape[0], picks_ref.shape[2]
    ids = ids_ref[...]
    names = [picks_ref[0, c : c + 1, :] == ids for c in (0, 1)]
    named = (names[0] | names[1]).astype(F32)
    earlier = lax.broadcasted_iota(jnp.int32, (block, block), 0) < lax.broadcasted_iota(
        jnp.int32, (block, block), 1
    )
    before = dot(named.astype(BF), earlier.astype(F32).astype(BF)) + carry[:, 0:1]
    spot = before + (lax.broadcasted_iota(jnp.int32, (experts, block), 0) * capacity).astype(F32)
    for c in (0, 1):
        found = jnp.sum(jnp.where(names[c], spot, 0.0), axis=0, keepdims=True).astype(jnp.int32)
        index_ref[0, c : c + 1, :] = jnp.where(picks_ref[0, 2 + c : 3 + c, :] > 0, found, -1)
    after = carry[...] + jnp.sum(named, axis=1, keepdims=True)
    carry[...] = after
    lane = lax.broadcasted_iota(jnp.int32, (experts, LANES), 1)
    starts_ref[...] = jnp.where(lane == step + 1, after.astype(jnp.int32), starts_ref[...])


def places(ids, picks, keep, capacity):
    count = picks.shape[0]
    blocks = count // BLOCK
    experts = ids.shape[0]
    turned = jnp.concatenate([picks, keep], axis=1).reshape(blocks, BLOCK, 4).transpose(0, 2, 1)
    return pl.pallas_call(
        functools.partial(place_kernel, capacity),
        grid=(blocks,),
        in_specs=[whole((experts, 1)), pl.BlockSpec((1, 4, BLOCK), lambda step: (step, 0, 0))],
        out_specs=[
            pl.BlockSpec((1, 2, BLOCK), lambda step: (step, 0, 0)), whole((experts, LANES)),
        ],
        out_shape=[
            jax.ShapeDtypeStruct((blocks, 2, BLOCK), jnp.int32),
            jax.ShapeDtypeStruct((experts, LANES), jnp.int32),
        ],
        scratch_shapes=[pltpu.VMEM((experts, LANES), F32)],
        compiler_params=params(),
        cost_estimate=cost(1e8, 1e5),
        name="places",
    )(ids[:, None], turned)


def window_rows(experts, capacity):
    return min(capacity, 1024 // experts)


def window_at(starts_ref, expert, step, turn, window, capacity):
    low = starts_ref[expert, step]
    begin = (low // 16) * 16 + turn * window
    at = pl.multiple_of(jnp.minimum(begin, capacity - window), 16)
    return begin, starts_ref[expert, step + 1], at


def turns(starts_ref, step, experts, window):
    most = 0
    for expert in experts:
        low = (starts_ref[expert, step] // 16) * 16
        most = jnp.maximum(most, (starts_ref[expert, step + 1] - low + window - 1) // window)
    return most


def dispatch_kernel(window, capacity, plan, sources, starts_ref, index_ref, *refs):
    src_refs, outs, (spots, got) = refs[:sources], refs[sources:-2], refs[-2:]
    owners = outs[0].shape[0]
    step = pl.program_id(0)
    named = [owners * part + owner for part, _ in plan for owner in range(owners)]

    @pl.when(step == 0)
    def _():
        for out in outs:
            out[...] = jnp.zeros(out.shape, out.dtype)

    place = lax.broadcasted_iota(jnp.int32, (window, index_ref.shape[2]), 0)
    first, second = index_ref[0, 0:1, :], index_ref[0, 1:2, :]

    def one_turn(turn, carry):
        for (part, used), out in zip(plan, outs):
            spans = []
            for owner in range(owners):
                expert = part * owners + owner
                begin, _, at = window_at(starts_ref, expert, step, turn, window, capacity)
                shift = expert * capacity
                near = jnp.where(first >= shift + begin, first - (shift + at), -1)
                far = jnp.where(second >= shift + begin, second - (shift + at), -1)
                hit = jnp.where((near >= 0) & (near < window), near, far)
                spots[window * owner : window * (owner + 1), :] = (
                    (place == hit).astype(F32).astype(BF)
                )
                spans.append(at)
            for order, which in enumerate(used):
                got[...] = dot(spots[...], src_refs[which][...])
                for owner, at in enumerate(spans):
                    rows = pl.ds(pl.multiple_of(at + order * capacity, 16), window)
                    held = out[owner, rows, :].astype(F32)
                    out[owner, rows, :] = (
                        held + got[window * owner : window * (owner + 1), :]
                    ).astype(BF)
        return carry

    lax.fori_loop(0, turns(starts_ref, step, named, window), one_turn, 0)


def dispatch(srcs, starts, index_rows, owners, capacity, plan):
    count, width = srcs[0].shape
    window = window_rows(starts.shape[0], capacity)
    shapes = [(owners, len(used) * capacity, width) for _, used in plan]
    return pl.pallas_call(
        functools.partial(dispatch_kernel, window, capacity, plan, len(srcs)),
        grid_spec=pltpu.PrefetchScalarGridSpec(
            num_scalar_prefetch=1,
            grid=(count // BLOCK,),
            in_specs=[pl.BlockSpec((1, 2, BLOCK), lambda step, *_: (step, 0, 0))]
            + [pl.BlockSpec((BLOCK, width), lambda step, *_: (step, 0))] * len(srcs),
            out_specs=[whole(shape) for shape in shapes],
            scratch_shapes=[
                pltpu.VMEM((owners * window, BLOCK), BF),
                pltpu.VMEM((owners * window, width), F32),
            ],
        ),
        out_shape=[jax.ShapeDtypeStruct(shape, BF) for shape in shapes],
        compiler_params=params(),
        cost_estimate=cost(6e9, 8e6),
        name="dispatch",
    )(starts, index_rows, *srcs)


def combine_block(window, step, me, starts_ref, index_ref, bufs, own_bufs, wins, acc):
    owners, capacity = bufs[0].shape[:2]
    experts = owners * len(bufs)
    lane = lax.broadcasted_iota(jnp.int32, (1, experts * window), 1)
    acc[...] = jnp.zeros(acc.shape, F32)

    def one_turn(turn, carry):
        seen = jnp.full((1, experts * window), -2, jnp.int32)
        for expert in range(experts):
            part, owner = expert // owners, expert % owners
            begin, high, at = window_at(starts_ref, expert, step, turn, window, capacity)
            slot = lane + (at - expert * window)
            fresh = (slot >= begin) & (slot < high)
            mine = (lane >= expert * window) & (lane < (expert + 1) * window)
            seen = jnp.where(mine & fresh, slot + expert * capacity, seen)
            to = slice(window * expert, window * (expert + 1))
            if own_bufs[part] is None:
                wins[to, :] = bufs[part][owner, pl.ds(at, window), :]
            else:
                wins[to, :] = jnp.where(
                    me == owner, own_bufs[part][0, pl.ds(at, window), :],
                    bufs[part][owner, pl.ds(at, window), :],
                )
        hit = (index_ref[:, 0:1] == seen) | (index_ref[:, 1:2] == seen)
        acc[...] += dot(hit.astype(F32).astype(BF), wins[...])
        return carry

    lax.fori_loop(0, turns(starts_ref, step, range(experts), window), one_turn, 0)


def top_kernel(early, starts_ref, here_ref, index_ref, hidden_ref, head_ref, tail_ref, own_first_ref, own_second_ref, out_ref, first, second, wins, acc, sems):
    step = pl.program_id(0)
    experts = starts_ref.shape[0]
    window, capacity = wins.shape[0] // experts, first.shape[1]
    late = capacity - early

    @pl.when(step == 0)
    def _():
        copies = [
            pltpu.make_async_copy(head_ref.at[:, pl.ds(capacity, early), :], first.at[:, pl.ds(0, early), :], sems.at[0]),
            pltpu.make_async_copy(tail_ref.at[:, pl.ds(0, late), :], first.at[:, pl.ds(early, late), :], sems.at[1]),
            pltpu.make_async_copy(tail_ref.at[:, pl.ds(late, capacity), :], second, sems.at[2]),
        ]
        for copy in copies:
            copy.start()
        for copy in copies:
            copy.wait()
        me = pl.ds(here_ref[1], 1)
        copies = [
            pltpu.make_async_copy(own_first_ref.at[me], first.at[me, pl.ds(early, late), :], sems.at[3]),
            pltpu.make_async_copy(own_second_ref, second.at[me], sems.at[4]),
        ]
        for copy in copies:
            copy.start()
        for copy in copies:
            copy.wait()

    combine_block(window, step, 0, starts_ref, index_ref, [first, second], [None, None], wins, acc)
    out_ref[...] = (hidden_ref[...] + acc[...]).astype(BF)


def top(starts, here, index, hidden, head, tail, own_first, own_second, early, capacity):
    count, width = hidden.shape
    experts = starts.shape[0]
    window = window_rows(experts, capacity)
    row = lambda shape: pl.BlockSpec(shape, lambda step, *_: (step, 0))
    held = pltpu.VMEM((head.shape[0], capacity, width), BF)
    return pl.pallas_call(
        functools.partial(top_kernel, early),
        grid_spec=pltpu.PrefetchScalarGridSpec(
            num_scalar_prefetch=2,
            grid=(count // BLOCK,),
            in_specs=[row((BLOCK, 2)), row((BLOCK, width))] + [pl.BlockSpec(memory_space=pl.ANY)] * 4,
            out_specs=row((BLOCK, width)),
            scratch_shapes=[
                held, held, pltpu.VMEM((experts * window, width), BF),
                pltpu.VMEM((BLOCK, width), F32), pltpu.SemaphoreType.DMA((5,)),
            ],
        ),
        out_shape=jax.ShapeDtypeStruct((count, width), BF),
        compiler_params=params(),
        cost_estimate=cost(6e9, 12e6),
        name="top",
    )(starts, here, index, hidden, head, tail, own_first, own_second)


def gelu_parts(values):
    size = 1.0 + (0.3275911 * 0.7071067811865476) * jnp.abs(values)
    near = pl.reciprocal(size, approx=True)
    near = near * (2.0 - size * near)
    expo = jnp.exp2((-0.5 * 1.4426950408889634) * (values * values))
    poly = 0.5 * 1.061405429
    for term in (-1.453152027, 1.421413741, -0.284496736, 0.254829592):
        poly = poly * near + 0.5 * term
    tail = poly * near * expo
    share = jnp.where(values >= 0, 1.0 - tail, tail)
    return values * share, share + values * (0.3989422804014327 * expo)


def expert_kernel(
    experts, fcut, begun, part, joins, mine_ref, up_ref, down_ref, router_ref, back_ref, x_ref, dy_ref, *refs
):
    given, refs = refs[: 3 * begun], refs[3 * begun :]
    if joins:
        before_ref, refs = refs[0], refs[1:]
    *grad_refs, grouter_ref = refs[2:-5]
    acc_up, acc_down, acc_router, acc_out, acc_dx = refs[-5:]
    step = pl.program_id(0)
    hidden_units = up_ref.shape[1]
    _, capacity, width = x_ref.shape
    count = capacity

    @pl.when(step == 0)
    def _():
        if begun:
            acc_up[...] = given[0][...].astype(F32)
            acc_down[...] = given[1][...].astype(F32)
            acc_router[:, :LANES] = given[2][...]
            acc_router[:, LANES:] = jnp.zeros((width, LANES), F32)
        else:
            acc_up[...] = jnp.zeros(acc_up.shape, F32)
            acc_down[...] = jnp.zeros(acc_down.shape, F32)
            acc_router[...] = jnp.zeros(acc_router.shape, F32)

    rows = x_ref[...].reshape(count, width)
    logits = dot(rows, router_ref[...])
    logits = logits[:, :LANES] + logits[:, LANES:]
    lane = lax.broadcasted_iota(jnp.int32, (count, LANES), 1)
    logits = jnp.where(lane < experts, logits, -1e30)
    expo = jnp.exp(logits - jnp.max(logits, axis=-1, keepdims=True))
    gates = expo / jnp.sum(expo, axis=-1, keepdims=True)
    own = (lane == mine_ref[0]).astype(F32)
    chosen = jnp.sum(gates * own, axis=-1, keepdims=True)
    pair = (chosen * dy_ref[...].reshape(count, width).astype(F32)).astype(BF)
    rows_t = rows.T
    pair_t = pair.T
    chunks = [slice(low, low + fcut) for low in range(0, hidden_units, fcut)]
    ahead = lambda cols: (dot(rows, up_ref[:, cols]), dot_rt(pair, down_ref[cols, :]))
    ready = ahead(chunks[0])
    for turn, cols in enumerate(chunks):
        pre, grad_act = ready
        if turn + 1 < len(chunks):
            ready = ahead(chunks[turn + 1])
        act, slope = gelu_parts(pre)
        act = act.astype(BF)
        grad_pre = (grad_act * slope).astype(BF)
        acc_up[:, cols] += dot(rows_t, grad_pre)
        acc_down[:, cols] += dot(pair_t, act)
        if turn == 0:
            acc_out[...] = dot(act, down_ref[cols, :])
            acc_dx[...] = dot_rt(grad_pre, up_ref[:, cols])
        else:
            acc_out[...] += dot(act, down_ref[cols, :])
            acc_dx[...] += dot_rt(grad_pre, up_ref[:, cols])
    inner = jnp.sum(acc_out[...] * pair.astype(F32), axis=-1, keepdims=True)
    grad_logits = inner * (own - gates)
    head = grad_logits.astype(BF)
    rest = (grad_logits - head.astype(F32)).astype(BF)
    acc_router[...] += dot(rows_t, jnp.concatenate([head, rest], axis=1))
    out = (chosen * acc_out[...]).astype(BF)
    grad_rows = (acc_dx[...] + dot(jnp.concatenate([head, head], axis=1), back_ref[...])).astype(BF)
    if part:
        refs[0][0] = grad_rows
        late = refs[1].shape[1] - capacity
        if late:
            refs[1][0, :late, :] = before_ref[0]
        refs[1][0, late:, :] = out
    else:
        early = refs[0].shape[1] - capacity
        refs[0][0, :capacity, :] = grad_rows
        refs[0][0, capacity:, :] = out[:early]
        refs[1][0] = out[early:]

    @pl.when(step == pl.num_programs(0) - 1)
    def _():
        grouter_ref[...] = acc_router[:, :LANES] + acc_router[:, LANES:]
        if not begun:
            grad_refs[0][...] = acc_up[...].astype(BF)
            grad_refs[1][...] = acc_down[...].astype(BF)
            return
        grad_ref = grad_refs[0]
        shards, tall, _ = grad_ref.shape
        up_rows, down_rows = width // shards, hidden_units // shards
        piece = tall - up_rows
        for shard in range(shards):
            grad_ref[shard, :up_rows, :] = acc_up[up_rows * shard : up_rows * (shard + 1), :].astype(BF)
            turned = acc_down[:, down_rows * shard : down_rows * (shard + 1)].T.astype(BF)
            for part in range(down_rows // piece):
                grad_ref[shard, up_rows:, width * part : width * (part + 1)] = (
                    turned[piece * part : piece * (part + 1), :]
                )


def expert_pass(part, mine, rows, grads, weights, early, experts, capacity, shards, own, given, before, taken):
    (rows, rows_at), (grads, grads_at) = rows, grads
    w_up, w_down, router, router_back = weights
    sources, _, width = rows.shape
    units = w_up.shape[2]
    source = lambda step, mine_ref: (mine_ref[1] + (0 if own else 1) + step) % sources
    block = lambda tall, at: pl.BlockSpec(
        (1, tall, width), lambda step, mine_ref: (source(step, mine_ref), at, 0)
    )
    weight = lambda shape: pl.BlockSpec((None,) + shape[1:], lambda *_: (part, 0, 0))
    late = capacity - early
    talls = [capacity, late + capacity] if part else [capacity + early, late]
    sent = [jax.ShapeDtypeStruct((sources, tall, width), BF) for tall in talls]
    sent_specs = [block(tall, 0) for tall in talls]
    if part and own:
        sent = [jax.ShapeDtypeStruct((1, capacity, width), BF)] * 2
        sent_specs = [whole((1, capacity, width))] * 2
    if given:
        sums = [jax.ShapeDtypeStruct((shards, width // shards * 2, units), BF)]
    else:
        sums = [jax.ShapeDtypeStruct((width, units), BF)] * 2
    sums.append(jax.ShapeDtypeStruct((width, LANES), F32))
    steps = 1 if own else sources - 1
    joins = bool(part) and not own
    more = list(given) + ([before] if joins else [])
    more_specs = [whole(array.shape) for array in given] + ([block(late, 0)] if joins else [])
    skip = 7 + len(more)

    def body(*refs):
        expert_kernel(
            experts, min(FCUT, units), bool(given), part, joins, *refs[:skip], *refs[skip + len(taken) :]
        )

    return pl.pallas_call(
        body,
        grid_spec=pltpu.PrefetchScalarGridSpec(
            num_scalar_prefetch=1,
            grid=(steps,),
            in_specs=[
                weight(w_up.shape), weight(w_down.shape), whole(router.shape),
                whole(router_back.shape), block(capacity, rows_at), block(capacity, grads_at),
            ] + more_specs + [pl.BlockSpec(memory_space=pl.ANY)] * len(taken),
            out_specs=sent_specs + [whole(array.shape) for array in sums],
            scratch_shapes=[
                pltpu.VMEM((width, units), F32),
                pltpu.VMEM((width, units), F32),
                pltpu.VMEM((width, 2 * LANES), F32),
                pltpu.VMEM((capacity, width), F32),
                pltpu.VMEM((capacity, width), F32),
            ],
        ),
        out_shape=sent + sums,
        input_output_aliases={skip + at: to for at, to in enumerate(taken)},
        compiler_params=params(),
        cost_estimate=cost(
            20 * steps * capacity * width * units, 30e6, 2 * steps * capacity * units
        ),
        name="expert_own" if own else "expert_others",
    )(mine, *weights, rows, grads, *more, *taken.values())


def back_kernel(
    window, groups, starts_ref, here_ref, index_ref, hidden_ref, tok_ref, dy_ref, qkv_ref,
    probs_ref, mixed_ref, gain_one_ref, qkv_w_ref, proj_w_ref, gain_two_ref, *refs,
):
    bufs, own_bufs, router_refs = refs[:2], [None, refs[2]], refs[3:5]
    ghid_ref, dqkv_ref, own_ref, sent_ref = refs[5:-9]
    wins, acc, compact, padded, acc_qkv, acc_proj, acc_gain, dscores, dscores_low = refs[-9:]
    experts = starts_ref.shape[0]
    step = pl.program_id(0)
    width = tok_ref.shape[1]
    factor_qk = (width // HEADS) ** (-0.5)

    @pl.when(step == 0)
    def _():
        for ref in (acc_qkv, acc_proj, acc_gain):
            ref[...] = jnp.zeros(ref.shape, F32)

    combine_block(window, step, here_ref[1], starts_ref, index_ref, bufs, own_bufs, wins, acc)
    clear_gaps(padded)
    hat_two, scale_two = norm_parts(hidden_ref[...])
    grad_normed = acc[...]
    acc_gain[...] += jnp.sum(grad_normed * hat_two, axis=0, keepdims=True)
    grad_hidden = dy_ref[...].astype(F32) + norm_back(
        grad_normed, hat_two, scale_two, gain_two_ref[...]
    )
    ghid_ref[...] = grad_hidden
    compact[...] = grad_hidden
    spread_rows(compact, padded)
    grad_attn = padded[...].astype(BF)
    acc_proj[...] += dot_lt(mixed_ref[...], grad_attn)
    grad_mixed = dot_rt(grad_attn, proj_w_ref[...]).astype(BF)
    low = low_half()
    for pair in range(BLOCK_PAIRS):
        rows = slice(PAIR_PAD * pair, PAIR_PAD * (pair + 1))
        for two in range(width // LANES):
            cols = slice(LANES * two, LANES * (two + 1))
            key_cols = slice(width + LANES * two, width + LANES * (two + 1))
            value_cols = slice(2 * width + LANES * two, 2 * width + LANES * (two + 1))
            at = (pair * (width // LANES) + two) * 2 * PAIR_PAD
            dscores[at : at + 2 * PAIR_PAD, :] = dot_rt(
                two_heads(grad_mixed[rows, cols], low), qkv_ref[rows, value_cols]
            )
    for pair in range(BLOCK_PAIRS):
        each = 2 * PAIR_PAD * (width // LANES)
        part = slice(each * pair, each * (pair + 1))
        wide, grad_probs = probs_ref[part, :].astype(F32), dscores[part, :]
        meet = jnp.sum(wide * grad_probs, axis=-1, keepdims=True)
        dscores_low[part, :] = (wide * (grad_probs - meet) * factor_qk).astype(BF)
    for pair in range(BLOCK_PAIRS):
        rows = slice(PAIR_PAD * pair, PAIR_PAD * (pair + 1))
        for two in range(width // LANES):
            cols = slice(LANES * two, LANES * (two + 1))
            key_cols = slice(width + LANES * two, width + LANES * (two + 1))
            value_cols = slice(2 * width + LANES * two, 2 * width + LANES * (two + 1))
            at = (pair * (width // LANES) + two) * 2 * PAIR_PAD
            probs = probs_ref[at : at + 2 * PAIR_PAD, :]
            grad_out = two_heads(grad_mixed[rows, cols], low)
            grad_scores = dscores_low[at : at + 2 * PAIR_PAD, :]
            grad_query = one_row(dot(grad_scores, qkv_ref[rows, key_cols]), low)
            dqkv_ref[rows, cols] = grad_query.astype(BF)
            dqkv_ref[rows, key_cols] = dot_lt(
                grad_scores, two_heads(qkv_ref[rows, cols], low)
            ).astype(BF)
            dqkv_ref[rows, value_cols] = dot_lt(probs, grad_out).astype(BF)
    compact[...] = norm_parts(tok_ref[...].astype(F32))[0] * gain_one_ref[...]
    spread_rows(compact, padded)
    acc_qkv[...] += dot_lt(padded[...].astype(BF), dqkv_ref[...])

    @pl.when(step == pl.num_programs(0) - 1)
    def _():
        cores, sides, layers = groups
        half = acc_qkv.shape[0] * 4 // cores
        tall = half // (sides * layers)

        def piece(row):
            part, at = row // width, row % width
            if part < 3:
                return acc_qkv[at : at + tall, width * part : width * (part + 1)]
            return acc_proj[at : at + tall, :]

        for side in range(sides):
            for layer in range(layers):
                low = (side * layers + layer) * tall
                spot = (side ^ here_ref[1]) * layers + (layer ^ here_ref[2])
                to = pl.ds(pl.multiple_of(spot * tall, tall), tall)
                even, odd = piece(low), piece(half + low)
                own_ref[to, :] = jnp.where(here_ref[0] == 0, even, odd).astype(BF)
                sent_ref[to, :] = jnp.where(here_ref[0] == 0, odd, even).astype(BF)
        gain_one_sum = jnp.sum(acc_qkv[...] * qkv_w_ref[...].astype(F32), axis=-1, keepdims=True)
        lane = lax.broadcasted_iota(jnp.int32, (width, LANES), 1)
        router = sum(ref[...] for ref in router_refs)
        small = jnp.where(lane == experts, gain_one_sum, router).T[: own_ref.shape[0] - half, :]
        row = lax.broadcasted_iota(jnp.int32, small.shape, 0)
        small = jnp.where(row == experts + 1, acc_gain[...], small).astype(BF)
        own_ref[half:, :] = small
        sent_ref[half:, :] = small


def small_rows(experts):
    return 16 * -(-(experts + 2) // 16)


def back(starts, here, groups, index, hidden, tokens, dy, qkv, probs, mixed, gain_one, w_qkv, w_proj, gain_two, downs, own, routers, capacity):
    count, width = tokens.shape
    blocks = count // BLOCK
    experts = starts.shape[0]
    window = window_rows(experts, capacity)
    row = lambda shape: pl.BlockSpec(shape, lambda step, *_: (step, 0))
    cores, sides, layers = groups
    assert cores == 2
    sum_shape = (2 * width + small_rows(experts), width)
    flops = 2 * blocks * BLOCK_PAD * width * (8 * width + 10 * PAIR_PAD)
    return pl.pallas_call(
        functools.partial(back_kernel, window, groups),
        grid_spec=pltpu.PrefetchScalarGridSpec(
            num_scalar_prefetch=2,
            grid=(blocks,),
            in_specs=[
                row((BLOCK, 2)), row((BLOCK, width)), row((BLOCK, width)), row((BLOCK, width)),
                row((BLOCK_PAD, 3 * width)), row((probs.shape[0] // blocks, PAIR_PAD)),
                row((BLOCK_PAD, width)),
                whole((1, width)), whole(w_qkv.shape), whole(w_proj.shape), whole((1, width)),
            ] + [whole((downs[0].shape[0], capacity, width))] * 2 + [whole(own.shape)]
            + [whole((width, LANES))] * 2,
            out_specs=[
                row((BLOCK, width)), row((BLOCK_PAD, 3 * width)), whole(sum_shape), whole(sum_shape),
            ],
            scratch_shapes=[
                pltpu.VMEM((experts * window, width), BF),
                pltpu.VMEM((BLOCK, width), F32),
                pltpu.VMEM((BLOCK, width), F32),
                pltpu.VMEM((BLOCK_PAD, width), F32),
                pltpu.VMEM(w_qkv.shape, F32),
                pltpu.VMEM(w_proj.shape, F32),
                pltpu.VMEM((1, width), F32),
                pltpu.VMEM((probs.shape[0] // blocks, PAIR_PAD), F32),
                pltpu.VMEM((probs.shape[0] // blocks, PAIR_PAD), BF),
            ],
        ),
        out_shape=[
            jax.ShapeDtypeStruct((count, width), F32),
            jax.ShapeDtypeStruct(qkv.shape, BF),
            jax.ShapeDtypeStruct(sum_shape, BF),
            jax.ShapeDtypeStruct(sum_shape, BF),
        ],
        compiler_params=params(),
        cost_estimate=cost(1e12, 4000e6),
        name="back",
    )(
        starts, here, index, hidden, tokens, dy, qkv, probs, mixed, gain_one[None, :], w_qkv,
        w_proj, gain_two[None, :], *downs, own, *routers,
    )


def last_kernel(dqkv_ref, ghid_ref, tok_ref, gain_one_ref, qkv_w_ref, *refs):
    out_ref, compact, padded = refs[-3:]
    padded[...] = dot_rt(dqkv_ref[...], qkv_w_ref[...])
    gather_rows(padded, compact)
    hat_one, scale_one = norm_parts(tok_ref[...].astype(F32))
    out_ref[...] = ghid_ref[...] + norm_back(compact[...], hat_one, scale_one, gain_one_ref[...])


def last(low, high, so_far, dqkv, ghid, tokens, gain_one, w_qkv):
    count, width = tokens.shape
    row = lambda shape: pl.BlockSpec(shape, lambda step: (step + low, 0))
    taken = [] if so_far is None else [so_far]
    return pl.pallas_call(
        last_kernel,
        grid=(high - low,),
        in_specs=[
            row((BLOCK_PAD, 3 * width)), row((BLOCK, width)), row((BLOCK, width)),
            whole((1, width)), whole(w_qkv.shape),
        ] + [pl.BlockSpec(memory_space=pl.ANY)] * len(taken),
        out_specs=row((BLOCK, width)),
        out_shape=jax.ShapeDtypeStruct((count, width), F32),
        scratch_shapes=[pltpu.VMEM((BLOCK, width), F32), pltpu.VMEM((BLOCK_PAD, width), F32)],
        input_output_aliases={5: 0} if taken else {},
        compiler_params=params(),
        cost_estimate=cost(6 * BLOCK_PAD * (high - low) * width * width, 20e6),
        name="last",
    )(dqkv, ghid, tokens, gain_one[None, :], w_qkv, *taken)


def lay_kernel(groups, here_ref, own_ref, other_ref, qkv_ref, proj_ref):
    cores, sides, layers = groups
    tall, width = own_ref.shape[1:]
    for core in range(cores):
        for side in range(sides):
            for layer in range(layers):
                low = ((core * sides + side) * layers + layer) * tall
                part, at = low // width, low % width
                spot = (side ^ here_ref[1]) * layers + (layer ^ here_ref[2])
                piece = jnp.where(core == here_ref[0], own_ref[spot].astype(F32), other_ref[spot].astype(F32))
                if part < 3:
                    qkv_ref[at : at + tall, width * part : width * (part + 1)] = piece
                else:
                    proj_ref[at : at + tall, :] = piece


def lay(groups, here, own, other):
    width = own.shape[2]
    return pl.pallas_call(
        functools.partial(lay_kernel, groups),
        grid_spec=pltpu.PrefetchScalarGridSpec(
            num_scalar_prefetch=1,
            grid=(1,),
            in_specs=[whole(own.shape)] * 2,
            out_specs=[whole((width, 3 * width)), whole((width, width))],
        ),
        out_shape=[
            jax.ShapeDtypeStruct((width, 3 * width), F32),
            jax.ShapeDtypeStruct((width, width), F32),
        ],
        compiler_params=params(),
        cost_estimate=cost(1e6, 8e6),
        name="lay",
    )(here, own, other)


def jump(value, axis, far):
    size = lax.axis_size(axis)
    return lax.ppermute(value, axis, [(at, at ^ far) for at in range(size)])


def merge_kernel(cuts, extra, count, *refs):
    parts, outs = refs[:count], refs[count:]
    tall = (parts[0].shape[0] - extra) // cuts

    def total(rows):
        value = parts[0][rows, :].astype(F32)
        for part in parts[1:]:
            value = value + part[rows, :].astype(F32)
        return value

    small = total(slice(cuts * tall, None))
    for cut, out in enumerate(outs):
        if cut == cuts:
            out[...] = small
            continue
        out[:tall, :] = total(slice(cut * tall, (cut + 1) * tall)).astype(BF)
        if out.shape[0] > tall:
            out[tall:, :] = small.astype(BF)


def merge(parts, cuts, extra, ends):
    rows, width = parts[0].shape
    tall = (rows - extra) // cuts
    if ends:
        outs = [jax.ShapeDtypeStruct((tall, width), BF), jax.ShapeDtypeStruct((extra, width), F32)]
    else:
        outs = [jax.ShapeDtypeStruct((tall + extra, width), BF)] * cuts
    return pl.pallas_call(
        functools.partial(merge_kernel, cuts, extra, len(parts)),
        grid=(1,),
        in_specs=[whole((rows, width))] * len(parts),
        out_specs=[whole(out.shape) for out in outs],
        out_shape=outs,
        compiler_params=params(),
        cost_estimate=cost(1e6, 4e6),
        name="merge",
    )(*parts)


def after(value, *others):
    return lax.optimization_barrier((value, *others))[0]


def sum_over_all(own, sent, groups, extra, beside):
    cores, sides, layers = groups
    done = []

    def spread(own, sent, axis, scale):
        came = [jump(part, axis, scale * far) for far, part in enumerate(sent, 1)]
        work = beside[len(done)](own)
        done.append(work)
        return [own] + list(after(tuple(came), jax.tree.leaves(work)[0]))

    half = merge([own, jump(sent, "dp", 1)], sides, extra, False)
    flat = merge(spread(half[0], half[1:], "expert", 1), layers, extra, False)
    spot, small = merge(spread(flat[0], flat[1:], "dp", cores), 1, extra, True)
    flat = jnp.stack(spread(spot, [spot] * (layers - 1), "dp", cores))
    half = jnp.stack(spread(flat, [flat] * (sides - 1), "expert", 1))
    half = half.reshape(sides * layers, *spot.shape)
    return half, jump(half, "dp", 1), small, done


def per_device(
    tokens, gain_one, w_qkv, w_proj, gain_two, w_router, w_in, w_eout, picks, keep, grad_out
):
    count, width = tokens.shape
    local = w_in.shape[0]
    assert local == 2
    owners = lax.axis_size("expert")
    shards = lax.axis_size("dp")
    experts = local * owners
    capacity = 8 * ((21 * count + 80 * experts - 1) // (80 * experts))
    me, row = lax.axis_index("expert"), lax.axis_index("dp")
    cores = 2
    groups = (cores, owners, shards // cores)
    here = jnp.stack([row % cores, me, row // cores]).astype(jnp.int32)
    ids = jnp.arange(experts, dtype=jnp.int32).reshape(owners, local).T.reshape(-1)

    def swap(sent):
        return lax.all_to_all(sent, "expert", split_axis=0, concat_axis=0, tiled=True)

    index_rows, starts = places(ids, picks, keep, capacity)
    send = lambda srcs, *plan: dispatch(srcs, starts, index_rows, owners, capacity, plan)
    (dy_first,) = send([grad_out], (0, (0,)))
    got = swap(dy_first)
    hidden, rows, qkv, probs, mixed = attend(
        after(tokens, dy_first), gain_one, w_qkv, w_proj, gain_two
    )
    (x_first,) = send([rows], (0, (0,)))
    arrived = [[(swap(after(x_first, got)), 0), (got, 0)]]
    kept = [[(x_first, 0), (dy_first, 0)]]
    others = send([after(rows, x_first), grad_out], *[(part, (0, 1)) for part in range(1, local)])
    for sent in others:
        got = swap(after(sent, arrived[-1][0][0]))
        arrived.append([(got, 0), (got, 1)])
        kept.append([(sent, 0), (sent, 1)])
    index = index_rows.transpose(0, 2, 1).reshape(count, 2)
    head = w_router.astype(BF)
    rest = (w_router - head.astype(F32)).astype(BF)
    gap = ((0, 0), (0, LANES - experts))
    router = jnp.concatenate([jnp.pad(head, gap), jnp.pad(rest, gap)], axis=1)
    router_back = jnp.concatenate([jnp.pad(head, gap).T, jnp.pad(rest, gap).T], axis=0)
    early = 16 * (capacity // 32)
    weights = (w_in, w_eout, router, router_back)

    def one(part, own, given, before, *taken):
        mine = jnp.stack([me * local + part, me]).astype(jnp.int32)
        came = (kept if own else arrived)[part]
        taken = dict(zip(range(2 - len(taken), 2), taken))
        return expert_pass(
            part, mine, *came, weights, early, experts, capacity, shards, own, given, before, taken
        )

    def reduce(grad):
        grad = grad.reshape(shards * grad.shape[1], grad.shape[2])
        return lax.psum_scatter(grad, "dp", scatter_dimension=0, tiled=True)

    head, tail, *given = one(0, True, [], None)
    head, tail, grad, router_first = one(0, False, given, None, head, tail)
    sums, tail_first = [reduce(grad)], tail
    head = swap(after(head, got))
    down, tail, *given = one(1, False, [], tail_first)
    down = swap(after(down, head))
    own_down, own_out, grad, router_second = one(1, True, given, None)
    sums.append(reduce(grad))
    tail = swap(after(tail, down))
    grad_hidden, dqkv, own, sent = back(
        starts, here, groups, index, hidden, tokens, grad_out, qkv, probs, mixed, gain_one,
        w_qkv, w_proj, gain_two, [head, down], own_down, [router_first, router_second], capacity,
    )
    sent = after(sent, tail)
    blocks = count // BLOCK
    cuts = [0, blocks // 3, 2 * blocks // 3, blocks]
    grad_tokens = [None]

    tall = width // shards

    def make_top(tie):
        return top(starts, here, index, after(hidden, tie), head, tail, tail_first, own_out, early, capacity)

    def make_last(turn, tie):
        grad_tokens.append(
            last(
                cuts[turn], cuts[turn + 1], grad_tokens[-1], after(dqkv, tie), grad_hidden,
                tokens, gain_one, w_qkv,
            )
        )
        if turn < 2:
            return grad_tokens[-1]
        parts = sums
        grad_in = jnp.stack([part[:tall] for part in parts]).astype(F32)
        grad_eout = jnp.stack(
            [part[tall:].reshape(tall, -1, width).transpose(1, 0, 2).reshape(-1, width) for part in parts]
        ).astype(F32)
        return grad_tokens[-1], grad_in, grad_eout

    own, other, small, done = sum_over_all(
        own, sent, groups, small_rows(experts), [make_top] + [functools.partial(make_last, turn) for turn in range(3)]
    )
    block_out, (grad_tokens, grad_in, grad_eout) = done[0], done[3]
    grad_qkv, grad_proj = lay(groups, here, own, other)
    return (
        block_out,
        grad_tokens,
        small[experts] / gain_one,
        grad_qkv,
        grad_proj,
        small[experts + 1],
        small[:experts].T,
        grad_in,
        grad_eout,
    )


def solution(mesh):
    rows = P(("dp", "expert"), None)
    experts = P("expert", None, None)
    return jax.shard_map(
        per_device,
        mesh=mesh,
        in_specs=(rows, P(), P(), P(), P(), P(), experts, experts, rows, rows, rows),
        out_specs=(
            rows, rows, P(), P(), P(), P(), P(), P("expert", "dp", None), P("expert", "dp", None),
        ),
        check_vma=False,
    )
```

```python
import functools

import jax
import jax.numpy as jnp
from jax import lax
from jax.experimental import pallas as pl
from jax.experimental.pallas import tpu as pltpu
from jax.sharding import PartitionSpec as P

HEADS = 8
PATCHES = 49
LANES = 128
PAIR = 2 * PATCHES
PAIR_PAD = 112
BLOCK_PAIRS = 4
BLOCK = BLOCK_PAIRS * PAIR
BLOCK_PAD = BLOCK_PAIRS * PAIR_PAD
BF = jnp.bfloat16
F32 = jnp.float32
VMEM_BYTES = 62 * 1024 * 1024
FCUT = 256
CHUNK = 256


def params():
    return pltpu.CompilerParams(
        dimension_semantics=("arbitrary",), vmem_limit_bytes=VMEM_BYTES
    )


def cost(flops, moved, special=0):
    return pl.CostEstimate(
        flops=int(flops), bytes_accessed=int(moved), transcendentals=int(special)
    )


def whole(shape):
    return pl.BlockSpec(shape, lambda *_: (0,) * len(shape))


def dot(left, right):
    return jnp.dot(left, right, preferred_element_type=F32)


def dot_rt(left, right):
    return lax.dot_general(left, right, (((1,), (1,)), ((), ())), preferred_element_type=F32)


def dot_lt(left, right):
    return lax.dot_general(left, right, (((0,), (0,)), ((), ())), preferred_element_type=F32)


def norm_parts(values):
    mean = jnp.mean(values, axis=-1, keepdims=True)
    cent = values - mean
    factor = lax.rsqrt(jnp.mean(cent * cent, axis=-1, keepdims=True) + 1e-06)
    return cent * factor, factor


def norm_back(grad_normed, normed_hat, factor, gain):
    grad_hat = grad_normed * gain
    inner = grad_hat - jnp.mean(grad_hat, axis=-1, keepdims=True)
    inner = inner - normed_hat * jnp.mean(grad_hat * normed_hat, axis=-1, keepdims=True)
    return factor * inner


def spread_rows(compact, padded):
    for pair in range(BLOCK_PAIRS):
        padded[PAIR_PAD * pair : PAIR_PAD * pair + PAIR] = compact[PAIR * pair : PAIR * pair + PAIR]


def gather_rows(padded, compact):
    for pair in range(BLOCK_PAIRS):
        compact[PAIR * pair : PAIR * pair + PAIR] = padded[PAIR_PAD * pair : PAIR_PAD * pair + PAIR]


def clear_gaps(padded):
    for pair in range(BLOCK_PAIRS):
        low = PAIR_PAD * pair + PAIR
        padded[low : low + PAIR_PAD - PAIR] = jnp.zeros((PAIR_PAD - PAIR, padded.shape[1]), F32)


def image_of(position):
    return (position >= PATCHES).astype(jnp.int32) + (position >= PAIR).astype(jnp.int32)


def same_image():
    rows = lax.broadcasted_iota(jnp.int32, (2 * PAIR_PAD, PAIR_PAD), 0)
    rows = jnp.where(rows >= PAIR_PAD, rows - PAIR_PAD, rows)
    cols = lax.broadcasted_iota(jnp.int32, (2 * PAIR_PAD, PAIR_PAD), 1)
    return image_of(rows) == image_of(cols)


def low_half():
    return lax.broadcasted_iota(jnp.int32, (PAIR_PAD, LANES), 1) < LANES // 2


def two_heads(values, low):
    zero = jnp.zeros_like(values)
    return jnp.concatenate([jnp.where(low, values, zero), jnp.where(low, zero, values)], axis=0)


def one_row(values, low):
    return jnp.where(low, values[:PAIR_PAD], values[PAIR_PAD:])


def attend_kernel(
    tok_ref, gain_one_ref, qkv_w_ref, proj_w_ref, gain_two_ref,
    hidden_ref, rows_ref, qkv_ref, probs_ref, mixed_ref,
    compact, padded, scores,
):
    width = tok_ref.shape[1]
    factor_qk = (width // HEADS) ** (-0.5)
    clear_gaps(padded)
    inputs = tok_ref[...].astype(F32)
    compact[...] = norm_parts(inputs)[0] * gain_one_ref[...]
    spread_rows(compact, padded)
    qkv_ref[...] = dot(padded[...].astype(BF), qkv_w_ref[...]).astype(BF)
    valid = same_image()
    low = low_half()
    for pair in range(BLOCK_PAIRS):
        rows = slice(PAIR_PAD * pair, PAIR_PAD * (pair + 1))
        for two in range(width // LANES):
            cols = slice(LANES * two, LANES * (two + 1))
            query = qkv_ref[rows, cols]
            keys = qkv_ref[rows, width + LANES * two : width + LANES * (two + 1)]
            step = (pair * (width // LANES) + two) * 2 * PAIR_PAD
            scores[step : step + 2 * PAIR_PAD, :] = jnp.where(
                valid, dot_rt(two_heads(query, low), keys), -1e30
            )
    for pair in range(BLOCK_PAIRS):
        each = 2 * PAIR_PAD * (width // LANES)
        part = slice(each * pair, each * (pair + 1))
        logits = scores[part, :]
        highest = jnp.max(logits, axis=-1, keepdims=True)
        expo = jnp.exp((logits - highest) * factor_qk)
        probs_ref[part, :] = (expo / jnp.sum(expo, axis=-1, keepdims=True)).astype(BF)
    for pair in range(BLOCK_PAIRS):
        rows = slice(PAIR_PAD * pair, PAIR_PAD * (pair + 1))
        for two in range(width // LANES):
            cols = slice(LANES * two, LANES * (two + 1))
            values = qkv_ref[rows, 2 * width + LANES * two : 2 * width + LANES * (two + 1)]
            step = (pair * (width // LANES) + two) * 2 * PAIR_PAD
            probs = probs_ref[step : step + 2 * PAIR_PAD, :]
            mixed_ref[rows, cols] = one_row(dot(probs, values), low).astype(BF)
    padded[...] = dot(mixed_ref[...], proj_w_ref[...])
    gather_rows(padded, compact)
    hidden = inputs + compact[...]
    hidden_ref[...] = hidden
    rows_ref[...] = (norm_parts(hidden)[0] * gain_two_ref[...]).astype(BF)


def attend(tokens, gain_one, w_qkv, w_proj, gain_two):
    count, width = tokens.shape
    blocks = count // BLOCK
    prob_rows = BLOCK_PAIRS * (width // LANES) * 2 * PAIR_PAD
    row = lambda shape: pl.BlockSpec(shape, lambda step: (step, 0))
    flops = 2 * blocks * BLOCK_PAD * width * (4 * width + 4 * PAIR_PAD)
    return pl.pallas_call(
        attend_kernel,
        grid=(blocks,),
        in_specs=[
            row((BLOCK, width)), whole((1, width)), whole(w_qkv.shape), whole(w_proj.shape),
            whole((1, width)),
        ],
        out_specs=[
            row((BLOCK, width)), row((BLOCK, width)), row((BLOCK_PAD, 3 * width)),
            row((prob_rows, PAIR_PAD)), row((BLOCK_PAD, width)),
        ],
        out_shape=[
            jax.ShapeDtypeStruct((count, width), F32),
            jax.ShapeDtypeStruct((count, width), BF),
            jax.ShapeDtypeStruct((blocks * BLOCK_PAD, 3 * width), BF),
            jax.ShapeDtypeStruct((blocks * prob_rows, PAIR_PAD), BF),
            jax.ShapeDtypeStruct((blocks * BLOCK_PAD, width), BF),
        ],
        scratch_shapes=[
            pltpu.VMEM((BLOCK, width), F32), pltpu.VMEM((BLOCK_PAD, width), F32),
            pltpu.VMEM((prob_rows, PAIR_PAD), F32),
        ],
        compiler_params=params(),
        cost_estimate=cost(flops, 30e6, blocks * prob_rows * LANES),
        name="attend",
    )(tokens, gain_one[None, :], w_qkv, w_proj, gain_two[None, :])


def place_kernel(capacity, ids_ref, picks_ref, index_ref, starts_ref, carry):
    step = pl.program_id(0)

    @pl.when(step == 0)
    def _():
        carry[...] = jnp.zeros(carry.shape, F32)
        starts_ref[...] = jnp.zeros(starts_ref.shape, jnp.int32)

    experts, block = ids_ref.shape[0], picks_ref.shape[2]
    ids = ids_ref[...]
    names = [picks_ref[0, c : c + 1, :] == ids for c in (0, 1)]
    named = (names[0] | names[1]).astype(F32)
    earlier = lax.broadcasted_iota(jnp.int32, (block, block), 0) < lax.broadcasted_iota(
        jnp.int32, (block, block), 1
    )
    before = dot(named.astype(BF), earlier.astype(F32).astype(BF)) + carry[:, 0:1]
    spot = before + (lax.broadcasted_iota(jnp.int32, (experts, block), 0) * capacity).astype(F32)
    for c in (0, 1):
        found = jnp.sum(jnp.where(names[c], spot, 0.0), axis=0, keepdims=True).astype(jnp.int32)
        index_ref[0, c : c + 1, :] = jnp.where(picks_ref[0, 2 + c : 3 + c, :] > 0, found, -1)
    after = carry[...] + jnp.sum(named, axis=1, keepdims=True)
    carry[...] = after
    lane = lax.broadcasted_iota(jnp.int32, (experts, LANES), 1)
    starts_ref[...] = jnp.where(lane == step + 1, after.astype(jnp.int32), starts_ref[...])


def places(ids, picks, keep, capacity):
    count = picks.shape[0]
    blocks = count // BLOCK
    experts = ids.shape[0]
    turned = jnp.concatenate([picks, keep], axis=1).reshape(blocks, BLOCK, 4).transpose(0, 2, 1)
    return pl.pallas_call(
        functools.partial(place_kernel, capacity),
        grid=(blocks,),
        in_specs=[whole((experts, 1)), pl.BlockSpec((1, 4, BLOCK), lambda step: (step, 0, 0))],
        out_specs=[
            pl.BlockSpec((1, 2, BLOCK), lambda step: (step, 0, 0)), whole((experts, LANES)),
        ],
        out_shape=[
            jax.ShapeDtypeStruct((blocks, 2, BLOCK), jnp.int32),
            jax.ShapeDtypeStruct((experts, LANES), jnp.int32),
        ],
        scratch_shapes=[pltpu.VMEM((experts, LANES), F32)],
        compiler_params=params(),
        cost_estimate=cost(1e8, 1e5),
        name="places",
    )(ids[:, None], turned)


def window_rows(experts, capacity):
    return min(capacity, 1024 // experts)


def window_at(starts_ref, expert, step, turn, window, capacity):
    low = starts_ref[expert, step]
    begin = (low // 16) * 16 + turn * window
    at = pl.multiple_of(jnp.minimum(begin, capacity - window), 16)
    return begin, starts_ref[expert, step + 1], at


def turns(starts_ref, step, experts, window):
    most = 0
    for expert in experts:
        low = (starts_ref[expert, step] // 16) * 16
        most = jnp.maximum(most, (starts_ref[expert, step + 1] - low + window - 1) // window)
    return most


def dispatch_kernel(window, capacity, plan, sources, starts_ref, index_ref, *refs):
    src_refs, outs, (spots, got) = refs[:sources], refs[sources:-2], refs[-2:]
    owners = outs[0].shape[0]
    step = pl.program_id(0)
    named = [owners * part + owner for part, _ in plan for owner in range(owners)]

    @pl.when(step == 0)
    def _():
        for out in outs:
            out[...] = jnp.zeros(out.shape, out.dtype)

    place = lax.broadcasted_iota(jnp.int32, (window, index_ref.shape[2]), 0)
    first, second = index_ref[0, 0:1, :], index_ref[0, 1:2, :]

    def one_turn(turn, carry):
        for (part, used), out in zip(plan, outs):
            spans = []
            for owner in range(owners):
                expert = part * owners + owner
                begin, _, at = window_at(starts_ref, expert, step, turn, window, capacity)
                shift = expert * capacity
                near = jnp.where(first >= shift + begin, first - (shift + at), -1)
                far = jnp.where(second >= shift + begin, second - (shift + at), -1)
                hit = jnp.where((near >= 0) & (near < window), near, far)
                spots[window * owner : window * (owner + 1), :] = (
                    (place == hit).astype(F32).astype(BF)
                )
                spans.append(at)
            for order, which in enumerate(used):
                got[...] = dot(spots[...], src_refs[which][...])
                for owner, at in enumerate(spans):
                    rows = pl.ds(pl.multiple_of(at + order * capacity, 16), window)
                    held = out[owner, rows, :].astype(F32)
                    out[owner, rows, :] = (
                        held + got[window * owner : window * (owner + 1), :]
                    ).astype(BF)
        return carry

    lax.fori_loop(0, turns(starts_ref, step, named, window), one_turn, 0)


def dispatch(srcs, starts, index_rows, owners, capacity, plan):
    count, width = srcs[0].shape
    window = window_rows(starts.shape[0], capacity)
    shapes = [(owners, len(used) * capacity, width) for _, used in plan]
    return pl.pallas_call(
        functools.partial(dispatch_kernel, window, capacity, plan, len(srcs)),
        grid_spec=pltpu.PrefetchScalarGridSpec(
            num_scalar_prefetch=1,
            grid=(count // BLOCK,),
            in_specs=[pl.BlockSpec((1, 2, BLOCK), lambda step, *_: (step, 0, 0))]
            + [pl.BlockSpec((BLOCK, width), lambda step, *_: (step, 0))] * len(srcs),
            out_specs=[whole(shape) for shape in shapes],
            scratch_shapes=[
                pltpu.VMEM((owners * window, BLOCK), BF),
                pltpu.VMEM((owners * window, width), F32),
            ],
        ),
        out_shape=[jax.ShapeDtypeStruct(shape, BF) for shape in shapes],
        compiler_params=params(),
        cost_estimate=cost(6e9, 8e6),
        name="dispatch",
    )(starts, index_rows, *srcs)


def combine_block(window, step, me, starts_ref, index_ref, bufs, own_bufs, wins, acc):
    owners, capacity = bufs[0].shape[:2]
    experts = owners * len(bufs)
    lane = lax.broadcasted_iota(jnp.int32, (1, experts * window), 1)
    acc[...] = jnp.zeros(acc.shape, F32)

    def one_turn(turn, carry):
        seen = jnp.full((1, experts * window), -2, jnp.int32)
        for expert in range(experts):
            part, owner = expert // owners, expert % owners
            begin, high, at = window_at(starts_ref, expert, step, turn, window, capacity)
            slot = lane + (at - expert * window)
            fresh = (slot >= begin) & (slot < high)
            mine = (lane >= expert * window) & (lane < (expert + 1) * window)
            seen = jnp.where(mine & fresh, slot + expert * capacity, seen)
            to = slice(window * expert, window * (expert + 1))
            if own_bufs[part] is None:
                wins[to, :] = bufs[part][owner, pl.ds(at, window), :]
            else:
                wins[to, :] = jnp.where(
                    me == owner, own_bufs[part][0, pl.ds(at, window), :],
                    bufs[part][owner, pl.ds(at, window), :],
                )
        total = acc[...]
        for low in range(0, experts * window, CHUNK):
            part = slice(low, min(low + CHUNK, experts * window))
            hit = (index_ref[:, 0:1] == seen[:, part]) | (index_ref[:, 1:2] == seen[:, part])
            total = total + dot(hit.astype(F32).astype(BF), wins[part, :])
        acc[...] = total
        return carry

    lax.fori_loop(0, turns(starts_ref, step, range(experts), window), one_turn, 0)


def top_kernel(early, starts_ref, here_ref, index_ref, hidden_ref, head_ref, tail_ref, own_first_ref, own_second_ref, out_ref, first, second, wins, acc, sems):
    step = pl.program_id(0)
    experts = starts_ref.shape[0]
    window, capacity = wins.shape[0] // experts, first.shape[1]
    late = capacity - early

    @pl.when(step == 0)
    def _():
        copies = [
            pltpu.make_async_copy(head_ref.at[:, pl.ds(capacity, early), :], first.at[:, pl.ds(0, early), :], sems.at[0]),
            pltpu.make_async_copy(tail_ref.at[:, pl.ds(0, late), :], first.at[:, pl.ds(early, late), :], sems.at[1]),
            pltpu.make_async_copy(tail_ref.at[:, pl.ds(late, capacity), :], second, sems.at[2]),
        ]
        for copy in copies:
            copy.start()
        for copy in copies:
            copy.wait()
        me = pl.ds(here_ref[1], 1)
        copies = [
            pltpu.make_async_copy(own_first_ref.at[me], first.at[me, pl.ds(early, late), :], sems.at[3]),
            pltpu.make_async_copy(own_second_ref, second.at[me], sems.at[4]),
        ]
        for copy in copies:
            copy.start()
        for copy in copies:
            copy.wait()

    combine_block(window, step, 0, starts_ref, index_ref, [first, second], [None, None], wins, acc)
    out_ref[...] = (hidden_ref[...] + acc[...]).astype(BF)


def top(starts, here, index, hidden, head, tail, own_first, own_second, early, capacity):
    count, width = hidden.shape
    experts = starts.shape[0]
    window = window_rows(experts, capacity)
    row = lambda shape: pl.BlockSpec(shape, lambda step, *_: (step, 0))
    held = pltpu.VMEM((head.shape[0], capacity, width), BF)
    return pl.pallas_call(
        functools.partial(top_kernel, early),
        grid_spec=pltpu.PrefetchScalarGridSpec(
            num_scalar_prefetch=2,
            grid=(count // BLOCK,),
            in_specs=[row((BLOCK, 2)), row((BLOCK, width))] + [pl.BlockSpec(memory_space=pl.ANY)] * 4,
            out_specs=row((BLOCK, width)),
            scratch_shapes=[
                held, held, pltpu.VMEM((experts * window, width), BF),
                pltpu.VMEM((BLOCK, width), F32), pltpu.SemaphoreType.DMA((5,)),
            ],
        ),
        out_shape=jax.ShapeDtypeStruct((count, width), BF),
        compiler_params=params(),
        cost_estimate=cost(6e9, 12e6),
        name="top",
    )(starts, here, index, hidden, head, tail, own_first, own_second)


def gelu_parts(values):
    size = 1.0 + (0.3275911 * 0.7071067811865476) * jnp.abs(values)
    near = pl.reciprocal(size, approx=True)
    near = near * (2.0 - size * near)
    expo = jnp.exp2((-0.5 * 1.4426950408889634) * (values * values))
    poly = 0.5 * 1.061405429
    for term in (-1.453152027, 1.421413741, -0.284496736, 0.254829592):
        poly = poly * near + 0.5 * term
    tail = poly * near * expo
    share = jnp.where(values >= 0, 1.0 - tail, tail)
    return values * share, share + values * (0.3989422804014327 * expo)


def expert_kernel(
    experts, fcut, begun, part, joins, mine_ref, up_ref, down_ref, router_ref, back_ref, x_ref, dy_ref, *refs
):
    given, refs = refs[: 3 * begun], refs[3 * begun :]
    if joins:
        before_ref, refs = refs[0], refs[1:]
    *grad_refs, grouter_ref = refs[2:-5]
    acc_up, acc_down, acc_router, acc_out, acc_dx = refs[-5:]
    step = pl.program_id(0)
    hidden_units = up_ref.shape[1]
    _, capacity, width = x_ref.shape
    count = capacity

    @pl.when(step == 0)
    def _():
        if begun:
            acc_up[...] = given[0][...].astype(F32)
            acc_down[...] = given[1][...].astype(F32)
            acc_router[:, :LANES] = given[2][...]
            acc_router[:, LANES:] = jnp.zeros((width, LANES), F32)
        else:
            acc_up[...] = jnp.zeros(acc_up.shape, F32)
            acc_down[...] = jnp.zeros(acc_down.shape, F32)
            acc_router[...] = jnp.zeros(acc_router.shape, F32)

    rows = x_ref[...].reshape(count, width)
    logits = dot(rows, router_ref[...])
    logits = logits[:, :LANES] + logits[:, LANES:]
    lane = lax.broadcasted_iota(jnp.int32, (count, LANES), 1)
    logits = jnp.where(lane < experts, logits, -1e30)
    expo = jnp.exp(logits - jnp.max(logits, axis=-1, keepdims=True))
    gates = expo / jnp.sum(expo, axis=-1, keepdims=True)
    own = (lane == mine_ref[0]).astype(F32)
    chosen = jnp.sum(gates * own, axis=-1, keepdims=True)
    pair = (chosen * dy_ref[...].reshape(count, width).astype(F32)).astype(BF)
    rows_t = rows.T
    pair_t = pair.T
    chunks = [slice(low, low + fcut) for low in range(0, hidden_units, fcut)]
    ahead = lambda cols: (dot(rows, up_ref[:, cols]), dot_rt(pair, down_ref[cols, :]))
    ready = ahead(chunks[0])
    for turn, cols in enumerate(chunks):
        pre, grad_act = ready
        if turn + 1 < len(chunks):
            ready = ahead(chunks[turn + 1])
        act, slope = gelu_parts(pre)
        act = act.astype(BF)
        grad_pre = (grad_act * slope).astype(BF)
        acc_up[:, cols] += dot(rows_t, grad_pre)
        acc_down[:, cols] += dot(pair_t, act)
        if turn == 0:
            acc_out[...] = dot(act, down_ref[cols, :])
            acc_dx[...] = dot_rt(grad_pre, up_ref[:, cols])
        else:
            acc_out[...] += dot(act, down_ref[cols, :])
            acc_dx[...] += dot_rt(grad_pre, up_ref[:, cols])
    inner = jnp.sum(acc_out[...] * pair.astype(F32), axis=-1, keepdims=True)
    grad_logits = inner * (own - gates)
    head = grad_logits.astype(BF)
    rest = (grad_logits - head.astype(F32)).astype(BF)
    acc_router[...] += dot(rows_t, jnp.concatenate([head, rest], axis=1))
    out = (chosen * acc_out[...]).astype(BF)
    grad_rows = (acc_dx[...] + dot(jnp.concatenate([head, head], axis=1), back_ref[...])).astype(BF)
    if part:
        refs[0][0] = grad_rows
        late = refs[1].shape[1] - capacity
        if late:
            refs[1][0, :late, :] = before_ref[0]
        refs[1][0, late:, :] = out
    else:
        early = refs[0].shape[1] - capacity
        refs[0][0, :capacity, :] = grad_rows
        refs[0][0, capacity:, :] = out[:early]
        refs[1][0] = out[early:]

    @pl.when(step == pl.num_programs(0) - 1)
    def _():
        grouter_ref[...] = acc_router[:, :LANES] + acc_router[:, LANES:]
        if not begun:
            grad_refs[0][...] = acc_up[...].astype(BF)
            grad_refs[1][...] = acc_down[...].astype(BF)
            return
        grad_ref = grad_refs[0]
        shards, tall, _ = grad_ref.shape
        up_rows, down_rows = width // shards, hidden_units // shards
        piece = tall - up_rows
        for shard in range(shards):
            grad_ref[shard, :up_rows, :] = acc_up[up_rows * shard : up_rows * (shard + 1), :].astype(BF)
            turned = acc_down[:, down_rows * shard : down_rows * (shard + 1)].T.astype(BF)
            for part in range(down_rows // piece):
                grad_ref[shard, up_rows:, width * part : width * (part + 1)] = (
                    turned[piece * part : piece * (part + 1), :]
                )


def expert_pass(part, mine, rows, grads, weights, early, experts, capacity, shards, own, given, before, taken):
    (rows, rows_at), (grads, grads_at) = rows, grads
    w_up, w_down, router, router_back = weights
    sources, _, width = rows.shape
    units = w_up.shape[2]
    source = lambda step, mine_ref: (mine_ref[1] + (0 if own else 1) + step) % sources
    block = lambda tall, at: pl.BlockSpec(
        (1, tall, width), lambda step, mine_ref: (source(step, mine_ref), at, 0)
    )
    weight = lambda shape: pl.BlockSpec((None,) + shape[1:], lambda *_: (part, 0, 0))
    late = capacity - early
    talls = [capacity, late + capacity] if part else [capacity + early, late]
    sent = [jax.ShapeDtypeStruct((sources, tall, width), BF) for tall in talls]
    sent_specs = [block(tall, 0) for tall in talls]
    if part and own:
        sent = [jax.ShapeDtypeStruct((1, capacity, width), BF)] * 2
        sent_specs = [whole((1, capacity, width))] * 2
    if given:
        sums = [jax.ShapeDtypeStruct((shards, width // shards * 2, units), BF)]
    else:
        sums = [jax.ShapeDtypeStruct((width, units), BF)] * 2
    sums.append(jax.ShapeDtypeStruct((width, LANES), F32))
    steps = 1 if own else sources - 1
    joins = bool(part) and not own
    more = list(given) + ([before] if joins else [])
    more_specs = [whole(array.shape) for array in given] + ([block(late, 0)] if joins else [])
    skip = 7 + len(more)

    def body(*refs):
        expert_kernel(
            experts, min(FCUT, units), bool(given), part, joins, *refs[:skip], *refs[skip + len(taken) :]
        )

    return pl.pallas_call(
        body,
        grid_spec=pltpu.PrefetchScalarGridSpec(
            num_scalar_prefetch=1,
            grid=(steps,),
            in_specs=[
                weight(w_up.shape), weight(w_down.shape), whole(router.shape),
                whole(router_back.shape), block(capacity, rows_at), block(capacity, grads_at),
            ] + more_specs + [pl.BlockSpec(memory_space=pl.ANY)] * len(taken),
            out_specs=sent_specs + [whole(array.shape) for array in sums],
            scratch_shapes=[
                pltpu.VMEM((width, units), F32),
                pltpu.VMEM((width, units), F32),
                pltpu.VMEM((width, 2 * LANES), F32),
                pltpu.VMEM((capacity, width), F32),
                pltpu.VMEM((capacity, width), F32),
            ],
        ),
        out_shape=sent + sums,
        input_output_aliases={skip + at: to for at, to in enumerate(taken)},
        compiler_params=params(),
        cost_estimate=cost(
            20 * steps * capacity * width * units, 30e6, 2 * steps * capacity * units
        ),
        name="expert_own" if own else "expert_others",
    )(mine, *weights, rows, grads, *more, *taken.values())


def back_kernel(
    window, groups, starts_ref, here_ref, index_ref, hidden_ref, tok_ref, dy_ref, qkv_ref,
    probs_ref, mixed_ref, gain_one_ref, qkv_w_ref, proj_w_ref, gain_two_ref, *refs,
):
    bufs, own_bufs, router_refs = refs[:2], [None, refs[2]], refs[3:5]
    ghid_ref, dqkv_ref, own_ref, sent_ref = refs[5:-9]
    wins, acc, compact, padded, acc_qkv, acc_proj, acc_gain, dscores, dscores_low = refs[-9:]
    experts = starts_ref.shape[0]
    step = pl.program_id(0)
    width = tok_ref.shape[1]
    factor_qk = (width // HEADS) ** (-0.5)

    @pl.when(step == 0)
    def _():
        for ref in (acc_qkv, acc_proj, acc_gain):
            ref[...] = jnp.zeros(ref.shape, F32)

    combine_block(window, step, here_ref[1], starts_ref, index_ref, bufs, own_bufs, wins, acc)
    clear_gaps(padded)
    hat_two, scale_two = norm_parts(hidden_ref[...])
    grad_normed = acc[...]
    acc_gain[...] += jnp.sum(grad_normed * hat_two, axis=0, keepdims=True)
    grad_hidden = dy_ref[...].astype(F32) + norm_back(
        grad_normed, hat_two, scale_two, gain_two_ref[...]
    )
    ghid_ref[...] = grad_hidden
    compact[...] = grad_hidden
    spread_rows(compact, padded)
    grad_attn = padded[...].astype(BF)
    acc_proj[...] += dot_lt(mixed_ref[...], grad_attn)
    grad_mixed = dot_rt(grad_attn, proj_w_ref[...]).astype(BF)
    low = low_half()
    for pair in range(BLOCK_PAIRS):
        rows = slice(PAIR_PAD * pair, PAIR_PAD * (pair + 1))
        for two in range(width // LANES):
            cols = slice(LANES * two, LANES * (two + 1))
            key_cols = slice(width + LANES * two, width + LANES * (two + 1))
            value_cols = slice(2 * width + LANES * two, 2 * width + LANES * (two + 1))
            at = (pair * (width // LANES) + two) * 2 * PAIR_PAD
            dscores[at : at + 2 * PAIR_PAD, :] = dot_rt(
                two_heads(grad_mixed[rows, cols], low), qkv_ref[rows, value_cols]
            )
    for pair in range(BLOCK_PAIRS):
        each = 2 * PAIR_PAD * (width // LANES)
        part = slice(each * pair, each * (pair + 1))
        wide, grad_probs = probs_ref[part, :].astype(F32), dscores[part, :]
        meet = jnp.sum(wide * grad_probs, axis=-1, keepdims=True)
        dscores_low[part, :] = (wide * (grad_probs - meet) * factor_qk).astype(BF)
    for pair in range(BLOCK_PAIRS):
        rows = slice(PAIR_PAD * pair, PAIR_PAD * (pair + 1))
        for two in range(width // LANES):
            cols = slice(LANES * two, LANES * (two + 1))
            key_cols = slice(width + LANES * two, width + LANES * (two + 1))
            value_cols = slice(2 * width + LANES * two, 2 * width + LANES * (two + 1))
            at = (pair * (width // LANES) + two) * 2 * PAIR_PAD
            probs = probs_ref[at : at + 2 * PAIR_PAD, :]
            grad_out = two_heads(grad_mixed[rows, cols], low)
            grad_scores = dscores_low[at : at + 2 * PAIR_PAD, :]
            grad_query = one_row(dot(grad_scores, qkv_ref[rows, key_cols]), low)
            dqkv_ref[rows, cols] = grad_query.astype(BF)
            dqkv_ref[rows, key_cols] = dot_lt(
                grad_scores, two_heads(qkv_ref[rows, cols], low)
            ).astype(BF)
            dqkv_ref[rows, value_cols] = dot_lt(probs, grad_out).astype(BF)
    compact[...] = norm_parts(tok_ref[...].astype(F32))[0] * gain_one_ref[...]
    spread_rows(compact, padded)
    acc_qkv[...] += dot_lt(padded[...].astype(BF), dqkv_ref[...])

    @pl.when(step == pl.num_programs(0) - 1)
    def _():
        cores, sides, layers = groups
        half = acc_qkv.shape[0] * 4 // cores
        tall = half // (sides * layers)

        def piece(row):
            part, at = row // width, row % width
            if part < 3:
                return acc_qkv[at : at + tall, width * part : width * (part + 1)]
            return acc_proj[at : at + tall, :]

        for side in range(sides):
            for layer in range(layers):
                low = (side * layers + layer) * tall
                spot = (side ^ here_ref[1]) * layers + (layer ^ here_ref[2])
                to = pl.ds(pl.multiple_of(spot * tall, tall), tall)
                even, odd = piece(low), piece(half + low)
                own_ref[to, :] = jnp.where(here_ref[0] == 0, even, odd).astype(BF)
                sent_ref[to, :] = jnp.where(here_ref[0] == 0, odd, even).astype(BF)
        gain_one_sum = jnp.sum(acc_qkv[...] * qkv_w_ref[...].astype(F32), axis=-1, keepdims=True)
        lane = lax.broadcasted_iota(jnp.int32, (width, LANES), 1)
        router = sum(ref[...] for ref in router_refs)
        small = jnp.where(lane == experts, gain_one_sum, router).T[: own_ref.shape[0] - half, :]
        row = lax.broadcasted_iota(jnp.int32, small.shape, 0)
        small = jnp.where(row == experts + 1, acc_gain[...], small).astype(BF)
        own_ref[half:, :] = small
        sent_ref[half:, :] = small


def small_rows(experts):
    return 16 * -(-(experts + 2) // 16)


def back(starts, here, groups, index, hidden, tokens, dy, qkv, probs, mixed, gain_one, w_qkv, w_proj, gain_two, downs, own, routers, capacity):
    count, width = tokens.shape
    blocks = count // BLOCK
    experts = starts.shape[0]
    window = window_rows(experts, capacity)
    row = lambda shape: pl.BlockSpec(shape, lambda step, *_: (step, 0))
    cores, sides, layers = groups
    assert cores == 2
    sum_shape = (2 * width + small_rows(experts), width)
    flops = 2 * blocks * BLOCK_PAD * width * (8 * width + 10 * PAIR_PAD)
    return pl.pallas_call(
        functools.partial(back_kernel, window, groups),
        grid_spec=pltpu.PrefetchScalarGridSpec(
            num_scalar_prefetch=2,
            grid=(blocks,),
            in_specs=[
                row((BLOCK, 2)), row((BLOCK, width)), row((BLOCK, width)), row((BLOCK, width)),
                row((BLOCK_PAD, 3 * width)), row((probs.shape[0] // blocks, PAIR_PAD)),
                row((BLOCK_PAD, width)),
                whole((1, width)), whole(w_qkv.shape), whole(w_proj.shape), whole((1, width)),
            ] + [whole((downs[0].shape[0], capacity, width))] * 2 + [whole(own.shape)]
            + [whole((width, LANES))] * 2,
            out_specs=[
                row((BLOCK, width)), row((BLOCK_PAD, 3 * width)), whole(sum_shape), whole(sum_shape),
            ],
            scratch_shapes=[
                pltpu.VMEM((experts * window, width), BF),
                pltpu.VMEM((BLOCK, width), F32),
                pltpu.VMEM((BLOCK, width), F32),
                pltpu.VMEM((BLOCK_PAD, width), F32),
                pltpu.VMEM(w_qkv.shape, F32),
                pltpu.VMEM(w_proj.shape, F32),
                pltpu.VMEM((1, width), F32),
                pltpu.VMEM((probs.shape[0] // blocks, PAIR_PAD), F32),
                pltpu.VMEM((probs.shape[0] // blocks, PAIR_PAD), BF),
            ],
        ),
        out_shape=[
            jax.ShapeDtypeStruct((count, width), F32),
            jax.ShapeDtypeStruct(qkv.shape, BF),
            jax.ShapeDtypeStruct(sum_shape, BF),
            jax.ShapeDtypeStruct(sum_shape, BF),
        ],
        compiler_params=params(),
        cost_estimate=cost(1e12, 4000e6),
        name="back",
    )(
        starts, here, index, hidden, tokens, dy, qkv, probs, mixed, gain_one[None, :], w_qkv,
        w_proj, gain_two[None, :], *downs, own, *routers,
    )


def last_kernel(dqkv_ref, ghid_ref, tok_ref, gain_one_ref, qkv_w_ref, *refs):
    out_ref, compact, padded = refs[-3:]
    padded[...] = dot_rt(dqkv_ref[...], qkv_w_ref[...])
    gather_rows(padded, compact)
    hat_one, scale_one = norm_parts(tok_ref[...].astype(F32))
    out_ref[...] = ghid_ref[...] + norm_back(compact[...], hat_one, scale_one, gain_one_ref[...])


def last(low, high, so_far, dqkv, ghid, tokens, gain_one, w_qkv):
    count, width = tokens.shape
    row = lambda shape: pl.BlockSpec(shape, lambda step: (step + low, 0))
    taken = [] if so_far is None else [so_far]
    return pl.pallas_call(
        last_kernel,
        grid=(high - low,),
        in_specs=[
            row((BLOCK_PAD, 3 * width)), row((BLOCK, width)), row((BLOCK, width)),
            whole((1, width)), whole(w_qkv.shape),
        ] + [pl.BlockSpec(memory_space=pl.ANY)] * len(taken),
        out_specs=row((BLOCK, width)),
        out_shape=jax.ShapeDtypeStruct((count, width), F32),
        scratch_shapes=[pltpu.VMEM((BLOCK, width), F32), pltpu.VMEM((BLOCK_PAD, width), F32)],
        input_output_aliases={5: 0} if taken else {},
        compiler_params=params(),
        cost_estimate=cost(6 * BLOCK_PAD * (high - low) * width * width, 20e6),
        name="last",
    )(dqkv, ghid, tokens, gain_one[None, :], w_qkv, *taken)


def lay_kernel(groups, here_ref, own_ref, other_ref, qkv_ref, proj_ref):
    cores, sides, layers = groups
    tall, width = own_ref.shape[1:]
    each = width // tall
    for part in range(4):

        @pl.when(pl.program_id(0) == part)
        def _():
            for turn in range(each):
                core, spot = divmod(part * each + turn, sides * layers)
                side, layer = divmod(spot, layers)
                spot = (side ^ here_ref[1]) * layers + (layer ^ here_ref[2])
                piece = jnp.where(
                    core == here_ref[0], own_ref[spot].astype(F32), other_ref[spot].astype(F32)
                )
                (qkv_ref if part < 3 else proj_ref)[tall * turn : tall * (turn + 1), :] = piece


def lay(groups, here, own, other):
    width = own.shape[2]
    return pl.pallas_call(
        functools.partial(lay_kernel, groups),
        grid_spec=pltpu.PrefetchScalarGridSpec(
            num_scalar_prefetch=1,
            grid=(4,),
            in_specs=[whole(own.shape)] * 2,
            out_specs=[
                pl.BlockSpec((width, width), lambda step, *_: (0, jnp.minimum(step, 2))),
                whole((width, width)),
            ],
        ),
        out_shape=[
            jax.ShapeDtypeStruct((width, 3 * width), F32),
            jax.ShapeDtypeStruct((width, width), F32),
        ],
        compiler_params=params(),
        cost_estimate=cost(1e6, 8e6),
        name="lay",
    )(here, own, other)


def unpack_kernel(*refs):
    parts, (up_ref, down_ref) = refs[:-2], refs[-2:]
    tall, width = up_ref.shape[1], down_ref.shape[2]
    for which, part in enumerate(parts):
        up_ref[which] = part[:tall, :].astype(F32)
        for turn in range(down_ref.shape[1] // tall):
            down_ref[which, tall * turn : tall * (turn + 1), :] = (
                part[tall:, width * turn : width * (turn + 1)].astype(F32)
            )


def unpack(parts, width):
    tall, units = parts[0].shape[0] // 2, parts[0].shape[1]
    outs = [
        jax.ShapeDtypeStruct((len(parts), tall, units), F32),
        jax.ShapeDtypeStruct((len(parts), tall * units // width, width), F32),
    ]
    return pl.pallas_call(
        unpack_kernel,
        grid=(1,),
        in_specs=[whole(part.shape) for part in parts],
        out_specs=[whole(out.shape) for out in outs],
        out_shape=outs,
        compiler_params=params(),
        cost_estimate=cost(1e6, 4e6),
        name="unpack",
    )(*parts)


def jump(value, axis, far):
    size = lax.axis_size(axis)
    return lax.ppermute(value, axis, [(at, at ^ far) for at in range(size)])


def merge_kernel(cuts, extra, count, *refs):
    parts, outs = refs[:count], refs[count:]
    tall = (parts[0].shape[0] - extra) // cuts

    def total(rows):
        value = parts[0][rows, :].astype(F32)
        for part in parts[1:]:
            value = value + part[rows, :].astype(F32)
        return value

    small = total(slice(cuts * tall, None))
    for cut, out in enumerate(outs):
        if cut == cuts:
            out[...] = small
            continue
        out[:tall, :] = total(slice(cut * tall, (cut + 1) * tall)).astype(BF)
        if out.shape[0] > tall:
            out[tall:, :] = small.astype(BF)


def merge(parts, cuts, extra, ends):
    rows, width = parts[0].shape
    tall = (rows - extra) // cuts
    if ends:
        outs = [jax.ShapeDtypeStruct((tall, width), BF), jax.ShapeDtypeStruct((extra, width), F32)]
    else:
        outs = [jax.ShapeDtypeStruct((tall + extra, width), BF)] * cuts
    return pl.pallas_call(
        functools.partial(merge_kernel, cuts, extra, len(parts)),
        grid=(1,),
        in_specs=[whole((rows, width))] * len(parts),
        out_specs=[whole(out.shape) for out in outs],
        out_shape=outs,
        compiler_params=params(),
        cost_estimate=cost(1e6, 4e6),
        name="merge",
    )(*parts)


def after(value, *others):
    return lax.optimization_barrier((value, *others))[0]


def sum_over_all(own, sent, groups, extra, arrived, beside):
    cores, sides, layers = groups
    beside = iter(beside)

    def spread(own, sent, axis, scale):
        came = [jump(part, axis, scale * far) for far, part in enumerate(sent, 1)]
        return [own] + list(after(tuple(came), next(beside)(own)))

    half = merge([own, jump(sent, "dp", 1)], sides, extra, False)
    half = list(after(tuple(half), arrived))
    flat = merge(spread(half[0], half[1:], "expert", 1), layers, extra, False)
    spot, small = merge(spread(flat[0], flat[1:], "dp", cores), 1, extra, True)
    flat = jnp.stack(spread(spot, [spot] * (layers - 1), "dp", cores))
    half = jnp.stack(spread(flat, [flat] * (sides - 1), "expert", 1))
    half = half.reshape(sides * layers, *spot.shape)
    return half, jump(half, "dp", 1), small


def per_device(
    tokens, gain_one, w_qkv, w_proj, gain_two, w_router, w_in, w_eout, picks, keep, grad_out
):
    count, width = tokens.shape
    local = w_in.shape[0]
    assert local == 2
    owners = lax.axis_size("expert")
    shards = lax.axis_size("dp")
    experts = local * owners
    capacity = 8 * ((21 * count + 80 * experts - 1) // (80 * experts))
    me, row = lax.axis_index("expert"), lax.axis_index("dp")
    cores = 2
    groups = (cores, owners, shards // cores)
    here = jnp.stack([row % cores, me, row // cores]).astype(jnp.int32)
    ids = jnp.arange(experts, dtype=jnp.int32).reshape(owners, local).T.reshape(-1)

    def swap(sent):
        return lax.all_to_all(sent, "expert", split_axis=0, concat_axis=0, tiled=True)

    index_rows, starts = places(ids, picks, keep, capacity)
    send = lambda srcs, *plan: dispatch(srcs, starts, index_rows, owners, capacity, plan)
    (dy_first,) = send([grad_out], (0, (0,)))
    got = swap(dy_first)
    hidden, rows, qkv, probs, mixed = attend(
        after(tokens, dy_first), gain_one, w_qkv, w_proj, gain_two
    )
    (x_first,) = send([rows], (0, (0,)))
    arrived = [[(swap(after(x_first, got)), 0), (got, 0)]]
    kept = [[(x_first, 0), (dy_first, 0)]]
    others = send([after(rows, x_first), grad_out], *[(part, (0, 1)) for part in range(1, local)])
    for sent in others:
        got = swap(after(sent, arrived[-1][0][0]))
        arrived.append([(got, 0), (got, 1)])
        kept.append([(sent, 0), (sent, 1)])
    index = index_rows.transpose(0, 2, 1).reshape(count, 2)
    head = w_router.astype(BF)
    rest = (w_router - head.astype(F32)).astype(BF)
    gap = ((0, 0), (0, LANES - experts))
    router = jnp.concatenate([jnp.pad(head, gap), jnp.pad(rest, gap)], axis=1)
    router_back = jnp.concatenate([jnp.pad(head, gap).T, jnp.pad(rest, gap).T], axis=0)
    early = 16 * (capacity // 32)
    weights = (w_in, w_eout, router, router_back)

    def one(part, own, given, before, *taken):
        mine = jnp.stack([me * local + part, me]).astype(jnp.int32)
        came = (kept if own else arrived)[part]
        taken = dict(zip(range(2 - len(taken), 2), taken))
        return expert_pass(
            part, mine, *came, weights, early, experts, capacity, shards, own, given, before, taken
        )

    def reduce(grad):
        grad = grad.reshape(shards * grad.shape[1], grad.shape[2])
        return lax.psum_scatter(grad, "dp", scatter_dimension=0, tiled=True)

    head, tail, *given = one(0, True, [], None)
    head, tail, grad, router_first = one(0, False, given, None, head, tail)
    sums, tail_first = [reduce(grad)], tail
    head = swap(after(head, got))
    down, tail, *given = one(1, False, [], tail_first)
    down = swap(after(down, head))
    own_down, own_out, grad, router_second = one(1, True, given, None)
    sums.append(reduce(grad))
    tail = swap(after(tail, down))
    grad_hidden, dqkv, own, sent = back(
        starts, here, groups, index, hidden, tokens, grad_out, qkv, probs, mixed, gain_one,
        w_qkv, w_proj, gain_two, [head, down], own_down, [router_first, router_second], capacity,
    )
    blocks = count // BLOCK
    some = blocks // 3

    def make_top(tie):
        return top(
            starts, here, index, after(hidden, tie), head, tail, tail_first, own_out, early, capacity
        )

    def make_unpack(tie):
        return unpack(after(tuple(sums), tie), width)

    def make_last(low, high, tie, so_far=None):
        return last(
            low, high, so_far, after(dqkv, tie), grad_hidden, tokens, gain_one, w_qkv
        )

    made = {}

    def beside(name, work):
        def go(tie):
            made[name] = work(tie)
            return jax.tree.leaves(made[name])[0]

        return go

    own, other, small = sum_over_all(
        own, sent, groups, small_rows(experts), tail,
        [
            beside("top", make_top),
            beside("unpack", make_unpack),
            beside("some", lambda tie: make_last(0, some, tie)),
            beside("last", lambda tie: make_last(some, blocks, tie, made["some"])),
        ],
    )
    block_out, grad_tokens, (grad_in, grad_eout) = made["top"], made["last"], made["unpack"]
    grad_qkv, grad_proj = lay(groups, here, own, other)
    return (
        block_out,
        grad_tokens,
        small[experts] / gain_one,
        grad_qkv,
        grad_proj,
        small[experts + 1],
        small[:experts].T,
        grad_in,
        grad_eout,
    )


def solution(mesh):
    rows = P(("dp", "expert"), None)
    experts = P("expert", None, None)
    return jax.shard_map(
        per_device,
        mesh=mesh,
        in_specs=(rows, P(), P(), P(), P(), P(), experts, experts, rows, rows, rows),
        out_specs=(
            rows, rows, P(), P(), P(), P(), P(), P("expert", "dp", None), P("expert", "dp", None),
        ),
        check_vma=False,
    )
```

```python
import functools

import jax
import jax.numpy as jnp
from jax import lax
from jax.experimental import pallas as pl
from jax.experimental.pallas import tpu as pltpu
from jax.sharding import PartitionSpec as P

HEADS = 8
PATCHES = 49
LANES = 128
PAIR = 2 * PATCHES
PAIR_PAD = 112
BLOCK_PAIRS = 4
BLOCK = BLOCK_PAIRS * PAIR
BLOCK_PAD = BLOCK_PAIRS * PAIR_PAD
BF = jnp.bfloat16
F32 = jnp.float32
VMEM_BYTES = 62 * 1024 * 1024
FCUT = 256
CHUNK = 256
TOP_SUBS, SEND_SUBS, LAST_SUBS = 2, 2, 2


def params():
    return pltpu.CompilerParams(
        dimension_semantics=("arbitrary",), vmem_limit_bytes=VMEM_BYTES
    )


def cost(flops, moved, special=0):
    return pl.CostEstimate(
        flops=int(flops), bytes_accessed=int(moved), transcendentals=int(special)
    )


def step_blocks(blocks, most):
    return max(n for n in range(1, most + 1) if blocks % n == 0)


def whole(shape):
    return pl.BlockSpec(shape, lambda *_: (0,) * len(shape))


def dot(left, right):
    return jnp.dot(left, right, preferred_element_type=F32)


def dot_rt(left, right):
    return lax.dot_general(left, right, (((1,), (1,)), ((), ())), preferred_element_type=F32)


def dot_lt(left, right):
    return lax.dot_general(left, right, (((0,), (0,)), ((), ())), preferred_element_type=F32)


def norm_parts(values):
    mean = jnp.mean(values, axis=-1, keepdims=True)
    cent = values - mean
    factor = lax.rsqrt(jnp.mean(cent * cent, axis=-1, keepdims=True) + 1e-06)
    return cent * factor, factor


def norm_back(grad_normed, normed_hat, factor, gain):
    grad_hat = grad_normed * gain
    inner = grad_hat - jnp.mean(grad_hat, axis=-1, keepdims=True)
    inner = inner - normed_hat * jnp.mean(grad_hat * normed_hat, axis=-1, keepdims=True)
    return factor * inner


def spread_rows(compact, padded):
    for pair in range(BLOCK_PAIRS):
        padded[PAIR_PAD * pair : PAIR_PAD * pair + PAIR] = compact[PAIR * pair : PAIR * pair + PAIR]


def gather_rows(padded, compact):
    for pair in range(BLOCK_PAIRS):
        compact[PAIR * pair : PAIR * pair + PAIR] = padded[PAIR_PAD * pair : PAIR_PAD * pair + PAIR]


def clear_gaps(padded):
    for pair in range(BLOCK_PAIRS):
        low = PAIR_PAD * pair + PAIR
        padded[low : low + PAIR_PAD - PAIR] = jnp.zeros((PAIR_PAD - PAIR, padded.shape[1]), F32)


def image_of(position):
    return (position >= PATCHES).astype(jnp.int32) + (position >= PAIR).astype(jnp.int32)


def same_image():
    rows = lax.broadcasted_iota(jnp.int32, (2 * PAIR_PAD, PAIR_PAD), 0)
    rows = jnp.where(rows >= PAIR_PAD, rows - PAIR_PAD, rows)
    cols = lax.broadcasted_iota(jnp.int32, (2 * PAIR_PAD, PAIR_PAD), 1)
    return image_of(rows) == image_of(cols)


def low_half():
    return lax.broadcasted_iota(jnp.int32, (PAIR_PAD, LANES), 1) < LANES // 2


def two_heads(values, low):
    zero = jnp.zeros_like(values)
    return jnp.concatenate([jnp.where(low, values, zero), jnp.where(low, zero, values)], axis=0)


def one_row(values, low):
    return jnp.where(low, values[:PAIR_PAD], values[PAIR_PAD:])


def attend_kernel(
    tok_ref, gain_one_ref, qkv_w_ref, proj_w_ref, gain_two_ref,
    hidden_ref, rows_ref, qkv_ref, probs_ref, mixed_ref,
    compact, padded, scores,
):
    width = tok_ref.shape[1]
    factor_qk = (width // HEADS) ** (-0.5)
    clear_gaps(padded)
    inputs = tok_ref[...].astype(F32)
    compact[...] = norm_parts(inputs)[0] * gain_one_ref[...]
    spread_rows(compact, padded)
    qkv_ref[...] = dot(padded[...].astype(BF), qkv_w_ref[...]).astype(BF)
    valid = same_image()
    low = low_half()
    for pair in range(BLOCK_PAIRS):
        rows = slice(PAIR_PAD * pair, PAIR_PAD * (pair + 1))
        for two in range(width // LANES):
            cols = slice(LANES * two, LANES * (two + 1))
            query = qkv_ref[rows, cols]
            keys = qkv_ref[rows, width + LANES * two : width + LANES * (two + 1)]
            step = (pair * (width // LANES) + two) * 2 * PAIR_PAD
            scores[step : step + 2 * PAIR_PAD, :] = jnp.where(
                valid, dot_rt(two_heads(query, low), keys), -1e30
            )
    for pair in range(BLOCK_PAIRS):
        each = 2 * PAIR_PAD * (width // LANES)
        part = slice(each * pair, each * (pair + 1))
        logits = scores[part, :]
        highest = jnp.max(logits, axis=-1, keepdims=True)
        expo = jnp.exp((logits - highest) * factor_qk)
        probs_ref[part, :] = (expo / jnp.sum(expo, axis=-1, keepdims=True)).astype(BF)
    for pair in range(BLOCK_PAIRS):
        rows = slice(PAIR_PAD * pair, PAIR_PAD * (pair + 1))
        for two in range(width // LANES):
            cols = slice(LANES * two, LANES * (two + 1))
            values = qkv_ref[rows, 2 * width + LANES * two : 2 * width + LANES * (two + 1)]
            step = (pair * (width // LANES) + two) * 2 * PAIR_PAD
            probs = probs_ref[step : step + 2 * PAIR_PAD, :]
            mixed_ref[rows, cols] = one_row(dot(probs, values), low).astype(BF)
    padded[...] = dot(mixed_ref[...], proj_w_ref[...])
    gather_rows(padded, compact)
    hidden = inputs + compact[...]
    hidden_ref[...] = hidden
    rows_ref[...] = (norm_parts(hidden)[0] * gain_two_ref[...]).astype(BF)


def attend(tokens, gain_one, w_qkv, w_proj, gain_two):
    count, width = tokens.shape
    blocks = count // BLOCK
    prob_rows = BLOCK_PAIRS * (width // LANES) * 2 * PAIR_PAD
    row = lambda shape: pl.BlockSpec(shape, lambda step: (step, 0))
    flops = 2 * blocks * BLOCK_PAD * width * (4 * width + 4 * PAIR_PAD)
    return pl.pallas_call(
        attend_kernel,
        grid=(blocks,),
        in_specs=[
            row((BLOCK, width)), whole((1, width)), whole(w_qkv.shape), whole(w_proj.shape),
            whole((1, width)),
        ],
        out_specs=[
            row((BLOCK, width)), row((BLOCK, width)), row((BLOCK_PAD, 3 * width)),
            row((prob_rows, PAIR_PAD)), row((BLOCK_PAD, width)),
        ],
        out_shape=[
            jax.ShapeDtypeStruct((count, width), F32),
            jax.ShapeDtypeStruct((count, width), BF),
            jax.ShapeDtypeStruct((blocks * BLOCK_PAD, 3 * width), BF),
            jax.ShapeDtypeStruct((blocks * prob_rows, PAIR_PAD), BF),
            jax.ShapeDtypeStruct((blocks * BLOCK_PAD, width), BF),
        ],
        scratch_shapes=[
            pltpu.VMEM((BLOCK, width), F32), pltpu.VMEM((BLOCK_PAD, width), F32),
            pltpu.VMEM((prob_rows, PAIR_PAD), F32),
        ],
        compiler_params=params(),
        cost_estimate=cost(flops, 30e6, blocks * prob_rows * LANES),
        name="attend",
    )(tokens, gain_one[None, :], w_qkv, w_proj, gain_two[None, :])


def place_kernel(local, capacity, picks_ref, keep_ref, index_ref, starts_ref):
    blocks, _, block = index_ref.shape
    experts = starts_ref.shape[0]
    owners = experts // local
    row = lax.broadcasted_iota(jnp.int32, (experts, block), 0)
    ids = row * local
    for part in range(1, local):
        ids = jnp.where(row >= owners * part, (row - owners * part) * local + part, ids)
    earlier = lax.broadcasted_iota(jnp.int32, (block, block), 0) < lax.broadcasted_iota(
        jnp.int32, (block, block), 1
    )
    earlier = earlier.astype(F32).astype(BF)
    base = (row * capacity).astype(F32)
    lane = lax.broadcasted_iota(jnp.int32, (experts, LANES), 1)
    starts = jnp.zeros((experts, LANES), jnp.int32)
    carry = jnp.zeros((experts, 1), F32)
    for step in range(blocks):
        cols = slice(block * step, block * (step + 1))
        names = [picks_ref[c : c + 1, cols] == ids for c in (0, 1)]
        named = (names[0] | names[1]).astype(F32)
        spot = base + (dot(named.astype(BF), earlier) + carry)
        for c in (0, 1):
            found = jnp.sum(jnp.where(names[c], spot, 0.0), axis=0, keepdims=True)
            index_ref[step, c : c + 1, :] = jnp.where(
                keep_ref[c : c + 1, cols] > 0, found.astype(jnp.int32), -1
            )
        carry = carry + jnp.sum(named, axis=1, keepdims=True)
        starts = jnp.where(lane == step + 1, carry.astype(jnp.int32), starts)
    starts_ref[...] = starts


def places(picks, keep, experts, local, capacity):
    count = picks.shape[0]
    outs = [
        jax.ShapeDtypeStruct((count // BLOCK, 2, BLOCK), jnp.int32),
        jax.ShapeDtypeStruct((experts, LANES), jnp.int32),
    ]
    return pl.pallas_call(
        functools.partial(place_kernel, local, capacity),
        grid=(1,),
        in_specs=[whole((2, count))] * 2,
        out_specs=[whole(out.shape) for out in outs],
        out_shape=outs,
        compiler_params=params(),
        cost_estimate=cost(1e8, 1e5),
        name="places",
    )(picks.T, keep.T)


def window_rows(experts, capacity):
    return min(capacity, 1024 // experts)


def window_at(starts_ref, expert, step, turn, window, capacity):
    low = starts_ref[expert, step]
    begin = (low // 16) * 16 + turn * window
    at = pl.multiple_of(jnp.minimum(begin, capacity - window), 16)
    return begin, starts_ref[expert, step + 1], at


def turns(starts_ref, step, experts, window):
    most = 0
    for expert in experts:
        low = (starts_ref[expert, step] // 16) * 16
        most = jnp.maximum(most, (starts_ref[expert, step + 1] - low + window - 1) // window)
    return most


def dispatch_kernel(window, capacity, plan, sources, starts_ref, index_ref, *refs):
    src_refs, outs, (spots, got) = refs[:sources], refs[sources:-2], refs[-2:]
    owners = outs[0].shape[0]
    named = [owners * part + owner for part, _ in plan for owner in range(owners)]
    subs = index_ref.shape[0]

    @pl.when(pl.program_id(0) == 0)
    def _():
        for out in outs:
            out[...] = jnp.zeros(out.shape, out.dtype)

    place = lax.broadcasted_iota(jnp.int32, (window, index_ref.shape[2]), 0)
    for sub in range(subs):
        step = pl.program_id(0) * subs + sub
        block = slice(BLOCK * sub, BLOCK * (sub + 1))
        first, second = index_ref[sub, 0:1, :], index_ref[sub, 1:2, :]

        def one_turn(turn, carry):
            for (part, used), out in zip(plan, outs):
                spans = []
                for owner in range(owners):
                    expert = part * owners + owner
                    begin, _, at = window_at(starts_ref, expert, step, turn, window, capacity)
                    shift = expert * capacity
                    near = jnp.where(first >= shift + begin, first - (shift + at), -1)
                    far = jnp.where(second >= shift + begin, second - (shift + at), -1)
                    hit = jnp.where((near >= 0) & (near < window), near, far)
                    spots[window * owner : window * (owner + 1), :] = (
                        (place == hit).astype(F32).astype(BF)
                    )
                    spans.append(at)
                for order, which in enumerate(used):
                    got[...] = dot(spots[...], src_refs[which][block, :])
                    for owner, at in enumerate(spans):
                        rows = pl.ds(pl.multiple_of(at + order * capacity, 16), window)
                        held = out[owner, rows, :].astype(F32)
                        out[owner, rows, :] = (
                            held + got[window * owner : window * (owner + 1), :]
                        ).astype(BF)
            return carry

        lax.fori_loop(0, turns(starts_ref, step, named, window), one_turn, 0)


def dispatch(srcs, starts, index_rows, owners, capacity, plan):
    count, width = srcs[0].shape
    subs = step_blocks(count // BLOCK, SEND_SUBS)
    window = window_rows(starts.shape[0], capacity)
    shapes = [(owners, len(used) * capacity, width) for _, used in plan]
    return pl.pallas_call(
        functools.partial(dispatch_kernel, window, capacity, plan, len(srcs)),
        grid_spec=pltpu.PrefetchScalarGridSpec(
            num_scalar_prefetch=1,
            grid=(count // BLOCK // subs,),
            in_specs=[pl.BlockSpec((subs, 2, BLOCK), lambda step, *_: (step, 0, 0))]
            + [pl.BlockSpec((BLOCK * subs, width), lambda step, *_: (step, 0))] * len(srcs),
            out_specs=[whole(shape) for shape in shapes],
            scratch_shapes=[
                pltpu.VMEM((owners * window, BLOCK), BF),
                pltpu.VMEM((owners * window, width), F32),
            ],
        ),
        out_shape=[jax.ShapeDtypeStruct(shape, BF) for shape in shapes],
        compiler_params=params(),
        cost_estimate=cost(6e9, 8e6),
        name="dispatch",
    )(starts, index_rows, *srcs)


def combine_block(window, step, me, starts_ref, index, bufs, own_bufs, wins, acc):
    owners, capacity = bufs[0].shape[:2]
    experts = owners * len(bufs)
    lane = lax.broadcasted_iota(jnp.int32, (1, experts * window), 1)
    acc[...] = jnp.zeros(acc.shape, F32)

    def one_turn(turn, carry):
        seen = jnp.full((1, experts * window), -2, jnp.int32)
        for expert in range(experts):
            part, owner = expert // owners, expert % owners
            begin, high, at = window_at(starts_ref, expert, step, turn, window, capacity)
            slot = lane + (at - expert * window)
            fresh = (slot >= begin) & (slot < high)
            mine = (lane >= expert * window) & (lane < (expert + 1) * window)
            seen = jnp.where(mine & fresh, slot + expert * capacity, seen)
            to = slice(window * expert, window * (expert + 1))
            if own_bufs[part] is None:
                wins[to, :] = bufs[part][owner, pl.ds(at, window), :]
            else:
                wins[to, :] = jnp.where(
                    me == owner, own_bufs[part][0, pl.ds(at, window), :],
                    bufs[part][owner, pl.ds(at, window), :],
                )
        total = acc[...]
        for low in range(0, experts * window, CHUNK):
            part = slice(low, min(low + CHUNK, experts * window))
            hit = (index[:, 0:1] == seen[:, part]) | (index[:, 1:2] == seen[:, part])
            total = total + dot(hit.astype(F32).astype(BF), wins[part, :])
        acc[...] = total
        return carry

    lax.fori_loop(0, turns(starts_ref, step, range(experts), window), one_turn, 0)


def top_kernel(early, starts_ref, here_ref, index_ref, hidden_ref, head_ref, tail_ref, own_first_ref, own_second_ref, out_ref, first, second, wins, acc, sems):
    step = pl.program_id(0)
    experts = starts_ref.shape[0]
    window, capacity = wins.shape[0] // experts, first.shape[1]
    late = capacity - early

    @pl.when(step == 0)
    def _():
        me, owners = here_ref[1], first.shape[0]

        def move(go):
            go(pltpu.make_async_copy(
                head_ref.at[:, pl.ds(capacity, early), :], first.at[:, pl.ds(0, early), :], sems.at[0]
            ))
            for owner in range(owners):
                to_first = first.at[owner, pl.ds(early, late), :]
                one, two = sems.at[1 + owner], sems.at[1 + owners + owner]

                @pl.when(me == owner)
                def _():
                    go(pltpu.make_async_copy(own_first_ref.at[owner], to_first, one))
                    go(pltpu.make_async_copy(own_second_ref.at[0], second.at[owner], two))

                @pl.when(me != owner)
                def _():
                    go(pltpu.make_async_copy(tail_ref.at[owner, pl.ds(0, late), :], to_first, one))
                    go(pltpu.make_async_copy(
                        tail_ref.at[owner, pl.ds(late, capacity), :], second.at[owner], two
                    ))

        move(lambda copy: copy.start())
        move(lambda copy: copy.wait())

    subs = hidden_ref.shape[0] // BLOCK
    for sub in range(subs):
        rows = slice(BLOCK * sub, BLOCK * (sub + 1))
        combine_block(
            window, step * subs + sub, 0, starts_ref, index_ref[rows, :], [first, second],
            [None, None], wins, acc,
        )
        out_ref[rows, :] = (hidden_ref[rows, :] + acc[...]).astype(BF)


def top(starts, here, index, hidden, head, tail, own_first, own_second, early, capacity):
    count, width = hidden.shape
    experts = starts.shape[0]
    window = window_rows(experts, capacity)
    row = lambda shape: pl.BlockSpec(shape, lambda step, *_: (step, 0))
    tall = BLOCK * step_blocks(count // BLOCK, TOP_SUBS)
    held = pltpu.VMEM((head.shape[0], capacity, width), BF)
    return pl.pallas_call(
        functools.partial(top_kernel, early),
        grid_spec=pltpu.PrefetchScalarGridSpec(
            num_scalar_prefetch=2,
            grid=(count // tall,),
            in_specs=[row((tall, 2)), row((tall, width))] + [pl.BlockSpec(memory_space=pl.ANY)] * 4,
            out_specs=pl.BlockSpec((tall, width), lambda step, *_: (step, 0)),
            scratch_shapes=[
                held, held, pltpu.VMEM((experts * window, width), BF),
                pltpu.VMEM((BLOCK, width), F32), pltpu.SemaphoreType.DMA((1 + 2 * head.shape[0],)),
            ],
        ),
        out_shape=jax.ShapeDtypeStruct((count, width), BF),
        compiler_params=params(),
        cost_estimate=cost(6e9, 12e6),
        name="top",
    )(starts, here, index, hidden, head, tail, own_first, own_second)


def gelu_parts(values):
    size = 1.0 + (0.3275911 * 0.7071067811865476) * jnp.abs(values)
    near = pl.reciprocal(size, approx=True)
    near = near * (2.0 - size * near)
    expo = jnp.exp2((-0.5 * 1.4426950408889634) * (values * values))
    poly = 0.5 * 1.061405429
    for term in (-1.453152027, 1.421413741, -0.284496736, 0.254829592):
        poly = poly * near + 0.5 * term
    tail = poly * near * expo
    share = jnp.where(values >= 0, 1.0 - tail, tail)
    return values * share, share + values * (0.3989422804014327 * expo)


def expert_kernel(
    experts, fcut, begun, part, joins, mine_ref, up_ref, down_ref, router_ref, back_ref, x_ref, dy_ref, *refs
):
    given, refs = refs[: 3 * begun], refs[3 * begun :]
    if joins:
        before_ref, refs = refs[0], refs[1:]
    *grad_refs, grouter_ref = refs[2:-5]
    acc_up, acc_down, acc_router, acc_out, acc_dx = refs[-5:]
    step = pl.program_id(0)
    hidden_units = up_ref.shape[1]
    _, capacity, width = x_ref.shape
    count = capacity

    @pl.when(step == 0)
    def _():
        if begun:
            acc_up[...] = given[0][...].astype(F32)
            acc_down[...] = given[1][...].astype(F32)
            acc_router[:, :LANES] = given[2][...]
            acc_router[:, LANES:] = jnp.zeros((width, LANES), F32)
        else:
            acc_up[...] = jnp.zeros(acc_up.shape, F32)
            acc_down[...] = jnp.zeros(acc_down.shape, F32)
            acc_router[...] = jnp.zeros(acc_router.shape, F32)

    rows = x_ref[...].reshape(count, width)
    logits = dot(rows, router_ref[...])
    logits = logits[:, :LANES] + logits[:, LANES:]
    lane = lax.broadcasted_iota(jnp.int32, (count, LANES), 1)
    logits = jnp.where(lane < experts, logits, -1e30)
    expo = jnp.exp(logits - jnp.max(logits, axis=-1, keepdims=True))
    gates = expo / jnp.sum(expo, axis=-1, keepdims=True)
    own = (lane == mine_ref[0]).astype(F32)
    chosen = jnp.sum(gates * own, axis=-1, keepdims=True)
    pair = (chosen * dy_ref[...].reshape(count, width).astype(F32)).astype(BF)
    rows_t = rows.T
    pair_t = pair.T
    chunks = [slice(low, low + fcut) for low in range(0, hidden_units, fcut)]
    ahead = lambda cols: (dot(rows, up_ref[:, cols]), dot_rt(pair, down_ref[cols, :]))
    ready = ahead(chunks[0])
    for turn, cols in enumerate(chunks):
        pre, grad_act = ready
        if turn + 1 < len(chunks):
            ready = ahead(chunks[turn + 1])
        act, slope = gelu_parts(pre)
        act = act.astype(BF)
        grad_pre = (grad_act * slope).astype(BF)
        acc_up[:, cols] += dot(rows_t, grad_pre)
        acc_down[:, cols] += dot(pair_t, act)
        if turn == 0:
            acc_out[...] = dot(act, down_ref[cols, :])
            acc_dx[...] = dot_rt(grad_pre, up_ref[:, cols])
        else:
            acc_out[...] += dot(act, down_ref[cols, :])
            acc_dx[...] += dot_rt(grad_pre, up_ref[:, cols])
    inner = jnp.sum(acc_out[...] * pair.astype(F32), axis=-1, keepdims=True)
    grad_logits = inner * (own - gates)
    head = grad_logits.astype(BF)
    rest = (grad_logits - head.astype(F32)).astype(BF)
    acc_router[...] += dot(rows_t, jnp.concatenate([head, rest], axis=1))
    out = (chosen * acc_out[...]).astype(BF)
    grad_rows = (acc_dx[...] + dot(jnp.concatenate([head, head], axis=1), back_ref[...])).astype(BF)
    if part:
        refs[0][0] = grad_rows
        late = refs[1].shape[1] - capacity
        if late:
            refs[1][0, :late, :] = before_ref[0]
        refs[1][0, late:, :] = out
    else:
        early = refs[0].shape[1] - capacity
        refs[0][0, :capacity, :] = grad_rows
        refs[0][0, capacity:, :] = out[:early]
        refs[1][0] = out[early:]

    @pl.when(step == pl.num_programs(0) - 1)
    def _():
        grouter_ref[...] = acc_router[:, :LANES] + acc_router[:, LANES:]
        if not begun:
            grad_refs[0][...] = acc_up[...].astype(BF)
            grad_refs[1][...] = acc_down[...].astype(BF)
            return
        grad_ref = grad_refs[0]
        shards, tall, _ = grad_ref.shape
        up_rows, down_rows = width // shards, hidden_units // shards
        piece = tall - up_rows
        for shard in range(shards):
            grad_ref[shard, :up_rows, :] = acc_up[up_rows * shard : up_rows * (shard + 1), :].astype(BF)
            turned = acc_down[:, down_rows * shard : down_rows * (shard + 1)].T.astype(BF)
            for part in range(down_rows // piece):
                grad_ref[shard, up_rows:, width * part : width * (part + 1)] = (
                    turned[piece * part : piece * (part + 1), :]
                )


def expert_pass(part, mine, rows, grads, weights, early, experts, capacity, shards, own, given, before, taken):
    (rows, rows_at), (grads, grads_at) = rows, grads
    w_up, w_down, router, router_back = weights
    sources, _, width = rows.shape
    units = w_up.shape[2]
    source = lambda step, mine_ref: (mine_ref[1] + (0 if own else 1) + step) % sources
    block = lambda tall, at: pl.BlockSpec(
        (1, tall, width), lambda step, mine_ref: (source(step, mine_ref), at, 0)
    )
    weight = lambda shape: pl.BlockSpec((None,) + shape[1:], lambda *_: (part, 0, 0))
    late = capacity - early
    talls = [capacity, late + capacity] if part else [capacity + early, late]
    sent = [jax.ShapeDtypeStruct((sources, tall, width), BF) for tall in talls]
    sent_specs = [block(tall, 0) for tall in talls]
    if part and own:
        sent = [jax.ShapeDtypeStruct((1, capacity, width), BF)] * 2
        sent_specs = [whole((1, capacity, width))] * 2
    if given:
        sums = [jax.ShapeDtypeStruct((shards, width // shards * 2, units), BF)]
    else:
        sums = [jax.ShapeDtypeStruct((width, units), BF)] * 2
    sums.append(jax.ShapeDtypeStruct((width, LANES), F32))
    steps = 1 if own else sources - 1
    joins = bool(part) and not own
    more = list(given) + ([before] if joins else [])
    more_specs = [whole(array.shape) for array in given] + ([block(late, 0)] if joins else [])
    skip = 7 + len(more)

    def body(*refs):
        expert_kernel(
            experts, min(FCUT, units), bool(given), part, joins, *refs[:skip], *refs[skip + len(taken) :]
        )

    return pl.pallas_call(
        body,
        grid_spec=pltpu.PrefetchScalarGridSpec(
            num_scalar_prefetch=1,
            grid=(steps,),
            in_specs=[
                weight(w_up.shape), weight(w_down.shape), whole(router.shape),
                whole(router_back.shape), block(capacity, rows_at), block(capacity, grads_at),
            ] + more_specs + [pl.BlockSpec(memory_space=pl.ANY)] * len(taken),
            out_specs=sent_specs + [whole(array.shape) for array in sums],
            scratch_shapes=[
                pltpu.VMEM((width, units), F32),
                pltpu.VMEM((width, units), F32),
                pltpu.VMEM((width, 2 * LANES), F32),
                pltpu.VMEM((capacity, width), F32),
                pltpu.VMEM((capacity, width), F32),
            ],
        ),
        out_shape=sent + sums,
        input_output_aliases={skip + at: to for at, to in enumerate(taken)},
        compiler_params=params(),
        cost_estimate=cost(
            20 * steps * capacity * width * units, 30e6, 2 * steps * capacity * units
        ),
        name="expert_own" if own else "expert_others",
    )(mine, *weights, rows, grads, *more, *taken.values())


def back_kernel(
    window, groups, starts_ref, here_ref, index_ref, hidden_ref, tok_ref, dy_ref, qkv_ref,
    probs_ref, mixed_ref, gain_one_ref, qkv_w_ref, proj_w_ref, gain_two_ref, *refs,
):
    bufs, own_bufs, router_refs = refs[:2], [None, refs[2]], refs[3:5]
    ghid_ref, dqkv_ref, own_ref, sent_ref = refs[5:-9]
    wins, acc, compact, padded, acc_qkv, acc_proj, acc_gain, dscores, dscores_low = refs[-9:]
    experts = starts_ref.shape[0]
    step = pl.program_id(0)
    width = tok_ref.shape[1]
    factor_qk = (width // HEADS) ** (-0.5)

    @pl.when(step == 0)
    def _():
        for ref in (acc_qkv, acc_proj, acc_gain):
            ref[...] = jnp.zeros(ref.shape, F32)

    combine_block(
        window, step, here_ref[1], starts_ref, index_ref[...], bufs, own_bufs, wins, acc
    )
    clear_gaps(padded)
    hat_two, scale_two = norm_parts(hidden_ref[...])
    grad_normed = acc[...]
    acc_gain[...] += jnp.sum(grad_normed * hat_two, axis=0, keepdims=True)
    grad_hidden = dy_ref[...].astype(F32) + norm_back(
        grad_normed, hat_two, scale_two, gain_two_ref[...]
    )
    ghid_ref[...] = grad_hidden
    compact[...] = grad_hidden
    spread_rows(compact, padded)
    grad_attn = padded[...].astype(BF)
    acc_proj[...] += dot_lt(mixed_ref[...], grad_attn)
    grad_mixed = dot_rt(grad_attn, proj_w_ref[...]).astype(BF)
    low = low_half()
    for pair in range(BLOCK_PAIRS):
        rows = slice(PAIR_PAD * pair, PAIR_PAD * (pair + 1))
        for two in range(width // LANES):
            cols = slice(LANES * two, LANES * (two + 1))
            key_cols = slice(width + LANES * two, width + LANES * (two + 1))
            value_cols = slice(2 * width + LANES * two, 2 * width + LANES * (two + 1))
            at = (pair * (width // LANES) + two) * 2 * PAIR_PAD
            dscores[at : at + 2 * PAIR_PAD, :] = dot_rt(
                two_heads(grad_mixed[rows, cols], low), qkv_ref[rows, value_cols]
            )
    for pair in range(BLOCK_PAIRS):
        each = 2 * PAIR_PAD * (width // LANES)
        part = slice(each * pair, each * (pair + 1))
        wide, grad_probs = probs_ref[part, :].astype(F32), dscores[part, :]
        meet = jnp.sum(wide * grad_probs, axis=-1, keepdims=True)
        dscores_low[part, :] = (wide * (grad_probs - meet) * factor_qk).astype(BF)
    for pair in range(BLOCK_PAIRS):
        rows = slice(PAIR_PAD * pair, PAIR_PAD * (pair + 1))
        for two in range(width // LANES):
            cols = slice(LANES * two, LANES * (two + 1))
            key_cols = slice(width + LANES * two, width + LANES * (two + 1))
            value_cols = slice(2 * width + LANES * two, 2 * width + LANES * (two + 1))
            at = (pair * (width // LANES) + two) * 2 * PAIR_PAD
            probs = probs_ref[at : at + 2 * PAIR_PAD, :]
            grad_out = two_heads(grad_mixed[rows, cols], low)
            grad_scores = dscores_low[at : at + 2 * PAIR_PAD, :]
            grad_query = one_row(dot(grad_scores, qkv_ref[rows, key_cols]), low)
            dqkv_ref[rows, cols] = grad_query.astype(BF)
            dqkv_ref[rows, key_cols] = dot_lt(
                grad_scores, two_heads(qkv_ref[rows, cols], low)
            ).astype(BF)
            dqkv_ref[rows, value_cols] = dot_lt(probs, grad_out).astype(BF)
    compact[...] = norm_parts(tok_ref[...].astype(F32))[0] * gain_one_ref[...]
    spread_rows(compact, padded)
    acc_qkv[...] += dot_lt(padded[...].astype(BF), dqkv_ref[...])

    @pl.when(step == pl.num_programs(0) - 1)
    def _():
        cores, sides, layers = groups
        half = acc_qkv.shape[0] * 4 // cores
        tall = half // (sides * layers)

        def piece(row):
            part, at = row // width, row % width
            if part < 3:
                return acc_qkv[at : at + tall, width * part : width * (part + 1)]
            return acc_proj[at : at + tall, :]

        for side in range(sides):
            for layer in range(layers):
                low = (side * layers + layer) * tall
                spot = (side ^ here_ref[1]) * layers + (layer ^ here_ref[2])
                to = pl.ds(pl.multiple_of(spot * tall, tall), tall)
                even, odd = piece(low), piece(half + low)
                own_ref[to, :] = jnp.where(here_ref[0] == 0, even, odd).astype(BF)
                sent_ref[to, :] = jnp.where(here_ref[0] == 0, odd, even).astype(BF)
        gain_one_sum = jnp.sum(acc_qkv[...] * qkv_w_ref[...].astype(F32), axis=-1, keepdims=True)
        lane = lax.broadcasted_iota(jnp.int32, (width, LANES), 1)
        router = sum(ref[...] for ref in router_refs)
        small = jnp.where(lane == experts, gain_one_sum, router).T[: own_ref.shape[0] - half, :]
        row = lax.broadcasted_iota(jnp.int32, small.shape, 0)
        small = jnp.where(row == experts + 1, acc_gain[...], small).astype(BF)
        own_ref[half:, :] = small
        sent_ref[half:, :] = small


def small_rows(experts):
    return 16 * -(-(experts + 2) // 16)


def back(starts, here, groups, index, hidden, tokens, dy, qkv, probs, mixed, gain_one, w_qkv, w_proj, gain_two, downs, own, routers, capacity):
    count, width = tokens.shape
    blocks = count // BLOCK
    experts = starts.shape[0]
    window = window_rows(experts, capacity)
    row = lambda shape: pl.BlockSpec(shape, lambda step, *_: (step, 0))
    cores, sides, layers = groups
    assert cores == 2
    sum_shape = (2 * width + small_rows(experts), width)
    flops = 2 * blocks * BLOCK_PAD * width * (8 * width + 10 * PAIR_PAD)
    return pl.pallas_call(
        functools.partial(back_kernel, window, groups),
        grid_spec=pltpu.PrefetchScalarGridSpec(
            num_scalar_prefetch=2,
            grid=(blocks,),
            in_specs=[
                row((BLOCK, 2)), row((BLOCK, width)), row((BLOCK, width)), row((BLOCK, width)),
                row((BLOCK_PAD, 3 * width)), row((probs.shape[0] // blocks, PAIR_PAD)),
                row((BLOCK_PAD, width)),
                whole((1, width)), whole(w_qkv.shape), whole(w_proj.shape), whole((1, width)),
            ] + [whole((downs[0].shape[0], capacity, width))] * 2 + [whole(own.shape)]
            + [whole((width, LANES))] * 2,
            out_specs=[
                row((BLOCK, width)), row((BLOCK_PAD, 3 * width)), whole(sum_shape), whole(sum_shape),
            ],
            scratch_shapes=[
                pltpu.VMEM((experts * window, width), BF),
                pltpu.VMEM((BLOCK, width), F32),
                pltpu.VMEM((BLOCK, width), F32),
                pltpu.VMEM((BLOCK_PAD, width), F32),
                pltpu.VMEM(w_qkv.shape, F32),
                pltpu.VMEM(w_proj.shape, F32),
                pltpu.VMEM((1, width), F32),
                pltpu.VMEM((probs.shape[0] // blocks, PAIR_PAD), F32),
                pltpu.VMEM((probs.shape[0] // blocks, PAIR_PAD), BF),
            ],
        ),
        out_shape=[
            jax.ShapeDtypeStruct((count, width), F32),
            jax.ShapeDtypeStruct(qkv.shape, BF),
            jax.ShapeDtypeStruct(sum_shape, BF),
            jax.ShapeDtypeStruct(sum_shape, BF),
        ],
        compiler_params=params(),
        cost_estimate=cost(1e12, 4000e6),
        name="back",
    )(
        starts, here, index, hidden, tokens, dy, qkv, probs, mixed, gain_one[None, :], w_qkv,
        w_proj, gain_two[None, :], *downs, own, *routers,
    )


def last_kernel(dqkv_ref, ghid_ref, tok_ref, gain_one_ref, qkv_w_ref, *refs):
    out_ref, compact, padded = refs[-3:]
    for sub in range(tok_ref.shape[0] // BLOCK):
        rows = slice(BLOCK * sub, BLOCK * (sub + 1))
        spread = slice(BLOCK_PAD * sub, BLOCK_PAD * (sub + 1))
        padded[...] = dot_rt(dqkv_ref[spread, :], qkv_w_ref[...])
        gather_rows(padded, compact)
        hat_one, scale_one = norm_parts(tok_ref[rows, :].astype(F32))
        out_ref[rows, :] = ghid_ref[rows, :] + norm_back(
            compact[...], hat_one, scale_one, gain_one_ref[...]
        )


def last(low, high, so_far, dqkv, ghid, tokens, gain_one, w_qkv):
    count, width = tokens.shape
    subs = max(n for n in range(1, LAST_SUBS + 1) if low % n == 0 and high % n == 0)
    row = lambda tall: pl.BlockSpec((tall * subs, width), lambda step: (step + low // subs, 0))
    wide = pl.BlockSpec((BLOCK_PAD * subs, 3 * width), lambda step: (step + low // subs, 0))
    taken = [] if so_far is None else [so_far]
    return pl.pallas_call(
        last_kernel,
        grid=((high - low) // subs,),
        in_specs=[wide, row(BLOCK), row(BLOCK), whole((1, width)), whole(w_qkv.shape)]
        + [pl.BlockSpec(memory_space=pl.ANY)] * len(taken),
        out_specs=row(BLOCK),
        out_shape=jax.ShapeDtypeStruct((count, width), F32),
        scratch_shapes=[pltpu.VMEM((BLOCK, width), F32), pltpu.VMEM((BLOCK_PAD, width), F32)],
        input_output_aliases={5: 0} if taken else {},
        compiler_params=params(),
        cost_estimate=cost(6 * BLOCK_PAD * (high - low) * width * width, 20e6),
        name="last",
    )(dqkv, ghid, tokens, gain_one[None, :], w_qkv, *taken)


def lay_kernel(groups, here_ref, own_ref, other_ref, qkv_ref, proj_ref):
    cores, sides, layers = groups
    tall, width = own_ref.shape[1:]
    each = width // tall
    for part in range(4):

        @pl.when(pl.program_id(0) == part)
        def _():
            for turn in range(each):
                core, spot = divmod(part * each + turn, sides * layers)
                side, layer = divmod(spot, layers)
                spot = (side ^ here_ref[1]) * layers + (layer ^ here_ref[2])
                piece = jnp.where(
                    core == here_ref[0], own_ref[spot].astype(F32), other_ref[spot].astype(F32)
                )
                (qkv_ref if part < 3 else proj_ref)[tall * turn : tall * (turn + 1), :] = piece


def lay(groups, here, own, other):
    width = own.shape[2]
    return pl.pallas_call(
        functools.partial(lay_kernel, groups),
        grid_spec=pltpu.PrefetchScalarGridSpec(
            num_scalar_prefetch=1,
            grid=(4,),
            in_specs=[whole(own.shape)] * 2,
            out_specs=[
                pl.BlockSpec((width, width), lambda step, *_: (0, jnp.minimum(step, 2))),
                whole((width, width)),
            ],
        ),
        out_shape=[
            jax.ShapeDtypeStruct((width, 3 * width), F32),
            jax.ShapeDtypeStruct((width, width), F32),
        ],
        compiler_params=params(),
        cost_estimate=cost(1e6, 8e6),
        name="lay",
    )(here, own, other)


def unpack_kernel(*refs):
    parts, (up_ref, down_ref) = refs[:-2], refs[-2:]
    tall, width = up_ref.shape[1], down_ref.shape[2]
    for which, part in enumerate(parts):
        up_ref[which] = part[:tall, :].astype(F32)
        for turn in range(down_ref.shape[1] // tall):
            down_ref[which, tall * turn : tall * (turn + 1), :] = (
                part[tall:, width * turn : width * (turn + 1)].astype(F32)
            )


def unpack(parts, width):
    tall, units = parts[0].shape[0] // 2, parts[0].shape[1]
    outs = [
        jax.ShapeDtypeStruct((len(parts), tall, units), F32),
        jax.ShapeDtypeStruct((len(parts), tall * units // width, width), F32),
    ]
    return pl.pallas_call(
        unpack_kernel,
        grid=(1,),
        in_specs=[whole(part.shape) for part in parts],
        out_specs=[whole(out.shape) for out in outs],
        out_shape=outs,
        compiler_params=params(),
        cost_estimate=cost(1e6, 4e6),
        name="unpack",
    )(*parts)


def jump(value, axis, far):
    size = lax.axis_size(axis)
    return lax.ppermute(value, axis, [(at, at ^ far) for at in range(size)])


def merge_kernel(cuts, extra, count, *refs):
    parts, outs = refs[:count], refs[count:]
    tall = (parts[0].shape[0] - extra) // cuts

    def total(rows):
        value = parts[0][rows, :].astype(F32)
        for part in parts[1:]:
            value = value + part[rows, :].astype(F32)
        return value

    small = total(slice(cuts * tall, None))
    for cut, out in enumerate(outs):
        if cut == cuts:
            out[...] = small
            continue
        out[:tall, :] = total(slice(cut * tall, (cut + 1) * tall)).astype(BF)
        if out.shape[0] > tall:
            out[tall:, :] = small.astype(BF)


def merge(parts, cuts, extra, ends):
    rows, width = parts[0].shape
    tall = (rows - extra) // cuts
    if ends:
        outs = [jax.ShapeDtypeStruct((tall, width), BF), jax.ShapeDtypeStruct((extra, width), F32)]
    else:
        outs = [jax.ShapeDtypeStruct((tall + extra, width), BF)] * cuts
    return pl.pallas_call(
        functools.partial(merge_kernel, cuts, extra, len(parts)),
        grid=(1,),
        in_specs=[whole((rows, width))] * len(parts),
        out_specs=[whole(out.shape) for out in outs],
        out_shape=outs,
        compiler_params=params(),
        cost_estimate=cost(1e6, 4e6),
        name="merge",
    )(*parts)


def after(value, *others):
    return lax.optimization_barrier((value, *others))[0]


def sum_over_all(own, sent, groups, extra, arrived, beside):
    cores, sides, layers = groups
    beside = iter(beside)

    def spread(own, sent, axis, scale):
        came = [jump(part, axis, scale * far) for far, part in enumerate(sent, 1)]
        return [own] + list(after(tuple(came), next(beside)(own)))

    half = merge([own, jump(sent, "dp", 1)], sides, extra, False)
    half = list(after(tuple(half), arrived))
    flat = merge(spread(half[0], half[1:], "expert", 1), layers, extra, False)
    spot, small = merge(spread(flat[0], flat[1:], "dp", cores), 1, extra, True)
    flat = jnp.stack(spread(spot, [spot] * (layers - 1), "dp", cores))
    half = jnp.stack(spread(flat, [flat] * (sides - 1), "expert", 1))
    half = half.reshape(sides * layers, *spot.shape)
    return half, jump(half, "dp", 1), small


def per_device(
    tokens, gain_one, w_qkv, w_proj, gain_two, w_router, w_in, w_eout, picks, keep, grad_out
):
    count, width = tokens.shape
    local = w_in.shape[0]
    assert local == 2
    owners = lax.axis_size("expert")
    shards = lax.axis_size("dp")
    experts = local * owners
    capacity = 8 * ((21 * count + 80 * experts - 1) // (80 * experts))
    me, row = lax.axis_index("expert"), lax.axis_index("dp")
    cores = 2
    groups = (cores, owners, shards // cores)
    here = jnp.stack([row % cores, me, row // cores]).astype(jnp.int32)

    def swap(sent):
        return lax.all_to_all(sent, "expert", split_axis=0, concat_axis=0, tiled=True)

    index_rows, starts = places(picks, keep, experts, local, capacity)
    send = lambda srcs, *plan: dispatch(srcs, starts, index_rows, owners, capacity, plan)
    (dy_first,) = send([grad_out], (0, (0,)))
    got = swap(dy_first)
    hidden, rows, qkv, probs, mixed = attend(
        after(tokens, dy_first), gain_one, w_qkv, w_proj, gain_two
    )
    (x_first,) = send([rows], (0, (0,)))
    arrived = [[(swap(after(x_first, got)), 0), (got, 0)]]
    kept = [[(x_first, 0), (dy_first, 0)]]
    others = send([after(rows, x_first), grad_out], *[(part, (0, 1)) for part in range(1, local)])
    for sent in others:
        got = swap(after(sent, arrived[-1][0][0]))
        arrived.append([(got, 0), (got, 1)])
        kept.append([(sent, 0), (sent, 1)])
    index = index_rows.transpose(0, 2, 1).reshape(count, 2)
    head = w_router.astype(BF)
    rest = (w_router - head.astype(F32)).astype(BF)
    gap = ((0, 0), (0, LANES - experts))
    router = jnp.concatenate([jnp.pad(head, gap), jnp.pad(rest, gap)], axis=1)
    router_back = jnp.concatenate([jnp.pad(head, gap).T, jnp.pad(rest, gap).T], axis=0)
    early = 16 * (capacity // 32)
    weights = (w_in, w_eout, router, router_back)

    def one(part, own, given, before, *taken):
        mine = jnp.stack([me * local + part, me]).astype(jnp.int32)
        came = (kept if own else arrived)[part]
        taken = dict(zip(range(2 - len(taken), 2), taken))
        return expert_pass(
            part, mine, *came, weights, early, experts, capacity, shards, own, given, before, taken
        )

    def reduce(grad):
        grad = grad.reshape(shards * grad.shape[1], grad.shape[2])
        return lax.psum_scatter(grad, "dp", scatter_dimension=0, tiled=True)

    head, tail, *given = one(0, True, [], None)
    head, tail, grad, router_first = one(0, False, given, None, head, tail)
    sums, tail_first = [reduce(grad)], tail
    head = swap(after(head, got))
    down, tail, *given = one(1, False, [], tail_first)
    down = swap(after(down, head))
    own_down, own_out, grad, router_second = one(1, True, given, None)
    sums.append(reduce(grad))
    tail = swap(after(tail, down))
    grad_hidden, dqkv, own, sent = back(
        starts, here, groups, index, hidden, tokens, grad_out, qkv, probs, mixed, gain_one,
        w_qkv, w_proj, gain_two, [head, down], own_down, [router_first, router_second], capacity,
    )
    blocks = count // BLOCK
    some = blocks // 3

    def make_top(tie):
        return top(
            starts, here, index, after(hidden, tie), head, tail, tail_first, own_out, early, capacity
        )

    def make_unpack(tie):
        return unpack(after(tuple(sums), tie), width)

    def make_last(low, high, tie, so_far=None):
        return last(
            low, high, so_far, after(dqkv, tie), grad_hidden, tokens, gain_one, w_qkv
        )

    made = {}

    def beside(name, work):
        def go(tie):
            made[name] = work(tie)
            return jax.tree.leaves(made[name])[0]

        return go

    own, other, small = sum_over_all(
        own, sent, groups, small_rows(experts), tail,
        [
            beside("top", make_top),
            beside("unpack", make_unpack),
            beside("some", lambda tie: make_last(0, some, tie)),
            beside("last", lambda tie: make_last(some, blocks, tie, made["some"])),
        ],
    )
    block_out, grad_tokens, (grad_in, grad_eout) = made["top"], made["last"], made["unpack"]
    grad_qkv, grad_proj = lay(groups, here, own, other)
    return (
        block_out,
        grad_tokens,
        small[experts] / gain_one,
        grad_qkv,
        grad_proj,
        small[experts + 1],
        small[:experts].T,
        grad_in,
        grad_eout,
    )


def solution(mesh):
    rows = P(("dp", "expert"), None)
    experts = P("expert", None, None)
    return jax.shard_map(
        per_device,
        mesh=mesh,
        in_specs=(rows, P(), P(), P(), P(), P(), experts, experts, rows, rows, rows),
        out_specs=(
            rows, rows, P(), P(), P(), P(), P(), P("expert", "dp", None), P("expert", "dp", None),
        ),
        check_vma=False,
    )
```

```python
import functools

import jax
import jax.numpy as jnp
from jax import lax
from jax.experimental import pallas as pl
from jax.experimental.pallas import tpu as pltpu
from jax.sharding import PartitionSpec as P

HEADS = 8
PATCHES = 49
LANES = 128
PAIR = 2 * PATCHES
PAIR_PAD = 112
BLOCK_PAIRS = 4
BLOCK = BLOCK_PAIRS * PAIR
BLOCK_PAD = BLOCK_PAIRS * PAIR_PAD
BF = jnp.bfloat16
F32 = jnp.float32
VMEM_BYTES = 62 * 1024 * 1024
FCUT = 256
CHUNK = 256
TOP_SUBS, SEND_SUBS, LAST_SUBS = 2, 2, 2


def params():
    return pltpu.CompilerParams(
        dimension_semantics=("arbitrary",), vmem_limit_bytes=VMEM_BYTES
    )


def cost(flops, moved, special=0):
    return pl.CostEstimate(
        flops=int(flops), bytes_accessed=int(moved), transcendentals=int(special)
    )


def step_blocks(blocks, most):
    return max(n for n in range(1, most + 1) if blocks % n == 0)


def whole(shape):
    return pl.BlockSpec(shape, lambda *_: (0,) * len(shape))


def dot(left, right):
    return jnp.dot(left, right, preferred_element_type=F32)


def dot_rt(left, right):
    return lax.dot_general(left, right, (((1,), (1,)), ((), ())), preferred_element_type=F32)


def dot_lt(left, right):
    return lax.dot_general(left, right, (((0,), (0,)), ((), ())), preferred_element_type=F32)


def norm_parts(values):
    mean = jnp.mean(values, axis=-1, keepdims=True)
    cent = values - mean
    factor = lax.rsqrt(jnp.mean(cent * cent, axis=-1, keepdims=True) + 1e-06)
    return cent * factor, factor


def norm_back(grad_normed, normed_hat, factor, gain):
    grad_hat = grad_normed * gain
    inner = grad_hat - jnp.mean(grad_hat, axis=-1, keepdims=True)
    inner = inner - normed_hat * jnp.mean(grad_hat * normed_hat, axis=-1, keepdims=True)
    return factor * inner


def spread_rows(compact, padded):
    for pair in range(BLOCK_PAIRS):
        padded[PAIR_PAD * pair : PAIR_PAD * pair + PAIR] = compact[PAIR * pair : PAIR * pair + PAIR]


def gather_rows(padded, compact):
    for pair in range(BLOCK_PAIRS):
        compact[PAIR * pair : PAIR * pair + PAIR] = padded[PAIR_PAD * pair : PAIR_PAD * pair + PAIR]


def clear_gaps(padded):
    for pair in range(BLOCK_PAIRS):
        low = PAIR_PAD * pair + PAIR
        padded[low : low + PAIR_PAD - PAIR] = jnp.zeros((PAIR_PAD - PAIR, padded.shape[1]), F32)


def image_of(position):
    return (position >= PATCHES).astype(jnp.int32) + (position >= PAIR).astype(jnp.int32)


def same_image():
    rows = lax.broadcasted_iota(jnp.int32, (2 * PAIR_PAD, PAIR_PAD), 0)
    rows = jnp.where(rows >= PAIR_PAD, rows - PAIR_PAD, rows)
    cols = lax.broadcasted_iota(jnp.int32, (2 * PAIR_PAD, PAIR_PAD), 1)
    return image_of(rows) == image_of(cols)


def low_half():
    return lax.broadcasted_iota(jnp.int32, (PAIR_PAD, LANES), 1) < LANES // 2


def two_heads(values, low):
    zero = jnp.zeros_like(values)
    return jnp.concatenate([jnp.where(low, values, zero), jnp.where(low, zero, values)], axis=0)


def one_row(values, low):
    return jnp.where(low, values[:PAIR_PAD], values[PAIR_PAD:])


def attend_kernel(
    tok_ref, gain_one_ref, qkv_w_ref, proj_w_ref, gain_two_ref,
    hidden_ref, rows_ref, qkv_ref, probs_ref, mixed_ref,
    compact, padded, scores,
):
    width = tok_ref.shape[1]
    factor_qk = (width // HEADS) ** (-0.5)
    clear_gaps(padded)
    inputs = tok_ref[...].astype(F32)
    compact[...] = norm_parts(inputs)[0] * gain_one_ref[...]
    spread_rows(compact, padded)
    qkv_ref[...] = dot(padded[...].astype(BF), qkv_w_ref[...]).astype(BF)
    valid = same_image()
    low = low_half()
    for pair in range(BLOCK_PAIRS):
        rows = slice(PAIR_PAD * pair, PAIR_PAD * (pair + 1))
        for two in range(width // LANES):
            cols = slice(LANES * two, LANES * (two + 1))
            query = qkv_ref[rows, cols]
            keys = qkv_ref[rows, width + LANES * two : width + LANES * (two + 1)]
            step = (pair * (width // LANES) + two) * 2 * PAIR_PAD
            scores[step : step + 2 * PAIR_PAD, :] = jnp.where(
                valid, dot_rt(two_heads(query, low), keys), -1e30
            )
    for pair in range(BLOCK_PAIRS):
        each = 2 * PAIR_PAD * (width // LANES)
        part = slice(each * pair, each * (pair + 1))
        logits = scores[part, :]
        highest = jnp.max(logits, axis=-1, keepdims=True)
        expo = jnp.exp((logits - highest) * factor_qk)
        probs_ref[part, :] = (expo / jnp.sum(expo, axis=-1, keepdims=True)).astype(BF)
    for pair in range(BLOCK_PAIRS):
        rows = slice(PAIR_PAD * pair, PAIR_PAD * (pair + 1))
        for two in range(width // LANES):
            cols = slice(LANES * two, LANES * (two + 1))
            values = qkv_ref[rows, 2 * width + LANES * two : 2 * width + LANES * (two + 1)]
            step = (pair * (width // LANES) + two) * 2 * PAIR_PAD
            probs = probs_ref[step : step + 2 * PAIR_PAD, :]
            mixed_ref[rows, cols] = one_row(dot(probs, values), low).astype(BF)
    padded[...] = dot(mixed_ref[...], proj_w_ref[...])
    gather_rows(padded, compact)
    hidden = inputs + compact[...]
    hidden_ref[...] = hidden
    rows_ref[...] = (norm_parts(hidden)[0] * gain_two_ref[...]).astype(BF)


def attend(tokens, gain_one, w_qkv, w_proj, gain_two):
    count, width = tokens.shape
    blocks = count // BLOCK
    prob_rows = BLOCK_PAIRS * (width // LANES) * 2 * PAIR_PAD
    row = lambda shape: pl.BlockSpec(shape, lambda step: (step, 0))
    flops = 2 * blocks * BLOCK_PAD * width * (4 * width + 4 * PAIR_PAD)
    return pl.pallas_call(
        attend_kernel,
        grid=(blocks,),
        in_specs=[
            row((BLOCK, width)), whole((1, width)), whole(w_qkv.shape), whole(w_proj.shape),
            whole((1, width)),
        ],
        out_specs=[
            row((BLOCK, width)), row((BLOCK, width)), row((BLOCK_PAD, 3 * width)),
            row((prob_rows, PAIR_PAD)), row((BLOCK_PAD, width)),
        ],
        out_shape=[
            jax.ShapeDtypeStruct((count, width), F32),
            jax.ShapeDtypeStruct((count, width), BF),
            jax.ShapeDtypeStruct((blocks * BLOCK_PAD, 3 * width), BF),
            jax.ShapeDtypeStruct((blocks * prob_rows, PAIR_PAD), BF),
            jax.ShapeDtypeStruct((blocks * BLOCK_PAD, width), BF),
        ],
        scratch_shapes=[
            pltpu.VMEM((BLOCK, width), F32), pltpu.VMEM((BLOCK_PAD, width), F32),
            pltpu.VMEM((prob_rows, PAIR_PAD), F32),
        ],
        compiler_params=params(),
        cost_estimate=cost(flops, 30e6, blocks * prob_rows * LANES),
        name="attend",
    )(tokens, gain_one[None, :], w_qkv, w_proj, gain_two[None, :])


def place_kernel(local, capacity, picks_ref, keep_ref, index_ref, starts_ref):
    blocks, _, block = index_ref.shape
    experts = starts_ref.shape[0]
    owners = experts // local
    row = lax.broadcasted_iota(jnp.int32, (experts, block), 0)
    ids = row * local
    for part in range(1, local):
        ids = jnp.where(row >= owners * part, (row - owners * part) * local + part, ids)
    earlier = lax.broadcasted_iota(jnp.int32, (block, block), 0) < lax.broadcasted_iota(
        jnp.int32, (block, block), 1
    )
    earlier = earlier.astype(F32).astype(BF)
    base = (row * capacity).astype(F32)
    lane = lax.broadcasted_iota(jnp.int32, (experts, LANES), 1)
    starts = jnp.zeros((experts, LANES), jnp.int32)
    carry = jnp.zeros((experts, 1), F32)
    for step in range(blocks):
        cols = slice(block * step, block * (step + 1))
        names = [picks_ref[c : c + 1, cols] == ids for c in (0, 1)]
        named = (names[0] | names[1]).astype(F32)
        spot = base + (dot(named.astype(BF), earlier) + carry)
        for c in (0, 1):
            found = jnp.sum(jnp.where(names[c], spot, 0.0), axis=0, keepdims=True)
            index_ref[step, c : c + 1, :] = jnp.where(
                keep_ref[c : c + 1, cols] > 0, found.astype(jnp.int32), -1
            )
        carry = carry + jnp.sum(named, axis=1, keepdims=True)
        starts = jnp.where(lane == step + 1, carry.astype(jnp.int32), starts)
    starts_ref[...] = starts


def places(picks, keep, experts, local, capacity):
    count = picks.shape[0]
    outs = [
        jax.ShapeDtypeStruct((count // BLOCK, 2, BLOCK), jnp.int32),
        jax.ShapeDtypeStruct((experts, LANES), jnp.int32),
    ]
    return pl.pallas_call(
        functools.partial(place_kernel, local, capacity),
        grid=(1,),
        in_specs=[whole((2, count))] * 2,
        out_specs=[whole(out.shape) for out in outs],
        out_shape=outs,
        compiler_params=params(),
        cost_estimate=cost(1e8, 1e5),
        name="places",
    )(picks.T, keep.T)


def window_rows(experts, capacity):
    return min(capacity, 1024 // experts)


def window_at(starts_ref, expert, step, turn, window, capacity):
    low = starts_ref[expert, step]
    begin = (low // 16) * 16 + turn * window
    at = pl.multiple_of(jnp.minimum(begin, capacity - window), 16)
    return begin, starts_ref[expert, step + 1], at


def turns(starts_ref, step, experts, window):
    most = 0
    for expert in experts:
        low = (starts_ref[expert, step] // 16) * 16
        most = jnp.maximum(most, (starts_ref[expert, step + 1] - low + window - 1) // window)
    return most


def dispatch_kernel(window, capacity, plan, sources, starts_ref, index_ref, *refs):
    src_refs, outs, (spots, got) = refs[:sources], refs[sources:-2], refs[-2:]
    owners = outs[0].shape[0]
    named = [owners * part + owner for part, _ in plan for owner in range(owners)]
    subs = index_ref.shape[0]

    @pl.when(pl.program_id(0) == 0)
    def _():
        for out in outs:
            out[...] = jnp.zeros(out.shape, out.dtype)

    place = lax.broadcasted_iota(jnp.int32, (window, index_ref.shape[2]), 0)
    for sub in range(subs):
        step = pl.program_id(0) * subs + sub
        block = slice(BLOCK * sub, BLOCK * (sub + 1))
        first, second = index_ref[sub, 0:1, :], index_ref[sub, 1:2, :]

        def one_turn(turn, carry):
            for (part, used), out in zip(plan, outs):
                spans = []
                for owner in range(owners):
                    expert = part * owners + owner
                    begin, _, at = window_at(starts_ref, expert, step, turn, window, capacity)
                    shift = expert * capacity
                    near = jnp.where(first >= shift + begin, first - (shift + at), -1)
                    far = jnp.where(second >= shift + begin, second - (shift + at), -1)
                    hit = jnp.where((near >= 0) & (near < window), near, far)
                    spots[window * owner : window * (owner + 1), :] = (
                        (place == hit).astype(F32).astype(BF)
                    )
                    spans.append(at)
                for order, which in enumerate(used):
                    got[...] = dot(spots[...], src_refs[which][block, :])
                    for owner, at in enumerate(spans):
                        rows = pl.ds(pl.multiple_of(at + order * capacity, 16), window)
                        held = out[owner, rows, :].astype(F32)
                        out[owner, rows, :] = (
                            held + got[window * owner : window * (owner + 1), :]
                        ).astype(BF)
            return carry

        lax.fori_loop(0, turns(starts_ref, step, named, window), one_turn, 0)


def dispatch(srcs, starts, index_rows, owners, capacity, plan):
    count, width = srcs[0].shape
    subs = step_blocks(count // BLOCK, SEND_SUBS)
    window = window_rows(starts.shape[0], capacity)
    shapes = [(owners, len(used) * capacity, width) for _, used in plan]
    return pl.pallas_call(
        functools.partial(dispatch_kernel, window, capacity, plan, len(srcs)),
        grid_spec=pltpu.PrefetchScalarGridSpec(
            num_scalar_prefetch=1,
            grid=(count // BLOCK // subs,),
            in_specs=[pl.BlockSpec((subs, 2, BLOCK), lambda step, *_: (step, 0, 0))]
            + [pl.BlockSpec((BLOCK * subs, width), lambda step, *_: (step, 0))] * len(srcs),
            out_specs=[whole(shape) for shape in shapes],
            scratch_shapes=[
                pltpu.VMEM((owners * window, BLOCK), BF),
                pltpu.VMEM((owners * window, width), F32),
            ],
        ),
        out_shape=[jax.ShapeDtypeStruct(shape, BF) for shape in shapes],
        compiler_params=params(),
        cost_estimate=cost(6e9, 8e6),
        name="dispatch",
    )(starts, index_rows, *srcs)


def combine_block(window, step, me, starts_ref, index, bufs, own_bufs, wins, acc):
    owners, capacity = bufs[0].shape[:2]
    experts = owners * len(bufs)
    lane = lax.broadcasted_iota(jnp.int32, (1, experts * window), 1)
    acc[...] = jnp.zeros(acc.shape, F32)

    def one_turn(turn, carry):
        seen = jnp.full((1, experts * window), -2, jnp.int32)
        for expert in range(experts):
            part, owner = expert // owners, expert % owners
            begin, high, at = window_at(starts_ref, expert, step, turn, window, capacity)
            slot = lane + (at - expert * window)
            fresh = (slot >= begin) & (slot < high)
            mine = (lane >= expert * window) & (lane < (expert + 1) * window)
            seen = jnp.where(mine & fresh, slot + expert * capacity, seen)
            to = slice(window * expert, window * (expert + 1))
            if own_bufs[part] is None:
                wins[to, :] = bufs[part][owner, pl.ds(at, window), :]
            else:
                wins[to, :] = jnp.where(
                    me == owner, own_bufs[part][0, pl.ds(at, window), :],
                    bufs[part][owner, pl.ds(at, window), :],
                )
        total = acc[...]
        for low in range(0, experts * window, CHUNK):
            part = slice(low, min(low + CHUNK, experts * window))
            hit = (index[:, 0:1] == seen[:, part]) | (index[:, 1:2] == seen[:, part])
            total = total + dot(hit.astype(F32).astype(BF), wins[part, :])
        acc[...] = total
        return carry

    lax.fori_loop(0, turns(starts_ref, step, range(experts), window), one_turn, 0)


def top_kernel(early, starts_ref, here_ref, index_ref, hidden_ref, head_ref, tail_ref, own_first_ref, own_second_ref, out_ref, first, second, wins, acc, sems):
    step = pl.program_id(0)
    experts = starts_ref.shape[0]
    window, capacity = wins.shape[0] // experts, first.shape[1]
    late = capacity - early

    @pl.when(step == 0)
    def _():
        me, owners = here_ref[1], first.shape[0]

        def move(go):
            go(pltpu.make_async_copy(
                head_ref.at[:, pl.ds(capacity, early), :], first.at[:, pl.ds(0, early), :], sems.at[0]
            ))
            for owner in range(owners):
                to_first = first.at[owner, pl.ds(early, late), :]
                one, two = sems.at[1 + owner], sems.at[1 + owners + owner]

                @pl.when(me == owner)
                def _():
                    go(pltpu.make_async_copy(own_first_ref.at[owner], to_first, one))
                    go(pltpu.make_async_copy(own_second_ref.at[0], second.at[owner], two))

                @pl.when(me != owner)
                def _():
                    go(pltpu.make_async_copy(tail_ref.at[owner, pl.ds(0, late), :], to_first, one))
                    go(pltpu.make_async_copy(
                        tail_ref.at[owner, pl.ds(late, capacity), :], second.at[owner], two
                    ))

        move(lambda copy: copy.start())
        move(lambda copy: copy.wait())

    subs = hidden_ref.shape[0] // BLOCK
    for sub in range(subs):
        rows = slice(BLOCK * sub, BLOCK * (sub + 1))
        combine_block(
            window, step * subs + sub, 0, starts_ref, index_ref[rows, :], [first, second],
            [None, None], wins, acc,
        )
        out_ref[rows, :] = (hidden_ref[rows, :] + acc[...]).astype(BF)


def top(starts, here, index, hidden, head, tail, own_first, own_second, early, capacity):
    count, width = hidden.shape
    experts = starts.shape[0]
    window = window_rows(experts, capacity)
    row = lambda shape: pl.BlockSpec(shape, lambda step, *_: (step, 0))
    tall = BLOCK * step_blocks(count // BLOCK, TOP_SUBS)
    held = pltpu.VMEM((head.shape[0], capacity, width), BF)
    return pl.pallas_call(
        functools.partial(top_kernel, early),
        grid_spec=pltpu.PrefetchScalarGridSpec(
            num_scalar_prefetch=2,
            grid=(count // tall,),
            in_specs=[row((tall, 2)), row((tall, width))] + [pl.BlockSpec(memory_space=pl.ANY)] * 4,
            out_specs=pl.BlockSpec((tall, width), lambda step, *_: (step, 0)),
            scratch_shapes=[
                held, held, pltpu.VMEM((experts * window, width), BF),
                pltpu.VMEM((BLOCK, width), F32), pltpu.SemaphoreType.DMA((1 + 2 * head.shape[0],)),
            ],
        ),
        out_shape=jax.ShapeDtypeStruct((count, width), BF),
        compiler_params=params(),
        cost_estimate=cost(6e9, 12e6),
        name="top",
    )(starts, here, index, hidden, head, tail, own_first, own_second)


def gelu_parts(values):
    size = 1.0 + (0.3275911 * 0.7071067811865476) * jnp.abs(values)
    near = pl.reciprocal(size, approx=True)
    near = near * (2.0 - size * near)
    expo = jnp.exp2((-0.5 * 1.4426950408889634) * (values * values))
    poly = 0.5 * 1.061405429
    for term in (-1.453152027, 1.421413741, -0.284496736, 0.254829592):
        poly = poly * near + 0.5 * term
    tail = poly * near * expo
    share = jnp.where(values >= 0, 1.0 - tail, tail)
    return values * share, share + values * (0.3989422804014327 * expo)


def expert_kernel(
    experts, fcut, begun, part, joins, mine_ref, up_ref, down_ref, router_ref, back_ref, x_ref, dy_ref, *refs
):
    given, refs = refs[: 3 * begun], refs[3 * begun :]
    if joins:
        before_ref, refs = refs[0], refs[1:]
    *grad_refs, grouter_ref = refs[2:-5]
    acc_up, acc_down, acc_router, acc_out, acc_dx = refs[-5:]
    step = pl.program_id(0)
    hidden_units = up_ref.shape[1]
    _, capacity, width = x_ref.shape
    count = capacity

    @pl.when(step == 0)
    def _():
        if begun:
            acc_up[...] = given[0][...].astype(F32)
            acc_down[...] = given[1][...].astype(F32)
            acc_router[:, :LANES] = given[2][...]
            acc_router[:, LANES:] = jnp.zeros((width, LANES), F32)
        else:
            acc_up[...] = jnp.zeros(acc_up.shape, F32)
            acc_down[...] = jnp.zeros(acc_down.shape, F32)
            acc_router[...] = jnp.zeros(acc_router.shape, F32)

    rows = x_ref[...].reshape(count, width)
    logits = dot(rows, router_ref[...])
    logits = logits[:, :LANES] + logits[:, LANES:]
    lane = lax.broadcasted_iota(jnp.int32, (count, LANES), 1)
    logits = jnp.where(lane < experts, logits, -1e30)
    expo = jnp.exp(logits - jnp.max(logits, axis=-1, keepdims=True))
    gates = expo / jnp.sum(expo, axis=-1, keepdims=True)
    own = (lane == mine_ref[0]).astype(F32)
    chosen = jnp.sum(gates * own, axis=-1, keepdims=True)
    pair = (chosen * dy_ref[...].reshape(count, width).astype(F32)).astype(BF)
    rows_t = rows.T
    pair_t = pair.T
    chunks = [slice(low, low + fcut) for low in range(0, hidden_units, fcut)]
    ahead = lambda cols: (dot(rows, up_ref[:, cols]), dot_rt(pair, down_ref[cols, :]))
    ready = ahead(chunks[0])
    for turn, cols in enumerate(chunks):
        pre, grad_act = ready
        if turn + 1 < len(chunks):
            ready = ahead(chunks[turn + 1])
        act, slope = gelu_parts(pre)
        act = act.astype(BF)
        grad_pre = (grad_act * slope).astype(BF)
        acc_up[:, cols] += dot(rows_t, grad_pre)
        acc_down[:, cols] += dot(pair_t, act)
        if turn == 0:
            acc_out[...] = dot(act, down_ref[cols, :])
            acc_dx[...] = dot_rt(grad_pre, up_ref[:, cols])
        else:
            acc_out[...] += dot(act, down_ref[cols, :])
            acc_dx[...] += dot_rt(grad_pre, up_ref[:, cols])
    inner = jnp.sum(acc_out[...] * pair.astype(F32), axis=-1, keepdims=True)
    grad_logits = inner * (own - gates)
    head = grad_logits.astype(BF)
    rest = (grad_logits - head.astype(F32)).astype(BF)
    acc_router[...] += dot(rows_t, jnp.concatenate([head, rest], axis=1))
    out = (chosen * acc_out[...]).astype(BF)
    grad_rows = (acc_dx[...] + dot(jnp.concatenate([head, head], axis=1), back_ref[...])).astype(BF)
    if part:
        refs[0][0] = grad_rows
        late = refs[1].shape[1] - capacity
        if late:
            refs[1][0, :late, :] = before_ref[0]
        refs[1][0, late:, :] = out
    else:
        early = refs[0].shape[1] - capacity
        refs[0][0, :capacity, :] = grad_rows
        refs[0][0, capacity:, :] = out[:early]
        refs[1][0] = out[early:]

    @pl.when(step == pl.num_programs(0) - 1)
    def _():
        grouter_ref[...] = acc_router[:, :LANES] + acc_router[:, LANES:]
        if not begun:
            grad_refs[0][...] = acc_up[...].astype(BF)
            grad_refs[1][...] = acc_down[...].astype(BF)
            return
        grad_ref = grad_refs[0]
        shards, tall, _ = grad_ref.shape
        up_rows, down_rows = width // shards, hidden_units // shards
        piece = tall - up_rows
        for shard in range(shards):
            grad_ref[shard, :up_rows, :] = acc_up[up_rows * shard : up_rows * (shard + 1), :].astype(BF)
            turned = acc_down[:, down_rows * shard : down_rows * (shard + 1)].T.astype(BF)
            for part in range(down_rows // piece):
                grad_ref[shard, up_rows:, width * part : width * (part + 1)] = (
                    turned[piece * part : piece * (part + 1), :]
                )


def expert_pass(part, mine, rows, grads, weights, early, experts, capacity, shards, own, given, before, taken):
    (rows, rows_at), (grads, grads_at) = rows, grads
    w_up, w_down, router, router_back = weights
    sources, _, width = rows.shape
    units = w_up.shape[2]
    source = lambda step, mine_ref: (mine_ref[1] + (0 if own else 1) + step) % sources
    block = lambda tall, at: pl.BlockSpec(
        (1, tall, width), lambda step, mine_ref: (source(step, mine_ref), at, 0)
    )
    weight = lambda shape: pl.BlockSpec((None,) + shape[1:], lambda *_: (part, 0, 0))
    late = capacity - early
    talls = [capacity, late + capacity] if part else [capacity + early, late]
    sent = [jax.ShapeDtypeStruct((sources, tall, width), BF) for tall in talls]
    sent_specs = [block(tall, 0) for tall in talls]
    if part and own:
        sent = [jax.ShapeDtypeStruct((1, capacity, width), BF)] * 2
        sent_specs = [whole((1, capacity, width))] * 2
    if given:
        sums = [jax.ShapeDtypeStruct((shards, width // shards * 2, units), BF)]
    else:
        sums = [jax.ShapeDtypeStruct((width, units), BF)] * 2
    sums.append(jax.ShapeDtypeStruct((width, LANES), F32))
    steps = 1 if own else sources - 1
    joins = bool(part) and not own
    more = list(given) + ([before] if joins else [])
    more_specs = [whole(array.shape) for array in given] + ([block(late, 0)] if joins else [])
    skip = 7 + len(more)

    def body(*refs):
        expert_kernel(
            experts, min(FCUT, units), bool(given), part, joins, *refs[:skip], *refs[skip + len(taken) :]
        )

    return pl.pallas_call(
        body,
        grid_spec=pltpu.PrefetchScalarGridSpec(
            num_scalar_prefetch=1,
            grid=(steps,),
            in_specs=[
                weight(w_up.shape), weight(w_down.shape), whole(router.shape),
                whole(router_back.shape), block(capacity, rows_at), block(capacity, grads_at),
            ] + more_specs + [pl.BlockSpec(memory_space=pl.ANY)] * len(taken),
            out_specs=sent_specs + [whole(array.shape) for array in sums],
            scratch_shapes=[
                pltpu.VMEM((width, units), F32),
                pltpu.VMEM((width, units), F32),
                pltpu.VMEM((width, 2 * LANES), F32),
                pltpu.VMEM((capacity, width), F32),
                pltpu.VMEM((capacity, width), F32),
            ],
        ),
        out_shape=sent + sums,
        input_output_aliases={skip + at: to for at, to in enumerate(taken)},
        compiler_params=params(),
        cost_estimate=cost(
            20 * steps * capacity * width * units, 30e6, 2 * steps * capacity * units
        ),
        name="expert_own" if own else "expert_others",
    )(mine, *weights, rows, grads, *more, *taken.values())


def back_kernel(
    window, groups, starts_ref, here_ref, index_ref, hidden_ref, tok_ref, dy_ref, qkv_ref,
    probs_ref, mixed_ref, gain_one_ref, qkv_w_ref, proj_w_ref, gain_two_ref, *refs,
):
    bufs, own_bufs, router_refs = refs[:2], [None, refs[2]], refs[3:5]
    ghid_ref, dqkv_ref, own_ref, sent_ref = refs[5:-9]
    wins, acc, compact, padded, acc_qkv, acc_proj, acc_gain, dscores, dscores_low = refs[-9:]
    experts = starts_ref.shape[0]
    step = pl.program_id(0)
    width = tok_ref.shape[1]
    factor_qk = (width // HEADS) ** (-0.5)

    @pl.when(step == 0)
    def _():
        for ref in (acc_qkv, acc_proj, acc_gain):
            ref[...] = jnp.zeros(ref.shape, F32)

    combine_block(
        window, step, here_ref[1], starts_ref, index_ref[...], bufs, own_bufs, wins, acc
    )
    clear_gaps(padded)
    hat_two, scale_two = norm_parts(hidden_ref[...])
    grad_normed = acc[...]
    acc_gain[...] += jnp.sum(grad_normed * hat_two, axis=0, keepdims=True)
    grad_hidden = dy_ref[...].astype(F32) + norm_back(
        grad_normed, hat_two, scale_two, gain_two_ref[...]
    )
    ghid_ref[...] = grad_hidden
    compact[...] = grad_hidden
    spread_rows(compact, padded)
    grad_attn = padded[...].astype(BF)
    acc_proj[...] += dot_lt(mixed_ref[...], grad_attn)
    grad_mixed = dot_rt(grad_attn, proj_w_ref[...]).astype(BF)
    low = low_half()
    for pair in range(BLOCK_PAIRS):
        rows = slice(PAIR_PAD * pair, PAIR_PAD * (pair + 1))
        for two in range(width // LANES):
            cols = slice(LANES * two, LANES * (two + 1))
            key_cols = slice(width + LANES * two, width + LANES * (two + 1))
            value_cols = slice(2 * width + LANES * two, 2 * width + LANES * (two + 1))
            at = (pair * (width // LANES) + two) * 2 * PAIR_PAD
            dscores[at : at + 2 * PAIR_PAD, :] = dot_rt(
                two_heads(grad_mixed[rows, cols], low), qkv_ref[rows, value_cols]
            )
    for pair in range(BLOCK_PAIRS):
        each = 2 * PAIR_PAD * (width // LANES)
        part = slice(each * pair, each * (pair + 1))
        wide, grad_probs = probs_ref[part, :].astype(F32), dscores[part, :]
        meet = jnp.sum(wide * grad_probs, axis=-1, keepdims=True)
        dscores_low[part, :] = (wide * (grad_probs - meet) * factor_qk).astype(BF)
    for pair in range(BLOCK_PAIRS):
        rows = slice(PAIR_PAD * pair, PAIR_PAD * (pair + 1))
        for two in range(width // LANES):
            cols = slice(LANES * two, LANES * (two + 1))
            key_cols = slice(width + LANES * two, width + LANES * (two + 1))
            value_cols = slice(2 * width + LANES * two, 2 * width + LANES * (two + 1))
            at = (pair * (width // LANES) + two) * 2 * PAIR_PAD
            probs = probs_ref[at : at + 2 * PAIR_PAD, :]
            grad_out = two_heads(grad_mixed[rows, cols], low)
            grad_scores = dscores_low[at : at + 2 * PAIR_PAD, :]
            grad_query = one_row(dot(grad_scores, qkv_ref[rows, key_cols]), low)
            dqkv_ref[rows, cols] = grad_query.astype(BF)
            dqkv_ref[rows, key_cols] = dot_lt(
                grad_scores, two_heads(qkv_ref[rows, cols], low)
            ).astype(BF)
            dqkv_ref[rows, value_cols] = dot_lt(probs, grad_out).astype(BF)
    compact[...] = norm_parts(tok_ref[...].astype(F32))[0] * gain_one_ref[...]
    spread_rows(compact, padded)
    acc_qkv[...] += dot_lt(padded[...].astype(BF), dqkv_ref[...])

    @pl.when(step == pl.num_programs(0) - 1)
    def _():
        cores, sides, layers = groups
        half = acc_qkv.shape[0] * 4 // cores
        tall = half // (sides * layers)

        def piece(row):
            part, at = row // width, row % width
            if part < 3:
                return acc_qkv[at : at + tall, width * part : width * (part + 1)]
            return acc_proj[at : at + tall, :]

        for side in range(sides):
            for layer in range(layers):
                low = (side * layers + layer) * tall
                spot = (side ^ here_ref[1]) * layers + (layer ^ here_ref[2])
                to = pl.ds(pl.multiple_of(spot * tall, tall), tall)
                even, odd = piece(low), piece(half + low)
                own_ref[to, :] = jnp.where(here_ref[0] == 0, even, odd).astype(BF)
                sent_ref[to, :] = jnp.where(here_ref[0] == 0, odd, even).astype(BF)
        gain_one_sum = jnp.sum(acc_qkv[...] * qkv_w_ref[...].astype(F32), axis=-1, keepdims=True)
        lane = lax.broadcasted_iota(jnp.int32, (width, LANES), 1)
        router = sum(ref[...] for ref in router_refs)
        small = jnp.where(lane == experts, gain_one_sum, router).T[: own_ref.shape[0] - half, :]
        row = lax.broadcasted_iota(jnp.int32, small.shape, 0)
        small = jnp.where(row == experts + 1, acc_gain[...], small).astype(BF)
        own_ref[half:, :] = small
        sent_ref[half:, :] = small


def small_rows(experts):
    return 16 * -(-(experts + 2) // 16)


def back(starts, here, groups, index, hidden, tokens, dy, qkv, probs, mixed, gain_one, w_qkv, w_proj, gain_two, downs, own, routers, capacity):
    count, width = tokens.shape
    blocks = count // BLOCK
    experts = starts.shape[0]
    window = window_rows(experts, capacity)
    row = lambda shape: pl.BlockSpec(shape, lambda step, *_: (step, 0))
    cores, sides, layers = groups
    assert cores == 2
    sum_shape = (2 * width + small_rows(experts), width)
    flops = 2 * blocks * BLOCK_PAD * width * (8 * width + 10 * PAIR_PAD)
    return pl.pallas_call(
        functools.partial(back_kernel, window, groups),
        grid_spec=pltpu.PrefetchScalarGridSpec(
            num_scalar_prefetch=2,
            grid=(blocks,),
            in_specs=[
                row((BLOCK, 2)), row((BLOCK, width)), row((BLOCK, width)), row((BLOCK, width)),
                row((BLOCK_PAD, 3 * width)), row((probs.shape[0] // blocks, PAIR_PAD)),
                row((BLOCK_PAD, width)),
                whole((1, width)), whole(w_qkv.shape), whole(w_proj.shape), whole((1, width)),
            ] + [whole((downs[0].shape[0], capacity, width))] * 2 + [whole(own.shape)]
            + [whole((width, LANES))] * 2,
            out_specs=[
                row((BLOCK, width)), row((BLOCK_PAD, 3 * width)), whole(sum_shape), whole(sum_shape),
            ],
            scratch_shapes=[
                pltpu.VMEM((experts * window, width), BF),
                pltpu.VMEM((BLOCK, width), F32),
                pltpu.VMEM((BLOCK, width), F32),
                pltpu.VMEM((BLOCK_PAD, width), F32),
                pltpu.VMEM(w_qkv.shape, F32),
                pltpu.VMEM(w_proj.shape, F32),
                pltpu.VMEM((1, width), F32),
                pltpu.VMEM((probs.shape[0] // blocks, PAIR_PAD), F32),
                pltpu.VMEM((probs.shape[0] // blocks, PAIR_PAD), BF),
            ],
        ),
        out_shape=[
            jax.ShapeDtypeStruct((count, width), F32),
            jax.ShapeDtypeStruct(qkv.shape, BF),
            jax.ShapeDtypeStruct(sum_shape, BF),
            jax.ShapeDtypeStruct(sum_shape, BF),
        ],
        compiler_params=params(),
        cost_estimate=cost(1e12, 4000e6),
        name="back",
    )(
        starts, here, index, hidden, tokens, dy, qkv, probs, mixed, gain_one[None, :], w_qkv,
        w_proj, gain_two[None, :], *downs, own, *routers,
    )


def last_kernel(dqkv_ref, ghid_ref, tok_ref, gain_one_ref, qkv_w_ref, *refs):
    out_ref, compact, padded = refs[-3:]
    for sub in range(tok_ref.shape[0] // BLOCK):
        rows = slice(BLOCK * sub, BLOCK * (sub + 1))
        spread = slice(BLOCK_PAD * sub, BLOCK_PAD * (sub + 1))
        padded[...] = dot_rt(dqkv_ref[spread, :], qkv_w_ref[...])
        gather_rows(padded, compact)
        hat_one, scale_one = norm_parts(tok_ref[rows, :].astype(F32))
        out_ref[rows, :] = ghid_ref[rows, :] + norm_back(
            compact[...], hat_one, scale_one, gain_one_ref[...]
        )


def last(low, high, so_far, dqkv, ghid, tokens, gain_one, w_qkv):
    count, width = tokens.shape
    subs = max(n for n in range(1, LAST_SUBS + 1) if low % n == 0 and high % n == 0)
    row = lambda tall: pl.BlockSpec((tall * subs, width), lambda step: (step + low // subs, 0))
    wide = pl.BlockSpec((BLOCK_PAD * subs, 3 * width), lambda step: (step + low // subs, 0))
    taken = [] if so_far is None else [so_far]
    return pl.pallas_call(
        last_kernel,
        grid=((high - low) // subs,),
        in_specs=[wide, row(BLOCK), row(BLOCK), whole((1, width)), whole(w_qkv.shape)]
        + [pl.BlockSpec(memory_space=pl.ANY)] * len(taken),
        out_specs=row(BLOCK),
        out_shape=jax.ShapeDtypeStruct((count, width), F32),
        scratch_shapes=[pltpu.VMEM((BLOCK, width), F32), pltpu.VMEM((BLOCK_PAD, width), F32)],
        input_output_aliases={5: 0} if taken else {},
        compiler_params=params(),
        cost_estimate=cost(6 * BLOCK_PAD * (high - low) * width * width, 20e6),
        name="last",
    )(dqkv, ghid, tokens, gain_one[None, :], w_qkv, *taken)


def lay_kernel(groups, here_ref, own_ref, other_ref, qkv_ref, proj_ref):
    cores, sides, layers = groups
    tall, width = own_ref.shape[1:]
    each = width // tall

    def fill(core, source):
        for place in range(core * 2 * each, (core + 1) * 2 * each):
            part, turn = divmod(place, each)
            side, layer = divmod(place % (sides * layers), layers)
            spot = (side ^ here_ref[1]) * layers + (layer ^ here_ref[2])
            rows = slice(tall * turn, tall * (turn + 1))
            if part < 3:
                qkv_ref[rows, width * part : width * (part + 1)] = source[spot].astype(F32)
            else:
                proj_ref[rows, :] = source[spot].astype(F32)

    @pl.when(here_ref[0] == 0)
    def _():
        fill(0, own_ref)
        fill(1, other_ref)

    @pl.when(here_ref[0] == 1)
    def _():
        fill(0, other_ref)
        fill(1, own_ref)


def lay(groups, here, own, other):
    width = own.shape[2]
    return pl.pallas_call(
        functools.partial(lay_kernel, groups),
        grid_spec=pltpu.PrefetchScalarGridSpec(
            num_scalar_prefetch=1,
            grid=(1,),
            in_specs=[whole(own.shape)] * 2,
            out_specs=[whole((width, 3 * width)), whole((width, width))],
        ),
        out_shape=[
            jax.ShapeDtypeStruct((width, 3 * width), F32),
            jax.ShapeDtypeStruct((width, width), F32),
        ],
        compiler_params=params(),
        cost_estimate=cost(1e6, 8e6),
        name="lay",
    )(here, own, other)


def unpack_kernel(*refs):
    parts, (up_ref, down_ref) = refs[:-2], refs[-2:]
    tall, width = up_ref.shape[1], down_ref.shape[2]
    for which, part in enumerate(parts):
        up_ref[which] = part[:tall, :].astype(F32)
        for turn in range(down_ref.shape[1] // tall):
            down_ref[which, tall * turn : tall * (turn + 1), :] = (
                part[tall:, width * turn : width * (turn + 1)].astype(F32)
            )


def unpack(parts, width):
    tall, units = parts[0].shape[0] // 2, parts[0].shape[1]
    outs = [
        jax.ShapeDtypeStruct((len(parts), tall, units), F32),
        jax.ShapeDtypeStruct((len(parts), tall * units // width, width), F32),
    ]
    return pl.pallas_call(
        unpack_kernel,
        grid=(1,),
        in_specs=[whole(part.shape) for part in parts],
        out_specs=[whole(out.shape) for out in outs],
        out_shape=outs,
        compiler_params=params(),
        cost_estimate=cost(1e6, 4e6),
        name="unpack",
    )(*parts)


def jump(value, axis, far):
    size = lax.axis_size(axis)
    return lax.ppermute(value, axis, [(at, at ^ far) for at in range(size)])


def merge_kernel(cuts, extra, count, *refs):
    parts, outs = refs[:count], refs[count:]
    tall = (parts[0].shape[0] - extra) // cuts

    def total(rows):
        value = parts[0][rows, :].astype(F32)
        for part in parts[1:]:
            value = value + part[rows, :].astype(F32)
        return value

    small = total(slice(cuts * tall, None))
    for cut, out in enumerate(outs):
        if cut == cuts:
            out[...] = small
            continue
        out[:tall, :] = total(slice(cut * tall, (cut + 1) * tall)).astype(BF)
        if out.shape[0] > tall:
            out[tall:, :] = small.astype(BF)


def merge(parts, cuts, extra, ends):
    rows, width = parts[0].shape
    tall = (rows - extra) // cuts
    if ends:
        outs = [jax.ShapeDtypeStruct((tall, width), BF), jax.ShapeDtypeStruct((extra, width), F32)]
    else:
        outs = [jax.ShapeDtypeStruct((tall + extra, width), BF)] * cuts
    return pl.pallas_call(
        functools.partial(merge_kernel, cuts, extra, len(parts)),
        grid=(1,),
        in_specs=[whole((rows, width))] * len(parts),
        out_specs=[whole(out.shape) for out in outs],
        out_shape=outs,
        compiler_params=params(),
        cost_estimate=cost(1e6, 4e6),
        name="merge",
    )(*parts)


def after(value, *others):
    return lax.optimization_barrier((value, *others))[0]


def sum_over_all(own, sent, groups, extra, arrived, beside):
    cores, sides, layers = groups
    beside = iter(beside)

    def spread(own, sent, axis, scale):
        came = [jump(part, axis, scale * far) for far, part in enumerate(sent, 1)]
        return [own] + list(after(tuple(came), next(beside)(own)))

    half = merge([own, jump(sent, "dp", 1)], sides, extra, False)
    half = list(after(tuple(half), arrived))
    flat = merge(spread(half[0], half[1:], "expert", 1), layers, extra, False)
    spot, small = merge(spread(flat[0], flat[1:], "dp", cores), 1, extra, True)
    flat = jnp.stack(spread(spot, [spot] * (layers - 1), "dp", cores))
    half = jnp.stack(spread(flat, [flat] * (sides - 1), "expert", 1))
    half = half.reshape(sides * layers, *spot.shape)
    return half, jump(half, "dp", 1), small


def per_device(
    tokens, gain_one, w_qkv, w_proj, gain_two, w_router, w_in, w_eout, picks, keep, grad_out
):
    count, width = tokens.shape
    local = w_in.shape[0]
    assert local == 2
    owners = lax.axis_size("expert")
    shards = lax.axis_size("dp")
    experts = local * owners
    capacity = 8 * ((21 * count + 80 * experts - 1) // (80 * experts))
    me, row = lax.axis_index("expert"), lax.axis_index("dp")
    cores = 2
    groups = (cores, owners, shards // cores)
    here = jnp.stack([row % cores, me, row // cores]).astype(jnp.int32)

    def swap(sent):
        return lax.all_to_all(sent, "expert", split_axis=0, concat_axis=0, tiled=True)

    index_rows, starts = places(picks, keep, experts, local, capacity)
    send = lambda srcs, *plan: dispatch(srcs, starts, index_rows, owners, capacity, plan)
    (dy_first,) = send([grad_out], (0, (0,)))
    got = swap(dy_first)
    hidden, rows, qkv, probs, mixed = attend(
        after(tokens, dy_first), gain_one, w_qkv, w_proj, gain_two
    )
    (x_first,) = send([rows], (0, (0,)))
    arrived = [[(swap(after(x_first, got)), 0), (got, 0)]]
    kept = [[(x_first, 0), (dy_first, 0)]]
    others = send([after(rows, x_first), grad_out], *[(part, (0, 1)) for part in range(1, local)])
    for sent in others:
        got = swap(after(sent, arrived[-1][0][0]))
        arrived.append([(got, 0), (got, 1)])
        kept.append([(sent, 0), (sent, 1)])
    index = index_rows.transpose(0, 2, 1).reshape(count, 2)
    head = w_router.astype(BF)
    rest = (w_router - head.astype(F32)).astype(BF)
    gap = ((0, 0), (0, LANES - experts))
    router = jnp.concatenate([jnp.pad(head, gap), jnp.pad(rest, gap)], axis=1)
    router_back = jnp.concatenate([jnp.pad(head, gap).T, jnp.pad(rest, gap).T], axis=0)
    early = 16 * (capacity // 39)
    weights = (w_in, w_eout, router, router_back)

    def one(part, own, given, before, *taken):
        mine = jnp.stack([me * local + part, me]).astype(jnp.int32)
        came = (kept if own else arrived)[part]
        taken = dict(zip(range(2 - len(taken), 2), taken))
        return expert_pass(
            part, mine, *came, weights, early, experts, capacity, shards, own, given, before, taken
        )

    def reduce(grad):
        grad = grad.reshape(shards * grad.shape[1], grad.shape[2])
        return lax.psum_scatter(grad, "dp", scatter_dimension=0, tiled=True)

    head, tail, *given = one(0, True, [], None)
    head, tail, grad, router_first = one(0, False, given, None, head, tail)
    sums, tail_first = [reduce(grad)], tail
    head = swap(after(head, got))
    down, tail, *given = one(1, False, [], tail_first)
    down = swap(after(down, head))
    own_down, own_out, grad, router_second = one(1, True, given, None)
    sums.append(reduce(grad))
    tail = swap(after(tail, down))
    grad_hidden, dqkv, own, sent = back(
        starts, here, groups, index, hidden, tokens, grad_out, qkv, probs, mixed, gain_one,
        w_qkv, w_proj, gain_two, [head, down], own_down, [router_first, router_second], capacity,
    )
    blocks = count // BLOCK
    some = blocks // 3

    def make_top(tie):
        return top(
            starts, here, index, after(hidden, tie), head, tail, tail_first, own_out, early, capacity
        )

    def make_unpack(tie):
        return unpack(after(tuple(sums), tie), width)

    def make_last(low, high, tie, so_far=None):
        return last(
            low, high, so_far, after(dqkv, tie), grad_hidden, tokens, gain_one, w_qkv
        )

    made = {}

    def beside(name, work):
        def go(tie):
            made[name] = work(tie)
            return jax.tree.leaves(made[name])[0]

        return go

    own, other, small = sum_over_all(
        own, sent, groups, small_rows(experts), tail,
        [
            beside("top", make_top),
            beside("unpack", make_unpack),
            beside("some", lambda tie: make_last(0, some, tie)),
            beside("last", lambda tie: make_last(some, blocks, tie, made["some"])),
        ],
    )
    block_out, grad_tokens, (grad_in, grad_eout) = made["top"], made["last"], made["unpack"]
    grad_qkv, grad_proj = lay(groups, here, own, other)
    return (
        block_out,
        grad_tokens,
        small[experts] / gain_one,
        grad_qkv,
        grad_proj,
        small[experts + 1],
        small[:experts].T,
        grad_in,
        grad_eout,
    )


def solution(mesh):
    rows = P(("dp", "expert"), None)
    experts = P("expert", None, None)
    return jax.shard_map(
        per_device,
        mesh=mesh,
        in_specs=(rows, P(), P(), P(), P(), P(), experts, experts, rows, rows, rows),
        out_specs=(
            rows, rows, P(), P(), P(), P(), P(), P("expert", "dp", None), P("expert", "dp", None),
        ),
        check_vma=False,
    )
```

```python
import functools

import jax
import jax.numpy as jnp
from jax import lax
from jax.experimental import pallas as pl
from jax.experimental.pallas import tpu as pltpu
from jax.sharding import PartitionSpec as P

HEADS = 8
PATCHES = 49
LANES = 128
PAIR = 2 * PATCHES
PAIR_PAD = 112
BLOCK_PAIRS = 4
BLOCK = BLOCK_PAIRS * PAIR
BLOCK_PAD = BLOCK_PAIRS * PAIR_PAD
BF = jnp.bfloat16
F32 = jnp.float32
VMEM_BYTES = 62 * 1024 * 1024
VMEM_ALL = 64 * 1024 * 1024 - 32 * 1024
FCUT = 256
CHUNK = 256
TOP_SUBS, SEND_SUBS, LAST_SUBS = 2, 2, 2


def params(grant=VMEM_BYTES):
    return pltpu.CompilerParams(
        dimension_semantics=("arbitrary",), vmem_limit_bytes=grant
    )


def cost(flops, moved, special=0):
    return pl.CostEstimate(
        flops=int(flops), bytes_accessed=int(moved), transcendentals=int(special)
    )


def step_blocks(blocks, most):
    return max(n for n in range(1, most + 1) if blocks % n == 0)


def whole(shape):
    return pl.BlockSpec(shape, lambda *_: (0,) * len(shape))


def dot(left, right):
    return jnp.dot(left, right, preferred_element_type=F32)


def dot_rt(left, right):
    return lax.dot_general(left, right, (((1,), (1,)), ((), ())), preferred_element_type=F32)


def dot_lt(left, right):
    return lax.dot_general(left, right, (((0,), (0,)), ((), ())), preferred_element_type=F32)


def norm_parts(values):
    mean = jnp.mean(values, axis=-1, keepdims=True)
    cent = values - mean
    factor = lax.rsqrt(jnp.mean(cent * cent, axis=-1, keepdims=True) + 1e-06)
    return cent * factor, factor


def norm_back(grad_normed, normed_hat, factor, gain):
    grad_hat = grad_normed * gain
    inner = grad_hat - jnp.mean(grad_hat, axis=-1, keepdims=True)
    inner = inner - normed_hat * jnp.mean(grad_hat * normed_hat, axis=-1, keepdims=True)
    return factor * inner


def spread_rows(compact, padded):
    for pair in range(BLOCK_PAIRS):
        padded[PAIR_PAD * pair : PAIR_PAD * pair + PAIR] = compact[PAIR * pair : PAIR * pair + PAIR]


def gather_rows(padded, compact):
    for pair in range(BLOCK_PAIRS):
        compact[PAIR * pair : PAIR * pair + PAIR] = padded[PAIR_PAD * pair : PAIR_PAD * pair + PAIR]


def clear_gaps(padded):
    for pair in range(BLOCK_PAIRS):
        low = PAIR_PAD * pair + PAIR
        padded[low : low + PAIR_PAD - PAIR] = jnp.zeros((PAIR_PAD - PAIR, padded.shape[1]), F32)


def image_of(position):
    return (position >= PATCHES).astype(jnp.int32) + (position >= PAIR).astype(jnp.int32)


def same_image():
    rows = lax.broadcasted_iota(jnp.int32, (2 * PAIR_PAD, PAIR_PAD), 0)
    rows = jnp.where(rows >= PAIR_PAD, rows - PAIR_PAD, rows)
    cols = lax.broadcasted_iota(jnp.int32, (2 * PAIR_PAD, PAIR_PAD), 1)
    return image_of(rows) == image_of(cols)


def low_half():
    return lax.broadcasted_iota(jnp.int32, (PAIR_PAD, LANES), 1) < LANES // 2


def two_heads(values, low):
    zero = jnp.zeros_like(values)
    return jnp.concatenate([jnp.where(low, values, zero), jnp.where(low, zero, values)], axis=0)


def one_row(values, low):
    return jnp.where(low, values[:PAIR_PAD], values[PAIR_PAD:])


def attend_kernel(
    tok_ref, gain_one_ref, qkv_w_ref, proj_w_ref, gain_two_ref,
    hidden_ref, rows_ref, qkv_ref, probs_ref, mixed_ref,
    compact, padded, scores,
):
    width = tok_ref.shape[1]
    factor_qk = (width // HEADS) ** (-0.5)
    clear_gaps(padded)
    inputs = tok_ref[...].astype(F32)
    compact[...] = norm_parts(inputs)[0] * gain_one_ref[...]
    spread_rows(compact, padded)
    qkv_ref[...] = dot(padded[...].astype(BF), qkv_w_ref[...]).astype(BF)
    valid = same_image()
    low = low_half()
    for pair in range(BLOCK_PAIRS):
        rows = slice(PAIR_PAD * pair, PAIR_PAD * (pair + 1))
        for two in range(width // LANES):
            cols = slice(LANES * two, LANES * (two + 1))
            query = qkv_ref[rows, cols]
            keys = qkv_ref[rows, width + LANES * two : width + LANES * (two + 1)]
            step = (pair * (width // LANES) + two) * 2 * PAIR_PAD
            scores[step : step + 2 * PAIR_PAD, :] = jnp.where(
                valid, dot_rt(two_heads(query, low), keys), -1e30
            )
    for pair in range(BLOCK_PAIRS):
        each = 2 * PAIR_PAD * (width // LANES)
        part = slice(each * pair, each * (pair + 1))
        logits = scores[part, :]
        highest = jnp.max(logits, axis=-1, keepdims=True)
        expo = jnp.exp((logits - highest) * factor_qk)
        probs_ref[part, :] = (expo / jnp.sum(expo, axis=-1, keepdims=True)).astype(BF)
    for pair in range(BLOCK_PAIRS):
        rows = slice(PAIR_PAD * pair, PAIR_PAD * (pair + 1))
        for two in range(width // LANES):
            cols = slice(LANES * two, LANES * (two + 1))
            values = qkv_ref[rows, 2 * width + LANES * two : 2 * width + LANES * (two + 1)]
            step = (pair * (width // LANES) + two) * 2 * PAIR_PAD
            probs = probs_ref[step : step + 2 * PAIR_PAD, :]
            mixed_ref[rows, cols] = one_row(dot(probs, values), low).astype(BF)
    padded[...] = dot(mixed_ref[...], proj_w_ref[...])
    gather_rows(padded, compact)
    hidden = inputs + compact[...]
    hidden_ref[...] = hidden
    rows_ref[...] = (norm_parts(hidden)[0] * gain_two_ref[...]).astype(BF)


def attend(tokens, gain_one, w_qkv, w_proj, gain_two):
    count, width = tokens.shape
    blocks = count // BLOCK
    prob_rows = BLOCK_PAIRS * (width // LANES) * 2 * PAIR_PAD
    row = lambda shape: pl.BlockSpec(shape, lambda step: (step, 0))
    flops = 2 * blocks * BLOCK_PAD * width * (4 * width + 4 * PAIR_PAD)
    return pl.pallas_call(
        attend_kernel,
        grid=(blocks,),
        in_specs=[
            row((BLOCK, width)), whole((1, width)), whole(w_qkv.shape), whole(w_proj.shape),
            whole((1, width)),
        ],
        out_specs=[
            row((BLOCK, width)), row((BLOCK, width)), row((BLOCK_PAD, 3 * width)),
            row((prob_rows, PAIR_PAD)), row((BLOCK_PAD, width)),
        ],
        out_shape=[
            jax.ShapeDtypeStruct((count, width), F32),
            jax.ShapeDtypeStruct((count, width), BF),
            jax.ShapeDtypeStruct((blocks * BLOCK_PAD, 3 * width), BF),
            jax.ShapeDtypeStruct((blocks * prob_rows, PAIR_PAD), BF),
            jax.ShapeDtypeStruct((blocks * BLOCK_PAD, width), BF),
        ],
        scratch_shapes=[
            pltpu.VMEM((BLOCK, width), F32), pltpu.VMEM((BLOCK_PAD, width), F32),
            pltpu.VMEM((prob_rows, PAIR_PAD), F32),
        ],
        compiler_params=params(),
        cost_estimate=cost(flops, 30e6, blocks * prob_rows * LANES),
        name="attend",
    )(tokens, gain_one[None, :], w_qkv, w_proj, gain_two[None, :])


def place_kernel(local, capacity, picks_ref, keep_ref, index_ref, starts_ref):
    blocks, _, block = index_ref.shape
    experts = starts_ref.shape[0]
    owners = experts // local
    row = lax.broadcasted_iota(jnp.int32, (experts, block), 0)
    ids = row * local
    for part in range(1, local):
        ids = jnp.where(row >= owners * part, (row - owners * part) * local + part, ids)
    earlier = lax.broadcasted_iota(jnp.int32, (block, block), 0) < lax.broadcasted_iota(
        jnp.int32, (block, block), 1
    )
    earlier = earlier.astype(F32).astype(BF)
    base = (row * capacity).astype(F32)
    lane = lax.broadcasted_iota(jnp.int32, (experts, LANES), 1)
    starts = jnp.zeros((experts, LANES), jnp.int32)
    carry = jnp.zeros((experts, 1), F32)
    for step in range(blocks):
        cols = slice(block * step, block * (step + 1))
        names = [picks_ref[c : c + 1, cols] == ids for c in (0, 1)]
        named = (names[0] | names[1]).astype(F32)
        spot = base + (dot(named.astype(BF), earlier) + carry)
        for c in (0, 1):
            found = jnp.sum(jnp.where(names[c], spot, 0.0), axis=0, keepdims=True)
            index_ref[step, c : c + 1, :] = jnp.where(
                keep_ref[c : c + 1, cols] > 0, found.astype(jnp.int32), -1
            )
        carry = carry + jnp.sum(named, axis=1, keepdims=True)
        starts = jnp.where(lane == step + 1, carry.astype(jnp.int32), starts)
    starts_ref[...] = starts


def places(picks, keep, experts, local, capacity):
    count = picks.shape[0]
    outs = [
        jax.ShapeDtypeStruct((count // BLOCK, 2, BLOCK), jnp.int32),
        jax.ShapeDtypeStruct((experts, LANES), jnp.int32),
    ]
    return pl.pallas_call(
        functools.partial(place_kernel, local, capacity),
        grid=(1,),
        in_specs=[whole((2, count))] * 2,
        out_specs=[whole(out.shape) for out in outs],
        out_shape=outs,
        compiler_params=params(),
        cost_estimate=cost(1e8, 1e5),
        name="places",
    )(picks.T, keep.T)


def window_rows(experts, capacity):
    return min(capacity, 1024 // experts)


def window_at(starts_ref, expert, step, turn, window, capacity):
    low = starts_ref[expert, step]
    begin = (low // 16) * 16 + turn * window
    at = pl.multiple_of(jnp.minimum(begin, capacity - window), 16)
    return begin, starts_ref[expert, step + 1], at


def turns(starts_ref, step, experts, window):
    most = 0
    for expert in experts:
        low = (starts_ref[expert, step] // 16) * 16
        most = jnp.maximum(most, (starts_ref[expert, step + 1] - low + window - 1) // window)
    return most


def dispatch_kernel(window, capacity, plan, sources, starts_ref, index_ref, *refs):
    src_refs, outs, (spots, got) = refs[:sources], refs[sources:-2], refs[-2:]
    owners = outs[0].shape[0]
    named = [owners * part + owner for part, _ in plan for owner in range(owners)]
    subs = index_ref.shape[0]

    @pl.when(pl.program_id(0) == 0)
    def _():
        for out in outs:
            out[...] = jnp.zeros(out.shape, out.dtype)

    place = lax.broadcasted_iota(jnp.int32, (window, index_ref.shape[2]), 0)
    for sub in range(subs):
        step = pl.program_id(0) * subs + sub
        block = slice(BLOCK * sub, BLOCK * (sub + 1))
        first, second = index_ref[sub, 0:1, :], index_ref[sub, 1:2, :]

        def one_turn(turn, carry):
            for (part, used), out in zip(plan, outs):
                spans = []
                for owner in range(owners):
                    expert = part * owners + owner
                    begin, _, at = window_at(starts_ref, expert, step, turn, window, capacity)
                    shift = expert * capacity
                    near = jnp.where(first >= shift + begin, first - (shift + at), -1)
                    far = jnp.where(second >= shift + begin, second - (shift + at), -1)
                    hit = jnp.where((near >= 0) & (near < window), near, far)
                    spots[window * owner : window * (owner + 1), :] = (
                        (place == hit).astype(F32).astype(BF)
                    )
                    spans.append(at)
                for order, which in enumerate(used):
                    got[...] = dot(spots[...], src_refs[which][block, :])
                    for owner, at in enumerate(spans):
                        rows = pl.ds(pl.multiple_of(at + order * capacity, 16), window)
                        held = out[owner, rows, :].astype(F32)
                        out[owner, rows, :] = (
                            held + got[window * owner : window * (owner + 1), :]
                        ).astype(BF)
            return carry

        lax.fori_loop(0, turns(starts_ref, step, named, window), one_turn, 0)


def dispatch(srcs, starts, index_rows, owners, capacity, plan):
    count, width = srcs[0].shape
    subs = step_blocks(count // BLOCK, SEND_SUBS)
    window = window_rows(starts.shape[0], capacity)
    shapes = [(owners, len(used) * capacity, width) for _, used in plan]
    return pl.pallas_call(
        functools.partial(dispatch_kernel, window, capacity, plan, len(srcs)),
        grid_spec=pltpu.PrefetchScalarGridSpec(
            num_scalar_prefetch=1,
            grid=(count // BLOCK // subs,),
            in_specs=[pl.BlockSpec((subs, 2, BLOCK), lambda step, *_: (step, 0, 0))]
            + [pl.BlockSpec((BLOCK * subs, width), lambda step, *_: (step, 0))] * len(srcs),
            out_specs=[whole(shape) for shape in shapes],
            scratch_shapes=[
                pltpu.VMEM((owners * window, BLOCK), BF),
                pltpu.VMEM((owners * window, width), F32),
            ],
        ),
        out_shape=[jax.ShapeDtypeStruct(shape, BF) for shape in shapes],
        compiler_params=params(),
        cost_estimate=cost(6e9, 8e6),
        name="dispatch",
    )(starts, index_rows, *srcs)


def combine_block(window, step, me, starts_ref, index, bufs, own_bufs, wins, acc):
    owners, capacity = bufs[0].shape[:2]
    experts = owners * len(bufs)
    lane = lax.broadcasted_iota(jnp.int32, (1, experts * window), 1)
    acc[...] = jnp.zeros(acc.shape, F32)

    def one_turn(turn, carry):
        seen = jnp.full((1, experts * window), -2, jnp.int32)
        for expert in range(experts):
            part, owner = expert // owners, expert % owners
            begin, high, at = window_at(starts_ref, expert, step, turn, window, capacity)
            slot = lane + (at - expert * window)
            fresh = (slot >= begin) & (slot < high)
            mine = (lane >= expert * window) & (lane < (expert + 1) * window)
            seen = jnp.where(mine & fresh, slot + expert * capacity, seen)
            to = slice(window * expert, window * (expert + 1))
            if own_bufs[part] is None:
                wins[to, :] = bufs[part][owner, pl.ds(at, window), :]
            else:
                wins[to, :] = jnp.where(
                    me == owner, own_bufs[part][0, pl.ds(at, window), :],
                    bufs[part][owner, pl.ds(at, window), :],
                )
        total = acc[...]
        for low in range(0, experts * window, CHUNK):
            part = slice(low, min(low + CHUNK, experts * window))
            hit = (index[:, 0:1] == seen[:, part]) | (index[:, 1:2] == seen[:, part])
            total = total + dot(hit.astype(F32).astype(BF), wins[part, :])
        acc[...] = total
        return carry

    lax.fori_loop(0, turns(starts_ref, step, range(experts), window), one_turn, 0)


def top_kernel(early, starts_ref, here_ref, index_ref, hidden_ref, head_ref, tail_ref, own_first_ref, own_second_ref, out_ref, first, second, wins, acc, sems):
    step = pl.program_id(0)
    experts = starts_ref.shape[0]
    window, capacity = wins.shape[0] // experts, first.shape[1]
    late = capacity - early

    @pl.when(step == 0)
    def _():
        me, owners = here_ref[1], first.shape[0]

        def move(go):
            go(pltpu.make_async_copy(
                head_ref.at[:, pl.ds(capacity, early), :], first.at[:, pl.ds(0, early), :], sems.at[0]
            ))
            for owner in range(owners):
                to_first = first.at[owner, pl.ds(early, late), :]
                one, two = sems.at[1 + owner], sems.at[1 + owners + owner]

                @pl.when(me == owner)
                def _():
                    go(pltpu.make_async_copy(own_first_ref.at[owner], to_first, one))
                    go(pltpu.make_async_copy(own_second_ref.at[0], second.at[owner], two))

                @pl.when(me != owner)
                def _():
                    go(pltpu.make_async_copy(tail_ref.at[owner, pl.ds(0, late), :], to_first, one))
                    go(pltpu.make_async_copy(
                        tail_ref.at[owner, pl.ds(late, capacity), :], second.at[owner], two
                    ))

        move(lambda copy: copy.start())
        move(lambda copy: copy.wait())

    subs = hidden_ref.shape[0] // BLOCK
    for sub in range(subs):
        rows = slice(BLOCK * sub, BLOCK * (sub + 1))
        combine_block(
            window, step * subs + sub, 0, starts_ref, index_ref[rows, :], [first, second],
            [None, None], wins, acc,
        )
        out_ref[rows, :] = (hidden_ref[rows, :] + acc[...]).astype(BF)


def top(starts, here, index, hidden, head, tail, own_first, own_second, early, capacity):
    count, width = hidden.shape
    experts = starts.shape[0]
    window = window_rows(experts, capacity)
    row = lambda shape: pl.BlockSpec(shape, lambda step, *_: (step, 0))
    tall = BLOCK * step_blocks(count // BLOCK, TOP_SUBS)
    held = pltpu.VMEM((head.shape[0], capacity, width), BF)
    return pl.pallas_call(
        functools.partial(top_kernel, early),
        grid_spec=pltpu.PrefetchScalarGridSpec(
            num_scalar_prefetch=2,
            grid=(count // tall,),
            in_specs=[row((tall, 2)), row((tall, width))] + [pl.BlockSpec(memory_space=pl.ANY)] * 4,
            out_specs=pl.BlockSpec((tall, width), lambda step, *_: (step, 0)),
            scratch_shapes=[
                held, held, pltpu.VMEM((experts * window, width), BF),
                pltpu.VMEM((BLOCK, width), F32), pltpu.SemaphoreType.DMA((1 + 2 * head.shape[0],)),
            ],
        ),
        out_shape=jax.ShapeDtypeStruct((count, width), BF),
        compiler_params=params(),
        cost_estimate=cost(6e9, 12e6),
        name="top",
    )(starts, here, index, hidden, head, tail, own_first, own_second)


def gelu_parts(values):
    size = 1.0 + (0.3275911 * 0.7071067811865476) * jnp.abs(values)
    near = pl.reciprocal(size, approx=True)
    near = near * (2.0 - size * near)
    expo = jnp.exp2((-0.5 * 1.4426950408889634) * (values * values))
    poly = 0.5 * 1.061405429
    for term in (-1.453152027, 1.421413741, -0.284496736, 0.254829592):
        poly = poly * near + 0.5 * term
    tail = poly * near * expo
    share = jnp.where(values >= 0, 1.0 - tail, tail)
    return values * share, share + values * (0.3989422804014327 * expo)


def expert_kernel(
    experts, fcut, begun, part, joins, mine_ref, up_ref, down_ref, router_ref, back_ref, x_ref, dy_ref, *refs
):
    given, refs = refs[: 3 * begun], refs[3 * begun :]
    if joins:
        before_ref, refs = refs[0], refs[1:]
    *grad_refs, grouter_ref = refs[2:-5]
    acc_up, acc_down, acc_router, acc_out, acc_dx = refs[-5:]
    step = pl.program_id(0)
    hidden_units = up_ref.shape[1]
    _, capacity, width = x_ref.shape
    count = capacity

    @pl.when(step == 0)
    def _():
        if begun:
            acc_up[...] = given[0][...].astype(F32)
            acc_down[...] = given[1][...].astype(F32)
            acc_router[:, :LANES] = given[2][...]
            acc_router[:, LANES:] = jnp.zeros((width, LANES), F32)
        else:
            acc_up[...] = jnp.zeros(acc_up.shape, F32)
            acc_down[...] = jnp.zeros(acc_down.shape, F32)
            acc_router[...] = jnp.zeros(acc_router.shape, F32)

    rows = x_ref[...].reshape(count, width)
    logits = dot(rows, router_ref[...])
    logits = logits[:, :LANES] + logits[:, LANES:]
    lane = lax.broadcasted_iota(jnp.int32, (count, LANES), 1)
    logits = jnp.where(lane < experts, logits, -1e30)
    expo = jnp.exp(logits - jnp.max(logits, axis=-1, keepdims=True))
    gates = expo / jnp.sum(expo, axis=-1, keepdims=True)
    own = (lane == mine_ref[0]).astype(F32)
    chosen = jnp.sum(gates * own, axis=-1, keepdims=True)
    pair = (chosen * dy_ref[...].reshape(count, width).astype(F32)).astype(BF)
    rows_t = rows.T
    pair_t = pair.T
    chunks = [slice(low, low + fcut) for low in range(0, hidden_units, fcut)]
    ahead = lambda cols: (dot(rows, up_ref[:, cols]), dot_rt(pair, down_ref[cols, :]))
    ready = ahead(chunks[0])
    for turn, cols in enumerate(chunks):
        pre, grad_act = ready
        if turn + 1 < len(chunks):
            ready = ahead(chunks[turn + 1])
        act, slope = gelu_parts(pre)
        act = act.astype(BF)
        grad_pre = (grad_act * slope).astype(BF)
        acc_up[:, cols] += dot(rows_t, grad_pre)
        acc_down[:, cols] += dot(pair_t, act)
        if turn == 0:
            acc_out[...] = dot(act, down_ref[cols, :])
            acc_dx[...] = dot_rt(grad_pre, up_ref[:, cols])
        else:
            acc_out[...] += dot(act, down_ref[cols, :])
            acc_dx[...] += dot_rt(grad_pre, up_ref[:, cols])
    inner = jnp.sum(acc_out[...] * pair.astype(F32), axis=-1, keepdims=True)
    grad_logits = inner * (own - gates)
    head = grad_logits.astype(BF)
    rest = (grad_logits - head.astype(F32)).astype(BF)
    acc_router[...] += dot(rows_t, jnp.concatenate([head, rest], axis=1))
    out = (chosen * acc_out[...]).astype(BF)
    grad_rows = (acc_dx[...] + dot(jnp.concatenate([head, head], axis=1), back_ref[...])).astype(BF)
    if part:
        refs[0][0] = grad_rows
        late = refs[1].shape[1] - capacity
        if late:
            refs[1][0, :late, :] = before_ref[0]
        refs[1][0, late:, :] = out
    else:
        early = refs[0].shape[1] - capacity
        refs[0][0, :capacity, :] = grad_rows
        refs[0][0, capacity:, :] = out[:early]
        refs[1][0] = out[early:]

    @pl.when(step == pl.num_programs(0) - 1)
    def _():
        grouter_ref[...] = acc_router[:, :LANES] + acc_router[:, LANES:]
        if not begun:
            grad_refs[0][...] = acc_up[...].astype(BF)
            grad_refs[1][...] = acc_down[...].astype(BF)
            return
        grad_ref = grad_refs[0]
        shards, tall, _ = grad_ref.shape
        up_rows, down_rows = width // shards, hidden_units // shards
        piece = tall - up_rows
        for shard in range(shards):
            grad_ref[shard, :up_rows, :] = acc_up[up_rows * shard : up_rows * (shard + 1), :].astype(BF)
            turned = acc_down[:, down_rows * shard : down_rows * (shard + 1)].T.astype(BF)
            for part in range(down_rows // piece):
                grad_ref[shard, up_rows:, width * part : width * (part + 1)] = (
                    turned[piece * part : piece * (part + 1), :]
                )


def expert_pass(part, mine, rows, grads, weights, early, experts, capacity, shards, own, given, before, taken):
    (rows, rows_at), (grads, grads_at) = rows, grads
    w_up, w_down, router, router_back = weights
    sources, _, width = rows.shape
    units = w_up.shape[2]
    source = lambda step, mine_ref: (mine_ref[1] + (0 if own else 1) + step) % sources
    block = lambda tall, at: pl.BlockSpec(
        (1, tall, width), lambda step, mine_ref: (source(step, mine_ref), at, 0)
    )
    weight = lambda shape: pl.BlockSpec((None,) + shape[1:], lambda *_: (part, 0, 0))
    late = capacity - early
    talls = [capacity, late + capacity] if part else [capacity + early, late]
    sent = [jax.ShapeDtypeStruct((sources, tall, width), BF) for tall in talls]
    sent_specs = [block(tall, 0) for tall in talls]
    if part and own:
        sent = [jax.ShapeDtypeStruct((1, capacity, width), BF)] * 2
        sent_specs = [whole((1, capacity, width))] * 2
    if given:
        sums = [jax.ShapeDtypeStruct((shards, width // shards * 2, units), BF)]
    else:
        sums = [jax.ShapeDtypeStruct((width, units), BF)] * 2
    sums.append(jax.ShapeDtypeStruct((width, LANES), F32))
    steps = 1 if own else sources - 1
    joins = bool(part) and not own
    more = list(given) + ([before] if joins else [])
    more_specs = [whole(array.shape) for array in given] + ([block(late, 0)] if joins else [])
    skip = 7 + len(more)

    def body(*refs):
        expert_kernel(
            experts, min(FCUT, units), bool(given), part, joins, *refs[:skip], *refs[skip + len(taken) :]
        )

    return pl.pallas_call(
        body,
        grid_spec=pltpu.PrefetchScalarGridSpec(
            num_scalar_prefetch=1,
            grid=(steps,),
            in_specs=[
                weight(w_up.shape), weight(w_down.shape), whole(router.shape),
                whole(router_back.shape), block(capacity, rows_at), block(capacity, grads_at),
            ] + more_specs + [pl.BlockSpec(memory_space=pl.ANY)] * len(taken),
            out_specs=sent_specs + [whole(array.shape) for array in sums],
            scratch_shapes=[
                pltpu.VMEM((width, units), F32),
                pltpu.VMEM((width, units), F32),
                pltpu.VMEM((width, 2 * LANES), F32),
                pltpu.VMEM((capacity, width), F32),
                pltpu.VMEM((capacity, width), F32),
            ],
        ),
        out_shape=sent + sums,
        input_output_aliases={skip + at: to for at, to in enumerate(taken)},
        compiler_params=params(),
        cost_estimate=cost(
            20 * steps * capacity * width * units, 30e6, 2 * steps * capacity * units
        ),
        name="expert_own" if own else "expert_others",
    )(mine, *weights, rows, grads, *more, *taken.values())


def back_kernel(
    window, groups, starts_ref, here_ref, index_ref, hidden_ref, tok_ref, dy_ref, qkv_ref,
    probs_ref, mixed_ref, gain_one_ref, qkv_w_ref, proj_w_ref, gain_two_ref, *refs,
):
    bufs, own_bufs, router_refs = refs[:2], [None, refs[2]], refs[3:5]
    ghid_ref, dqkv_ref, own_ref, sent_ref = refs[5:-9]
    wins, acc, compact, padded, acc_qkv, acc_proj, acc_gain, dscores, dscores_low = refs[-9:]
    experts = starts_ref.shape[0]
    step = pl.program_id(0)
    width = tok_ref.shape[1]
    factor_qk = (width // HEADS) ** (-0.5)

    @pl.when(step == 0)
    def _():
        for ref in (acc_qkv, acc_proj, acc_gain):
            ref[...] = jnp.zeros(ref.shape, F32)

    combine_block(
        window, step, here_ref[1], starts_ref, index_ref[...], bufs, own_bufs, wins, acc
    )
    clear_gaps(padded)
    hat_two, scale_two = norm_parts(hidden_ref[...])
    grad_normed = acc[...]
    acc_gain[...] += jnp.sum(grad_normed * hat_two, axis=0, keepdims=True)
    grad_hidden = dy_ref[...].astype(F32) + norm_back(
        grad_normed, hat_two, scale_two, gain_two_ref[...]
    )
    ghid_ref[...] = grad_hidden
    compact[...] = grad_hidden
    spread_rows(compact, padded)
    grad_attn = padded[...].astype(BF)
    acc_proj[...] += dot_lt(mixed_ref[...], grad_attn)
    grad_mixed = dot_rt(grad_attn, proj_w_ref[...]).astype(BF)
    low = low_half()
    for pair in range(BLOCK_PAIRS):
        rows = slice(PAIR_PAD * pair, PAIR_PAD * (pair + 1))
        for two in range(width // LANES):
            cols = slice(LANES * two, LANES * (two + 1))
            key_cols = slice(width + LANES * two, width + LANES * (two + 1))
            value_cols = slice(2 * width + LANES * two, 2 * width + LANES * (two + 1))
            at = (pair * (width // LANES) + two) * 2 * PAIR_PAD
            dscores[at : at + 2 * PAIR_PAD, :] = dot_rt(
                two_heads(grad_mixed[rows, cols], low), qkv_ref[rows, value_cols]
            )
    for pair in range(BLOCK_PAIRS):
        each = 2 * PAIR_PAD * (width // LANES)
        part = slice(each * pair, each * (pair + 1))
        wide, grad_probs = probs_ref[part, :].astype(F32), dscores[part, :]
        meet = jnp.sum(wide * grad_probs, axis=-1, keepdims=True)
        dscores_low[part, :] = (wide * (grad_probs - meet) * factor_qk).astype(BF)
    for pair in range(BLOCK_PAIRS):
        rows = slice(PAIR_PAD * pair, PAIR_PAD * (pair + 1))
        for two in range(width // LANES):
            cols = slice(LANES * two, LANES * (two + 1))
            key_cols = slice(width + LANES * two, width + LANES * (two + 1))
            value_cols = slice(2 * width + LANES * two, 2 * width + LANES * (two + 1))
            at = (pair * (width // LANES) + two) * 2 * PAIR_PAD
            probs = probs_ref[at : at + 2 * PAIR_PAD, :]
            grad_out = two_heads(grad_mixed[rows, cols], low)
            grad_scores = dscores_low[at : at + 2 * PAIR_PAD, :]
            grad_query = one_row(dot(grad_scores, qkv_ref[rows, key_cols]), low)
            dqkv_ref[rows, cols] = grad_query.astype(BF)
            dqkv_ref[rows, key_cols] = dot_lt(
                grad_scores, two_heads(qkv_ref[rows, cols], low)
            ).astype(BF)
            dqkv_ref[rows, value_cols] = dot_lt(probs, grad_out).astype(BF)
    compact[...] = norm_parts(tok_ref[...].astype(F32))[0] * gain_one_ref[...]
    spread_rows(compact, padded)
    acc_qkv[...] += dot_lt(padded[...].astype(BF), dqkv_ref[...])

    @pl.when(step == pl.num_programs(0) - 1)
    def _():
        cores, sides, layers = groups
        half = acc_qkv.shape[0] * 4 // cores
        tall = half // (sides * layers)

        def piece(row):
            part, at = row // width, row % width
            if part < 3:
                return acc_qkv[at : at + tall, width * part : width * (part + 1)]
            return acc_proj[at : at + tall, :]

        for side in range(sides):
            for layer in range(layers):
                low = (side * layers + layer) * tall
                spot = (side ^ here_ref[1]) * layers + (layer ^ here_ref[2])
                to = pl.ds(pl.multiple_of(spot * tall, tall), tall)
                even, odd = piece(low), piece(half + low)
                own_ref[to, :] = jnp.where(here_ref[0] == 0, even, odd).astype(BF)
                sent_ref[to, :] = jnp.where(here_ref[0] == 0, odd, even).astype(BF)
        gain_one_sum = jnp.sum(acc_qkv[...] * qkv_w_ref[...].astype(F32), axis=-1, keepdims=True)
        lane = lax.broadcasted_iota(jnp.int32, (width, LANES), 1)
        router = sum(ref[...] for ref in router_refs)
        small = jnp.where(lane == experts, gain_one_sum, router).T[: own_ref.shape[0] - half, :]
        row = lax.broadcasted_iota(jnp.int32, small.shape, 0)
        small = jnp.where(row == experts + 1, acc_gain[...], small).astype(BF)
        own_ref[half:, :] = small
        sent_ref[half:, :] = small


def small_rows(experts):
    return 16 * -(-(experts + 2) // 16)


def back(starts, here, groups, index, hidden, tokens, dy, qkv, probs, mixed, gain_one, w_qkv, w_proj, gain_two, downs, own, routers, capacity):
    count, width = tokens.shape
    blocks = count // BLOCK
    experts = starts.shape[0]
    window = window_rows(experts, capacity)
    row = lambda shape: pl.BlockSpec(shape, lambda step, *_: (step, 0))
    cores, sides, layers = groups
    assert cores == 2
    sum_shape = (2 * width + small_rows(experts), width)
    flops = 2 * blocks * BLOCK_PAD * width * (8 * width + 10 * PAIR_PAD)
    return pl.pallas_call(
        functools.partial(back_kernel, window, groups),
        grid_spec=pltpu.PrefetchScalarGridSpec(
            num_scalar_prefetch=2,
            grid=(blocks,),
            in_specs=[
                row((BLOCK, 2)), row((BLOCK, width)), row((BLOCK, width)), row((BLOCK, width)),
                row((BLOCK_PAD, 3 * width)), row((probs.shape[0] // blocks, PAIR_PAD)),
                row((BLOCK_PAD, width)),
                whole((1, width)), whole(w_qkv.shape), whole(w_proj.shape), whole((1, width)),
            ] + [whole((downs[0].shape[0], capacity, width))] * 2 + [whole(own.shape)]
            + [whole((width, LANES))] * 2,
            out_specs=[
                row((BLOCK, width)), row((BLOCK_PAD, 3 * width)), whole(sum_shape), whole(sum_shape),
            ],
            scratch_shapes=[
                pltpu.VMEM((experts * window, width), BF),
                pltpu.VMEM((BLOCK, width), F32),
                pltpu.VMEM((BLOCK, width), F32),
                pltpu.VMEM((BLOCK_PAD, width), F32),
                pltpu.VMEM(w_qkv.shape, F32),
                pltpu.VMEM(w_proj.shape, F32),
                pltpu.VMEM((1, width), F32),
                pltpu.VMEM((probs.shape[0] // blocks, PAIR_PAD), F32),
                pltpu.VMEM((probs.shape[0] // blocks, PAIR_PAD), BF),
            ],
        ),
        out_shape=[
            jax.ShapeDtypeStruct((count, width), F32),
            jax.ShapeDtypeStruct(qkv.shape, BF),
            jax.ShapeDtypeStruct(sum_shape, BF),
            jax.ShapeDtypeStruct(sum_shape, BF),
        ],
        compiler_params=params(),
        cost_estimate=cost(1e12, 4000e6),
        name="back",
    )(
        starts, here, index, hidden, tokens, dy, qkv, probs, mixed, gain_one[None, :], w_qkv,
        w_proj, gain_two[None, :], *downs, own, *routers,
    )


def last_kernel(dqkv_ref, ghid_ref, tok_ref, gain_one_ref, qkv_w_ref, *refs):
    out_ref, compact, padded = refs[-3:]
    for sub in range(tok_ref.shape[0] // BLOCK):
        rows = slice(BLOCK * sub, BLOCK * (sub + 1))
        spread = slice(BLOCK_PAD * sub, BLOCK_PAD * (sub + 1))
        padded[...] = dot_rt(dqkv_ref[spread, :], qkv_w_ref[...])
        gather_rows(padded, compact)
        hat_one, scale_one = norm_parts(tok_ref[rows, :].astype(F32))
        out_ref[rows, :] = ghid_ref[rows, :] + norm_back(
            compact[...], hat_one, scale_one, gain_one_ref[...]
        )


def last(low, high, so_far, dqkv, ghid, tokens, gain_one, w_qkv):
    count, width = tokens.shape
    subs = max(n for n in range(1, LAST_SUBS + 1) if low % n == 0 and high % n == 0)
    row = lambda tall: pl.BlockSpec((tall * subs, width), lambda step: (step + low // subs, 0))
    wide = pl.BlockSpec((BLOCK_PAD * subs, 3 * width), lambda step: (step + low // subs, 0))
    taken = [] if so_far is None else [so_far]
    return pl.pallas_call(
        last_kernel,
        grid=((high - low) // subs,),
        in_specs=[wide, row(BLOCK), row(BLOCK), whole((1, width)), whole(w_qkv.shape)]
        + [pl.BlockSpec(memory_space=pl.ANY)] * len(taken),
        out_specs=row(BLOCK),
        out_shape=jax.ShapeDtypeStruct((count, width), F32),
        scratch_shapes=[pltpu.VMEM((BLOCK, width), F32), pltpu.VMEM((BLOCK_PAD, width), F32)],
        input_output_aliases={5: 0} if taken else {},
        compiler_params=params(),
        cost_estimate=cost(6 * BLOCK_PAD * (high - low) * width * width, 20e6),
        name="last",
    )(dqkv, ghid, tokens, gain_one[None, :], w_qkv, *taken)


def lay_kernel(groups, here_ref, own_ref, other_ref, qkv_ref, proj_ref):
    cores, sides, layers = groups
    tall, width = own_ref.shape[1:]
    each = width // tall

    def fill(core, source):
        for place in range(core * 2 * each, (core + 1) * 2 * each):
            part, turn = divmod(place, each)
            side, layer = divmod(place % (sides * layers), layers)
            spot = (side ^ here_ref[1]) * layers + (layer ^ here_ref[2])
            rows = slice(tall * turn, tall * (turn + 1))
            if part < 3:
                qkv_ref[rows, width * part : width * (part + 1)] = source[spot].astype(F32)
            else:
                proj_ref[rows, :] = source[spot].astype(F32)

    @pl.when(here_ref[0] == 0)
    def _():
        fill(0, own_ref)
        fill(1, other_ref)

    @pl.when(here_ref[0] == 1)
    def _():
        fill(0, other_ref)
        fill(1, own_ref)


def lay(groups, here, own, other):
    width = own.shape[2]
    return pl.pallas_call(
        functools.partial(lay_kernel, groups),
        grid_spec=pltpu.PrefetchScalarGridSpec(
            num_scalar_prefetch=1,
            grid=(1,),
            in_specs=[whole(own.shape)] * 2,
            out_specs=[whole((width, 3 * width)), whole((width, width))],
        ),
        out_shape=[
            jax.ShapeDtypeStruct((width, 3 * width), F32),
            jax.ShapeDtypeStruct((width, width), F32),
        ],
        compiler_params=params(VMEM_ALL),
        cost_estimate=cost(1e6, 8e6),
        name="lay",
    )(here, own, other)


def unpack_kernel(*refs):
    parts, (up_ref, down_ref) = refs[:-2], refs[-2:]
    tall, width = up_ref.shape[1], down_ref.shape[2]
    for which, part in enumerate(parts):
        up_ref[which] = part[:tall, :].astype(F32)
        for turn in range(down_ref.shape[1] // tall):
            down_ref[which, tall * turn : tall * (turn + 1), :] = (
                part[tall:, width * turn : width * (turn + 1)].astype(F32)
            )


def unpack(parts, width):
    tall, units = parts[0].shape[0] // 2, parts[0].shape[1]
    outs = [
        jax.ShapeDtypeStruct((len(parts), tall, units), F32),
        jax.ShapeDtypeStruct((len(parts), tall * units // width, width), F32),
    ]
    return pl.pallas_call(
        unpack_kernel,
        grid=(1,),
        in_specs=[whole(part.shape) for part in parts],
        out_specs=[whole(out.shape) for out in outs],
        out_shape=outs,
        compiler_params=params(),
        cost_estimate=cost(1e6, 4e6),
        name="unpack",
    )(*parts)


def jump(value, axis, far):
    size = lax.axis_size(axis)
    return lax.ppermute(value, axis, [(at, at ^ far) for at in range(size)])


def merge_kernel(cuts, extra, count, *refs):
    parts, outs = refs[:count], refs[count:]
    tall = (parts[0].shape[0] - extra) // cuts

    def total(rows):
        value = parts[0][rows, :].astype(F32)
        for part in parts[1:]:
            value = value + part[rows, :].astype(F32)
        return value

    small = total(slice(cuts * tall, None))
    for cut, out in enumerate(outs):
        if cut == cuts:
            out[...] = small
            continue
        out[:tall, :] = total(slice(cut * tall, (cut + 1) * tall)).astype(BF)
        if out.shape[0] > tall:
            out[tall:, :] = small.astype(BF)


def merge(parts, cuts, extra, ends):
    rows, width = parts[0].shape
    tall = (rows - extra) // cuts
    if ends:
        outs = [jax.ShapeDtypeStruct((tall, width), BF), jax.ShapeDtypeStruct((extra, width), F32)]
    else:
        outs = [jax.ShapeDtypeStruct((tall + extra, width), BF)] * cuts
    return pl.pallas_call(
        functools.partial(merge_kernel, cuts, extra, len(parts)),
        grid=(1,),
        in_specs=[whole((rows, width))] * len(parts),
        out_specs=[whole(out.shape) for out in outs],
        out_shape=outs,
        compiler_params=params(VMEM_ALL),
        cost_estimate=cost(1e6, 4e6),
        name="merge",
    )(*parts)


def after(value, *others):
    return lax.optimization_barrier((value, *others))[0]


def sum_over_all(own, sent, groups, extra, arrived, beside):
    cores, sides, layers = groups
    beside = iter(beside)

    def spread(own, sent, axis, scale):
        came = [jump(part, axis, scale * far) for far, part in enumerate(sent, 1)]
        return [own] + list(after(tuple(came), next(beside)(own)))

    half = merge([own, jump(sent, "dp", 1)], sides, extra, False)
    half = list(after(tuple(half), arrived))
    flat = merge(spread(half[0], half[1:], "expert", 1), layers, extra, False)
    spot, small = merge(spread(flat[0], flat[1:], "dp", cores), 1, extra, True)
    flat = jnp.stack(spread(spot, [spot] * (layers - 1), "dp", cores))
    half = jnp.stack(spread(flat, [flat] * (sides - 1), "expert", 1))
    half = half.reshape(sides * layers, *spot.shape)
    return half, jump(half, "dp", 1), small


def per_device(
    tokens, gain_one, w_qkv, w_proj, gain_two, w_router, w_in, w_eout, picks, keep, grad_out
):
    count, width = tokens.shape
    local = w_in.shape[0]
    assert local == 2
    owners = lax.axis_size("expert")
    shards = lax.axis_size("dp")
    experts = local * owners
    capacity = 8 * ((21 * count + 80 * experts - 1) // (80 * experts))
    me, row = lax.axis_index("expert"), lax.axis_index("dp")
    cores = 2
    groups = (cores, owners, shards // cores)
    here = jnp.stack([row % cores, me, row // cores]).astype(jnp.int32)

    def swap(sent):
        return lax.all_to_all(sent, "expert", split_axis=0, concat_axis=0, tiled=True)

    index_rows, starts = places(picks, keep, experts, local, capacity)
    send = lambda srcs, *plan: dispatch(srcs, starts, index_rows, owners, capacity, plan)
    (dy_first,) = send([grad_out], (0, (0,)))
    got = swap(dy_first)
    hidden, rows, qkv, probs, mixed = attend(
        after(tokens, dy_first), gain_one, w_qkv, w_proj, gain_two
    )
    (x_first,) = send([rows], (0, (0,)))
    arrived = [[(swap(after(x_first, got)), 0), (got, 0)]]
    kept = [[(x_first, 0), (dy_first, 0)]]
    others = send([after(rows, x_first), grad_out], *[(part, (0, 1)) for part in range(1, local)])
    for sent in others:
        got = swap(after(sent, arrived[-1][0][0]))
        arrived.append([(got, 0), (got, 1)])
        kept.append([(sent, 0), (sent, 1)])
    index = index_rows.transpose(0, 2, 1).reshape(count, 2)
    head = w_router.astype(BF)
    rest = (w_router - head.astype(F32)).astype(BF)
    gap = ((0, 0), (0, LANES - experts))
    router = jnp.concatenate([jnp.pad(head, gap), jnp.pad(rest, gap)], axis=1)
    router_back = jnp.concatenate([jnp.pad(head, gap).T, jnp.pad(rest, gap).T], axis=0)
    early = 16 * (capacity // 39)
    weights = (w_in, w_eout, router, router_back)

    def one(part, own, given, before, *taken):
        mine = jnp.stack([me * local + part, me]).astype(jnp.int32)
        came = (kept if own else arrived)[part]
        taken = dict(zip(range(2 - len(taken), 2), taken))
        return expert_pass(
            part, mine, *came, weights, early, experts, capacity, shards, own, given, before, taken
        )

    def reduce(grad):
        grad = grad.reshape(shards * grad.shape[1], grad.shape[2])
        return lax.psum_scatter(grad, "dp", scatter_dimension=0, tiled=True)

    head, tail, *given = one(0, True, [], None)
    head, tail, grad, router_first = one(0, False, given, None, head, tail)
    sums, tail_first = [reduce(grad)], tail
    head = swap(after(head, got))
    down, tail, *given = one(1, False, [], tail_first)
    down = swap(after(down, head))
    own_down, own_out, grad, router_second = one(1, True, given, None)
    sums.append(reduce(grad))
    tail = swap(after(tail, down))
    grad_hidden, dqkv, own, sent = back(
        starts, here, groups, index, hidden, tokens, grad_out, qkv, probs, mixed, gain_one,
        w_qkv, w_proj, gain_two, [head, down], own_down, [router_first, router_second], capacity,
    )
    blocks = count // BLOCK
    some = blocks // 3

    def make_top(tie):
        return top(
            starts, here, index, after(hidden, tie), head, tail, tail_first, own_out, early, capacity
        )

    def make_unpack(tie):
        return unpack(after(tuple(sums), tie), width)

    def make_last(low, high, tie, so_far=None):
        return last(
            low, high, so_far, after(dqkv, tie), grad_hidden, tokens, gain_one, w_qkv
        )

    made = {}

    def beside(name, work):
        def go(tie):
            made[name] = work(tie)
            return jax.tree.leaves(made[name])[0]

        return go

    own, other, small = sum_over_all(
        own, sent, groups, small_rows(experts), tail,
        [
            beside("top", make_top),
            beside("unpack", make_unpack),
            beside("some", lambda tie: make_last(0, some, tie)),
            beside("last", lambda tie: make_last(some, blocks, tie, made["some"])),
        ],
    )
    block_out, grad_tokens, (grad_in, grad_eout) = made["top"], made["last"], made["unpack"]
    grad_qkv, grad_proj = lay(groups, here, own, other)
    return (
        block_out,
        grad_tokens,
        small[experts] / gain_one,
        grad_qkv,
        grad_proj,
        small[experts + 1],
        small[:experts].T,
        grad_in,
        grad_eout,
    )


def solution(mesh):
    rows = P(("dp", "expert"), None)
    experts = P("expert", None, None)
    return jax.shard_map(
        per_device,
        mesh=mesh,
        in_specs=(rows, P(), P(), P(), P(), P(), experts, experts, rows, rows, rows),
        out_specs=(
            rows, rows, P(), P(), P(), P(), P(), P("expert", "dp", None), P("expert", "dp", None),
        ),
        check_vma=False,
    )
```
